32 devices in a mesh: pipe: 2 (over y), tensor: 4 (over x, core), dp: 4 (over z).
Axes of the slice: x: 2, y: 2, z: 4, core: 2. Of those that a mesh axis runs over, the one named last changes fastest.
Arguments:
- boundary: bfloat16 [2, 2, 4, 1280, 1024], P('pipe', None, 'dp', 'tensor'), may hold values from -6 to 6
- lengths: int32 [2, 4, 3], P(None, 'dp'), may hold values from 1 to 1024, 1280 in all within a row
- gains: bfloat16 [2, 2, 1024], P('pipe', None, ('tensor', 'dp')), may hold values from 0.5 to 1.5
- biases: bfloat16 [2, 4, 1024], P('pipe', None, ('tensor', 'dp')), may hold values from -1 to 1
- qkv_weight: bfloat16 [2, 1024, 3, 1024], P('pipe', 'dp', None, 'tensor'), may hold values from -0.1875 to 0.1875
- qkv_bias: bfloat16 [2, 3, 1024], P('pipe', None, ('tensor', 'dp')), may hold values from -1.5 to 1.5
- out_weight: bfloat16 [2, 1024, 1024], P('pipe', 'tensor', 'dp'), may hold values from -0.75 to 0.75
- up_weight: bfloat16 [2, 1024, 4096], P('pipe', 'dp', 'tensor'), may hold values from -0.1875 to 0.1875
- up_bias: bfloat16 [2, 4096], P('pipe', ('tensor', 'dp')), may hold values from -1.5 to 1.5
- down_weight: bfloat16 [2, 4096, 1024], P('pipe', 'tensor', 'dp'), may hold values from -0.09375 to 0.09375
Outputs:
- ends: float32 [2, 2, 4, 1280, 1024], P('pipe', None, 'dp', 'tensor')
- grad_gains: float32 [2, 2, 1024], P('pipe', None, ('tensor', 'dp'))
- grad_biases: float32 [2, 4, 1024], P('pipe', None, ('tensor', 'dp'))
- grad_qkv_weight: float32 [2, 1024, 3, 1024], P('pipe', 'dp', None, 'tensor')
- grad_qkv_bias: float32 [2, 3, 1024], P('pipe', None, ('tensor', 'dp'))
- grad_out_weight: float32 [2, 1024, 1024], P('pipe', 'tensor', 'dp')
- grad_up_weight: float32 [2, 1024, 4096], P('pipe', 'dp', 'tensor')
- grad_up_bias: float32 [2, 4096], P('pipe', ('tensor', 'dp'))
- grad_down_weight: float32 [2, 4096, 1024], P('pipe', 'tensor', 'dp')
The draws below stay inside these ranges and needn't reach their ends.
Inputs may be any that keep to these rules, and one draw needn't show every extreme that they name: Each row lengths[m, g] sums to 1280 and its largest entry is exactly 1024.
All inputs are finite; a program needn't handle non-finite values.
Results may differ from the reference program's by a relative error of at most 0.008.
Values may be sent and summed in bfloat16 or wider, within the bound.
No kernel may reach another device: no remote copies, remote signals or barrier semaphores. Data moves between devices by JAX's collectives and lax.ppermute only.
A program may use at most 192 MiB of HBM per device.

```python
import math
import jax
import jax.numpy as jnp
import numpy as np
from jax import lax

D = 1024
H = 16
HD = 64
ROT = 16
FF = 4096
SEQ = 1024
SEGS = 3
MB = 2
TOK_MB = 1280
GROUPS = 4
LAYERS = 2


def shard_levels(own_key, dims, cuts, least, high):
    level, own = 1.0, jax.random.fold_in(own_key, 6)
    for dim, parts in cuts:
        steps = jnp.exp(jax.random.uniform(jax.random.fold_in(own, dim), (parts,), jnp.float32, least / len(cuts), high / len(cuts)))
        level = level * jnp.repeat(steps, dims[dim] // parts).reshape([-1 if axis == dim else 1 for axis in range(len(dims))])
    return level


def split_up(amount, total, limit, skew):
    portions = [(1 << 20) // math.isqrt(rank ** skew) + 1 for rank in range(2, amount + 1)]
    spare, holding = total - limit - (amount - 1), [1] * (amount - 1)
    while spare > 0:
        free = [i for i in range(amount - 1) if holding[i] < limit]
        whole, remaining = sum([portions[i] for i in free]), spare
        for i in free:
            addition = min(limit - holding[i], max(1, remaining * portions[i] // whole), spare)
            holding[i] = holding[i] + addition
            spare = spare - addition
    return np.array([limit] + holding)


def uneven(rng, count, total, bound, skew):
    if count == 2:
        one = jax.random.randint(rng, (), max(1, total - bound), min(bound, total - 1) + 1)
        return jnp.stack([one, total - one])
    sizes = jnp.asarray(split_up(count, total, bound, skew), jnp.int32)
    couples = (count - 1) // 2
    donor, receiver = sizes[1:1 + 2 * couples:2], sizes[2:2 + 2 * couples:2]
    room = jnp.minimum(donor - 1, bound - receiver)
    passed = jax.random.randint(jax.random.fold_in(rng, 1), (couples,), 0, 1 << 20) % (room + 1)
    sizes = sizes.at[1:1 + 2 * couples:2].set(donor - passed).at[2:2 + 2 * couples:2].set(receiver + passed)
    return sizes[jax.random.permutation(jax.random.fold_in(rng, 2), count)]


def noise(own_key, extent, scale, limit, cuts=(), held_as=jnp.bfloat16):
    array = jax.random.normal(own_key, extent, jnp.float32) * scale
    if len(cuts) > 0:
        array = shard_levels(own_key, extent, cuts, -0.22, 0.18) * array
    return jnp.clip(array, min=-limit, max=limit).astype(held_as)


def setup_inputs(seed: int = 0) -> dict:
    key_list = jax.random.split(jax.random.key(seed), 11)
    boundary = noise(key_list[0], (2, MB, GROUPS, TOK_MB, D), 1.0, 6.0, ((0, 2), (2, 4), (3, 4)))
    lengths = jax.vmap(lambda own: uneven(own, SEGS, TOK_MB, SEQ, 2))(jax.random.split(key_list[1], MB * GROUPS)).reshape((MB, GROUPS, SEGS)).astype(jnp.int32)
    gains = jnp.clip(1.0 + 0.1 * jax.random.normal(key_list[2], (LAYERS, 2, D), jnp.float32), 0.5, 1.5).astype(jnp.bfloat16)
    biases = noise(key_list[3], (LAYERS, 4, D), 0.2, 1.0, ((0, 2), (2, 16)))
    qkv_weight = noise(key_list[4], (LAYERS, D, 3, D), D ** -0.5, 0.1875, ((0, 2), (1, 4), (3, 4)))
    qkv_bias = noise(key_list[5], (LAYERS, 3, D), 0.3, 1.5, ((0, 2), (2, 16)))
    out_weight = noise(key_list[6], (LAYERS, D, D), (D // 16) ** -0.5, 0.75, ((0, 2), (1, 4), (2, 4)))
    up_weight = noise(key_list[7], (LAYERS, D, FF), D ** -0.5, 0.1875, ((0, 2), (1, 4), (2, 4)))
    up_bias = noise(key_list[8], (LAYERS, FF), 0.3, 1.5, ((0, 2), (1, 16)))
    down_weight = noise(key_list[9], (LAYERS, FF, D), FF ** -0.5, 0.09375, ((0, 2), (1, 4), (2, 4)))
    return dict(boundary=boundary, lengths=lengths, gains=gains, biases=biases, qkv_weight=qkv_weight, qkv_bias=qkv_bias, out_weight=out_weight, up_weight=up_weight, up_bias=up_bias, down_weight=down_weight)


@jax.custom_vjp
def low(v):
    return lax.optimization_barrier(v.astype(jnp.bfloat16)).astype(jnp.float32)

@jax.custom_vjp
def low_back(v):
    return v

def low_keep(v):
    return (low(v), None)

def low_pass(kept, grad):
    return (grad,)

def back_keep(v):
    return (v, None)

def back_low(kept, grad):
    return (low(grad),)
low.defvjp(low_keep, low_pass)
low_back.defvjp(back_keep, back_low)
HIGHEST = lax.Precision.HIGHEST
epsilon = 1e-05

def norm_rows(inputs, gain, bias):
    middle_value = lax.optimization_barrier(jnp.mean(inputs, axis=-1, keepdims=True))
    centered = inputs - middle_value
    variance = lax.optimization_barrier(jnp.mean(centered * centered, axis=-1, keepdims=True))
    return centered * lax.rsqrt(variance + epsilon) * gain + bias

def angles_for(lengths_row):
    lengths_row = lengths_row.astype(jnp.int32)
    finish = jnp.cumsum(lengths_row).astype(jnp.int32)
    places = jnp.arange(TOK_MB, dtype=jnp.int32)
    after = (places[:, None] >= finish[None, :]).astype(jnp.int32)
    segment = lax.optimization_barrier(jnp.sum(after, axis=1)).astype(jnp.int32)
    starts = lax.optimization_barrier(jnp.sum(after * lengths_row[None, :], axis=1)).astype(jnp.int32)
    position = (places - starts).astype(jnp.float32)
    inverse_freq = 10000.0 ** (-jnp.arange(ROT // 2, dtype=jnp.float32) * 2.0 / ROT)
    phase = position[:, None] * inverse_freq[None, :]
    return (segment, jnp.cos(phase), jnp.sin(phase))

def rotate(values, cosine, sine):
    rot_half = ROT // 2
    first = values[..., :rot_half]
    second = values[..., rot_half:ROT]
    remain = values[..., ROT:]
    return jnp.concatenate([first * cosine - second * sine, second * cosine + first * sine, remain], axis=-1)

def attention(queries, keys, values, segment):
    block = TOK_MB // 2
    places = jnp.arange(TOK_MB, dtype=jnp.int32)
    scale = HD ** (-0.5)

    def one_block(pieces):
        q_rows, seg_rows, place_rows = pieces
        scores = low_back(jnp.einsum('qhd,khd->hqk', q_rows, keys, precision=HIGHEST) * scale)
        allowed = (seg_rows[:, None] == segment[None, :]) & (place_rows[:, None] >= places[None, :])
        scores = jnp.where(allowed[None], scores, -1e+30)
        top_score = lax.optimization_barrier(jnp.max(scores, axis=-1, keepdims=True))
        expd = jnp.exp(scores - top_score)
        probs = low(expd / lax.optimization_barrier(jnp.sum(expd, axis=-1, keepdims=True)))
        return jnp.einsum('hqk,khd->qhd', probs, values, precision=HIGHEST)
    blocks = lax.map(jax.checkpoint(one_block), (queries.reshape(2, block, H, HD), segment.reshape(2, block), places.reshape(2, block)))
    return blocks.reshape(TOK_MB, H, HD)

def layer(inputs, segment, cosine, sine, params):
    gains, biases, qkv_weight, qkv_bias, out_weight, up_weight, up_bias, down_weight = params
    first = low(norm_rows(inputs, gains[0], biases[0]))
    second = low(norm_rows(inputs, gains[1], biases[1]))
    raw = low_back(jnp.einsum('td,dcf->tcf', first, qkv_weight, precision=HIGHEST) + qkv_bias)
    split = raw.reshape(TOK_MB, 3, H, HD)
    queries = low(rotate(split[:, 0], cosine[:, None], sine[:, None]))
    keys = low(rotate(split[:, 1], cosine[:, None], sine[:, None]))
    values = low(split[:, 2])
    context = low_back(low(attention(queries, keys, values, segment).reshape(TOK_MB, D)))
    pre_act = low_back(jnp.dot(second, up_weight, precision=HIGHEST) + up_bias)
    hidden = low(jax.nn.gelu(pre_act, approximate=False))
    attended = jnp.dot(context, out_weight, precision=HIGHEST) + biases[2]
    mixed = jnp.dot(hidden, down_weight, precision=HIGHEST) + biases[3]
    return inputs + attended + mixed

def forward(inputs, lengths, params):
    units = inputs.reshape(MB * GROUPS, TOK_MB, D)
    length_rows = lengths.reshape(MB * GROUPS, SEGS)

    def one_unit(pieces):
        unit, lengths_row = pieces
        segment, cosine, sine = angles_for(lengths_row)
        middle = layer(unit, segment, cosine, sine, [weight[0] for weight in params])
        middle = low_back(low(middle))
        return layer(middle, segment, cosine, sine, [weight[1] for weight in params])
    return lax.map(one_unit, (units, length_rows)).reshape(MB, GROUPS, TOK_MB, D)

def reference(boundary, lengths, gains, biases, qkv_weight, qkv_bias, out_weight, up_weight, up_bias, down_weight):
    inputs = boundary[0].astype(jnp.float32)
    cotangent = boundary[1].astype(jnp.float32)

    def whole(inputs, gains, biases, qkv_weight, qkv_bias, out_weight, up_weight, up_bias, down_weight):
        return forward(inputs, lengths, (gains, biases, qkv_weight, qkv_bias, out_weight, up_weight, up_bias, down_weight))
    outputs, pull = jax.vjp(whole, inputs, gains.astype(jnp.float32), biases.astype(jnp.float32), qkv_weight.astype(jnp.float32), qkv_bias.astype(jnp.float32), out_weight.astype(jnp.float32), up_weight.astype(jnp.float32), up_bias.astype(jnp.float32), down_weight.astype(jnp.float32))
    grads = pull(cotangent)
    ends = jnp.stack([grads[0], outputs])
    return (ends, grads[1], grads[2], grads[3], grads[4], grads[5], grads[6], grads[7], grads[8])
```

```python
import functools

import jax
import jax.numpy as jnp
from jax import lax
from jax.experimental import pallas as pl
from jax.experimental.pallas import tpu as pltpu
from jax.sharding import PartitionSpec as P

D = 1024
H = 16
HD = 64
ROT = 16
MB = 2
TOK_MB = 1280
EPS = 1e-05
CHUNK = 256
CHUNKS = TOK_MB // CHUNK
BF = jnp.bfloat16
F32 = jnp.float32
ANY = pl.BlockSpec(memory_space=pl.ANY)
VMEM = pl.BlockSpec(memory_space=pltpu.VMEM)
SMEM = pl.BlockSpec(memory_space=pltpu.SMEM)
LIMIT = 58 * 1024 * 1024


def dot(left, right, left_dim, right_dim):
    return lax.dot_general(
        left, right, (((left_dim,), (right_dim,)), ((), ())), preferred_element_type=F32
    )


def shape(dims, dtype):
    return jax.ShapeDtypeStruct(dims, dtype)


def swap(value, axis, bit):
    count = lax.axis_size(axis)
    return lax.ppermute(value, axis, [(i, i ^ (1 << bit)) for i in range(count)])


def bits_of(axis):
    return lax.axis_size(axis).bit_length() - 1


def pick(value, index, axis):
    return lax.dynamic_index_in_dim(value, index, axis, keepdims=False)


def gather_blocks(value):
    blocks = {0: value}
    for bit in reversed(range(bits_of("tensor"))):
        for s in list(blocks):
            blocks[s | (1 << bit)] = swap(blocks[s], "tensor", bit)
    return [blocks[s] for s in range(len(blocks))]


def gather_tensor(value):
    index = lax.axis_index("tensor")
    value = value[None]
    for bit in reversed(range(bits_of("tensor"))):
        other = swap(value, "tensor", bit)
        mine = ((index >> bit) & 1) == 0
        low = jnp.where(mine, value, other)
        high = jnp.where(mine, other, value)
        value = jnp.stack([low, high], axis=1).reshape((-1,) + value.shape[1:])
    return value


def scatter_tensor(keep, send):
    index = lax.axis_index("tensor")
    value = keep.astype(F32) + swap(send, "tensor", 0).astype(F32)
    for bit in range(1, bits_of("tensor")):
        own = (index >> bit) & 1
        pairs = value.reshape((value.shape[0] // 2, 2) + value.shape[1:])
        other = swap(pick(pairs, 1 - own, 1).astype(BF), "tensor", bit)
        value = pick(pairs, own, 1) + other.astype(F32)
    return value[0]


def sum_pipe(value):
    low = value.astype(BF)
    return low, swap(low, "pipe", 0)


def scatter_line(value, axis, low):
    count = lax.axis_size(axis)
    index = lax.axis_index(axis)
    from_left = from_right = None
    for step in range(1, count):
        reach = count - step
        right_term = pick(value, jnp.minimum(index + reach, count - 1), 0).astype(F32)
        left_term = pick(value, jnp.maximum(index - reach, 0), 0).astype(F32)
        if from_left is not None:
            right_term = right_term + from_left.astype(F32)
            left_term = left_term + from_right.astype(F32)
        from_left = lax.ppermute(
            right_term.astype(low), axis, [(j, j + 1) for j in range(step)]
        )
        from_right = lax.ppermute(
            left_term.astype(low), axis, [(j + 1, j) for j in range(count - 1 - step, count - 1)]
        )
    own = pick(value, index, 0).astype(F32)
    if from_left is None:
        return own
    return own + from_left.astype(F32) + from_right.astype(F32)


def copies_of_blocks(index, blocks, target, sems):
    copies = []
    for s, block in enumerate(blocks):
        rows = block.shape[0]
        where = pl.multiple_of((index ^ s) * rows, rows)
        copies.append(pltpu.make_async_copy(block, target.at[pl.ds(where, rows)], sems.at[s]))
    return copies


def copies_to_halves(index, source, keep, send, sems, rows):
    copies = []
    own = index & 1
    for block in range(source.shape[0] // rows):
        part = source.at[pl.ds(block * rows, rows)]
        copies.append(
            (
                own == block & 1,
                pltpu.make_async_copy(part, keep.at[block >> 1], sems.at[block]),
                pltpu.make_async_copy(part, send.at[block >> 1], sems.at[block]),
            )
        )
    return copies


def start_half(copy):
    is_kept, to_keep, to_send = copy

    @pl.when(is_kept)
    def _():
        to_keep.start()

    @pl.when(jnp.logical_not(is_kept))
    def _():
        to_send.start()


def normalize(rows):
    rows = rows.astype(F32)
    centered = rows - jnp.mean(rows, axis=-1, keepdims=True)
    scale = lax.rsqrt(jnp.mean(centered * centered, axis=-1, keepdims=True) + EPS)
    return centered * scale, scale


def gelu_pair(values):
    share = 0.5 * (1.0 + lax.erf(values * 0.7071067811865476))
    density = jnp.exp(-0.5 * values * values) * 0.3989422804014327
    return values * share, share + values * density


def rotate(values, table_cos, table_sin, sign):
    width = values.shape[1]
    half = ROT // 2
    lanes = lax.broadcasted_iota(jnp.int32, values.shape, 1) % HD
    partner = jnp.where(
        lanes < half, pltpu.roll(values, width - half, 1), pltpu.roll(values, half, 1)
    )
    return values * table_cos + partner * (table_sin * sign)


def project_kernel(blocks, w, *refs):
    index_ref = refs[0]
    x_refs = refs[1 : 1 + blocks]
    (qkv_ref, up_ref, norms_ref, qkv_bias_ref, up_bias_ref, cos_ref, sin_ref) = refs[
        1 + blocks : 8 + blocks
    ]
    (first_ref, second_ref, q_ref, k_ref, v_ref, hidden_ref, slope_ref) = refs[
        8 + blocks : 15 + blocks
    ]
    x_all, sems = refs[15 + blocks :]
    step = pl.program_id(0)

    @pl.when(step == 0)
    def _():
        copies = copies_of_blocks(index_ref[0], x_refs, x_all, sems)
        for copy in copies:
            copy.start()
        for copy in copies:
            copy.wait()

    rows = x_all[pl.ds(pl.multiple_of(step * CHUNK, CHUNK), CHUNK)]
    hat, _ = normalize(rows)
    first = (hat * norms_ref[0:1] + norms_ref[2:3]).astype(BF)
    second = (hat * norms_ref[1:2] + norms_ref[3:4]).astype(BF)
    first_ref[...] = first
    second_ref[...] = second
    raw = dot(first, qkv_ref[...], 1, 0) + qkv_bias_ref[...]
    table_cos, table_sin = cos_ref[...], sin_ref[...]
    q_ref[...] = rotate(raw[:, :w], table_cos, table_sin, 1.0).astype(BF)
    k_ref[...] = rotate(raw[:, w : 2 * w], table_cos, table_sin, 1.0).astype(BF)
    v_ref[...] = raw[:, 2 * w :].astype(BF)
    hidden, slope = gelu_pair(dot(second, up_ref[...], 1, 0) + up_bias_ref[...])
    hidden_ref[...] = hidden.astype(BF)
    slope_ref[...] = slope.astype(BF)


def project(index, x_blocks, weights, angles):
    _, table_cos, table_sin = angles
    blocks = len(x_blocks)
    w = weights["w"]
    hidden = weights["up"].shape[1]

    def rows(width):
        return pl.BlockSpec((CHUNK, width), lambda i: (i, 0))

    def whole(value):
        return pl.BlockSpec(value.shape, lambda i: (0,) * value.ndim)

    fixed = [weights[name] for name in ("qkv", "up", "norms", "qkv_bias", "up_bias")]
    widths = [D, D, w, w, w, hidden, hidden]
    flops = 2 * TOK_MB * D * (3 * w + hidden)
    return pl.pallas_call(
        functools.partial(project_kernel, blocks, w),
        grid=(CHUNKS,),
        in_specs=[SMEM] + [ANY] * blocks + [whole(v) for v in fixed] + [rows(w)] * 2,
        out_specs=[rows(width) for width in widths],
        out_shape=[shape((TOK_MB, width), BF) for width in widths],
        scratch_shapes=[
            pltpu.VMEM((TOK_MB, D), BF),
            pltpu.SemaphoreType.DMA((blocks,)),
        ],
        compiler_params=pltpu.CompilerParams(vmem_limit_bytes=LIMIT),
        cost_estimate=pl.CostEstimate(flops=3 * flops, bytes_accessed=14 << 20, transcendentals=0),
        name="project",
    )(index, *x_blocks, *fixed, table_cos, table_sin)


def allowed_in(starts, q_block, k_block):
    key = lax.broadcasted_iota(jnp.int32, (CHUNK, CHUNK), 0) + k_block * CHUNK
    query = lax.broadcasted_iota(jnp.int32, (CHUNK, CHUNK), 1) + q_block * CHUNK
    return (key <= query) & (key >= starts)


def head_only(values, head):
    lanes = lax.broadcasted_iota(jnp.int32, values.shape, 1)
    inside = (lanes >= head * HD) & (lanes < (head + 1) * HD)
    return jnp.where(inside, values, jnp.zeros_like(values))


def chunk_of(block):
    return pl.ds(pl.multiple_of(block * CHUNK, CHUNK), CHUNK)


def attend_kernel(heads, w, *refs):
    (index_ref, first_key_ref, starts_ref, q_ref, k_ref, v_ref, hidden_ref, low_ref) = refs[:8]
    (keep_ref, send_ref, context_ref, logs_ref) = refs[8:12]
    (low_all, partial, v_turned, scores, low_sems, out_sems) = refs[12:]
    dp, share = low_ref.shape[0], low_ref.shape[2]
    rows = keep_ref.shape[1]
    loads = [
        pltpu.make_async_copy(low_ref.at[j], low_all.at[:, pl.ds(j * share, share)], low_sems.at[j])
        for j in range(dp)
    ]
    for load in loads:
        load.start()
    outs = copies_to_halves(index_ref[0], partial, keep_ref, send_ref, out_sems, rows)
    v_turned[...] = v_ref[...].T
    logs_ref[...] = jnp.zeros_like(logs_ref)
    for load in loads:
        load.wait()

    @pl.loop(0, CHUNKS)
    def _(block):
        at = chunk_of(block)
        starts = starts_ref[:, at]
        queries = q_ref[at] * BF(HD**-0.5)
        turned = []
        for head in range(heads):
            mine = head_only(queries, head)

            def score(key_block, top, mine=mine):
                s = dot(k_ref[chunk_of(key_block)], mine, 1, 1)
                s = jnp.where(allowed_in(starts, block, key_block), s, -1e30)
                scores[chunk_of(key_block)] = s
                return jnp.maximum(top, jnp.max(s, axis=0, keepdims=True))

            top = lax.fori_loop(
                first_key_ref[block], block + 1, score, jnp.full((1, CHUNK), -1e30, F32)
            )

            def weigh(key_block, carry, head=head, top=top):
                total, sums = carry
                e = jnp.exp(scores[chunk_of(key_block)] - top)
                total = total + jnp.sum(e, axis=0, keepdims=True)
                part = v_turned[head * HD : (head + 1) * HD, chunk_of(key_block)]
                return total, sums + dot(part, e.astype(BF), 1, 0)

            total, sums = lax.fori_loop(
                first_key_ref[block],
                block + 1,
                weigh,
                (jnp.zeros((1, CHUNK), F32), jnp.zeros((HD, CHUNK), F32)),
            )
            turned.append(sums / total)
            logs_ref[head : head + 1, at] = top + jnp.log(total)
        if heads * HD < w:
            turned.append(jnp.zeros((w - heads * HD, CHUNK), F32))
        context = jnp.concatenate(turned, axis=0).T.astype(BF)
        context_ref[at] = context
        total = dot(context, low_all[:w], 1, 0) + dot(hidden_ref[at], low_all[w:], 1, 0)
        partial[at] = total.astype(BF)

    for out in outs:
        start_half(out)
    for out in outs:
        out[1].wait()


def attend(index, kept, weights, angles):
    queries, keys, values, hidden = kept[2:6]
    starts, _, _ = angles
    first_key = starts[::CHUNK] // CHUNK
    w, heads, low = weights["w"], weights["heads"], weights["low"]
    dp = low.shape[0]
    tensor = lax.axis_size("tensor")
    rows = TOK_MB // tensor
    wide = w + hidden.shape[1]
    flops = 2 * TOK_MB * D * wide
    return pl.pallas_call(
        functools.partial(attend_kernel, heads, w),
        in_specs=[SMEM, SMEM, VMEM, VMEM, VMEM, VMEM, VMEM, ANY],
        out_specs=[ANY, ANY, VMEM, VMEM],
        out_shape=[
            shape((tensor // 2, rows, D), BF),
            shape((tensor // 2, rows, D), BF),
            shape((TOK_MB, w), BF),
            shape((8, TOK_MB), F32),
        ],
        scratch_shapes=[
            pltpu.VMEM((wide, D), BF),
            pltpu.VMEM((TOK_MB, D), BF),
            pltpu.VMEM((w, TOK_MB), BF),
            pltpu.VMEM((TOK_MB, CHUNK), F32),
            pltpu.SemaphoreType.DMA((dp,)),
            pltpu.SemaphoreType.DMA((tensor,)),
        ],
        compiler_params=pltpu.CompilerParams(vmem_limit_bytes=LIMIT),
        cost_estimate=pl.CostEstimate(flops=4 * flops, bytes_accessed=8 << 20, transcendentals=0),
        name="attend",
    )(index, first_key, starts[None], queries, keys, values, hidden, low)


def backward_kernel(blocks, heads, w, *refs):
    index_ref, first_key_ref = refs[:2]
    c_refs = refs[2 : 2 + blocks]
    x_refs = refs[2 + blocks : 2 + 2 * blocks]
    (starts_ref, q_ref, k_ref, v_ref, context_ref, logs_ref, slope_ref) = refs[
        2 + 2 * blocks : 9 + 2 * blocks
    ]
    (qkv_ref, up_ref, low_ref, norms_ref, cos_ref, sin_ref) = refs[
        9 + 2 * blocks : 15 + 2 * blocks
    ]
    (keep_ref, send_ref, raw_ref, pre_ref, vectors_ref, raw_sum_ref, pre_sum_ref) = refs[
        15 + 2 * blocks : 22 + 2 * blocks
    ]
    (
        c_all,
        x_all,
        low_all,
        partial,
        grad_context,
        k_turned,
        weighted,
        grad_q,
        grad_k,
        grad_v,
        c_sems,
        x_sems,
        low_sems,
        out_sems,
    ) = refs[22 + 2 * blocks :]
    index = index_ref[0]
    dp, share = low_ref.shape[0], low_ref.shape[2]
    rows = keep_ref.shape[1]
    loads = [
        pltpu.make_async_copy(low_ref.at[j], low_all.at[:, pl.ds(j * share, share)], low_sems.at[j])
        for j in range(dp)
    ]
    loads += copies_of_blocks(index, c_refs, c_all, c_sems)
    x_loads = copies_of_blocks(index, x_refs, x_all, x_sems)
    for load in loads + x_loads:
        load.start()
    outs = copies_to_halves(index, partial, keep_ref, send_ref, out_sems, rows)
    k_turned[...] = (k_ref[...] * BF(HD**-0.5)).T
    grad_k[...] = jnp.zeros_like(grad_k)
    grad_v[...] = jnp.zeros_like(grad_v)
    weighted[...] = jnp.zeros_like(weighted)
    vectors_ref[...] = jnp.zeros_like(vectors_ref)
    raw_sum_ref[...] = jnp.zeros_like(raw_sum_ref)
    pre_sum_ref[...] = jnp.zeros_like(pre_sum_ref)
    for load in loads:
        load.wait()

    @pl.loop(0, CHUNKS)
    def _(block):
        at = chunk_of(block)
        both = dot(c_all[at], low_all[...], 1, 1)
        context_part = both[:, :w].astype(BF)
        grad_context[at] = context_part
        products = (context_part.astype(F32) * context_ref[at].astype(F32)).T
        for head in range(heads):
            weighted[head : head + 1, at] = jnp.sum(
                products[head * HD : (head + 1) * HD], axis=0, keepdims=True
            )
        grad_pre = (both[:, w:] * slope_ref[at].astype(F32)).astype(BF)
        pre_ref[at] = grad_pre
        pre_sum_ref[...] += jnp.sum(grad_pre.astype(F32), axis=0, keepdims=True)

    @pl.loop(0, CHUNKS)
    def _(block):
        at = chunk_of(block)
        starts = starts_ref[:, at]
        queries = q_ref[at] * BF(HD**-0.5)
        grads = grad_context[at]
        queries_of = [head_only(queries, head) for head in range(heads)]
        grads_of = [head_only(grads, head) for head in range(heads)]

        def pair(key_block, sums):
            keys_at = chunk_of(key_block)
            allowed = allowed_in(starts, block, key_block)
            new_sums = []
            to_k = jnp.zeros((CHUNK, w), F32)
            to_v = jnp.zeros((CHUNK, w), F32)
            for head in range(heads):
                s = dot(k_ref[keys_at], queries_of[head], 1, 1)
                p = jnp.exp(jnp.where(allowed, s, -1e30) - logs_ref[head : head + 1, at])
                grad_p = dot(v_ref[keys_at], grads_of[head], 1, 1)
                grad_s = (p * (grad_p - weighted[head : head + 1, at])).astype(BF)
                to_k = to_k + dot(grad_s, queries_of[head], 1, 0)
                to_v = to_v + dot(p.astype(BF), grads_of[head], 1, 0)
                part = k_turned[head * HD : (head + 1) * HD, keys_at]
                new_sums.append(sums[head] + dot(part, grad_s, 1, 0))
            grad_k[keys_at] += to_k
            grad_v[keys_at] += to_v
            return tuple(new_sums)

        sums = lax.fori_loop(
            first_key_ref[block],
            block + 1,
            pair,
            tuple(jnp.zeros((HD, CHUNK), F32) for _ in range(heads)),
        )
        if heads * HD < w:
            sums = sums + (jnp.zeros((w - heads * HD, CHUNK), F32),)
        grad_q[at] = jnp.concatenate(sums, axis=0).T

    for load in x_loads:
        load.wait()

    @pl.loop(0, CHUNKS)
    def _(block):
        at = chunk_of(block)
        table_cos, table_sin = cos_ref[at], sin_ref[at]
        grad_raw = jnp.concatenate(
            [
                rotate(grad_q[at], table_cos, table_sin, -1.0),
                rotate(grad_k[at], table_cos, table_sin, -1.0),
                grad_v[at],
            ],
            axis=1,
        ).astype(BF)
        raw_ref[at] = grad_raw
        raw_sum_ref[...] += jnp.sum(grad_raw.astype(F32), axis=0, keepdims=True)
        grad_first = dot(grad_raw, qkv_ref[...], 1, 1)
        grad_second = dot(pre_ref[at], up_ref[...], 1, 1)
        hat, _ = normalize(x_all[at])
        vectors_ref[0:1] += jnp.sum(grad_first * hat, axis=0, keepdims=True)
        vectors_ref[1:2] += jnp.sum(grad_second * hat, axis=0, keepdims=True)
        vectors_ref[2:3] += jnp.sum(grad_first, axis=0, keepdims=True)
        vectors_ref[3:4] += jnp.sum(grad_second, axis=0, keepdims=True)
        partial[at] = (grad_first * norms_ref[0:1] + grad_second * norms_ref[1:2]).astype(BF)

    for out in outs:
        start_half(out)
    for out in outs:
        out[1].wait()


def backward(index, c_blocks, x_blocks, kept, weights, angles):
    _, _, queries, keys, values, hidden, slope, context, logs = kept
    starts, table_cos, table_sin = angles
    first_key = starts[::CHUNK] // CHUNK
    blocks = len(c_blocks)
    w, heads, low = weights["w"], weights["heads"], weights["low"]
    dp = low.shape[0]
    rows = TOK_MB // blocks
    ff = hidden.shape[1]
    flops = 2 * TOK_MB * D * (4 * w + 2 * ff)
    return pl.pallas_call(
        functools.partial(backward_kernel, blocks, heads, w),
        in_specs=[SMEM] * 2 + [ANY] * (2 * blocks) + [VMEM] * 9 + [ANY] + [VMEM] * 3,
        out_specs=[ANY, ANY] + [VMEM] * 5,
        out_shape=[
            shape((blocks // 2, rows, D), BF),
            shape((blocks // 2, rows, D), BF),
            shape((TOK_MB, 3 * w), BF),
            shape((TOK_MB, ff), BF),
            shape((8, D), F32),
            shape((1, 3 * w), F32),
            shape((1, ff), F32),
        ],
        scratch_shapes=[
            pltpu.VMEM((TOK_MB, D), BF),
            pltpu.VMEM((TOK_MB, D), BF),
            pltpu.VMEM((w + ff, D), BF),
            pltpu.VMEM((TOK_MB, D), BF),
            pltpu.VMEM((TOK_MB, w), BF),
            pltpu.VMEM((w, TOK_MB), BF),
            pltpu.VMEM((8, TOK_MB), F32),
            pltpu.VMEM((TOK_MB, w), F32),
            pltpu.VMEM((TOK_MB, w), F32),
            pltpu.VMEM((TOK_MB, w), F32),
            pltpu.SemaphoreType.DMA((blocks,)),
            pltpu.SemaphoreType.DMA((blocks,)),
            pltpu.SemaphoreType.DMA((dp,)),
            pltpu.SemaphoreType.DMA((blocks,)),
        ],
        compiler_params=pltpu.CompilerParams(vmem_limit_bytes=LIMIT),
        cost_estimate=pl.CostEstimate(flops=3 * flops, bytes_accessed=16 << 20, transcendentals=0),
        name="backward",
    )(
        index,
        first_key,
        *c_blocks,
        *x_blocks,
        starts[None],
        queries,
        keys,
        values,
        context,
        logs,
        slope,
        weights["qkv"],
        weights["up"],
        low,
        weights["norms"],
        table_cos,
        table_sin,
    )


def weights_kernel(blocks, *refs):
    index_ref = refs[0]
    c_refs = [refs[1 + unit * blocks : 1 + (unit + 1) * blocks] for unit in range(MB)]
    inner = refs[1 + MB * blocks : 1 + MB * (blocks + 6)]
    main_ref, low_ref = refs[1 + MB * (blocks + 6) : 3 + MB * (blocks + 6)]
    c_all, sems = refs[3 + MB * (blocks + 6) :]
    copies = []
    for unit in range(MB):
        copies += copies_of_blocks(index_ref[0], c_refs[unit], c_all.at[unit], sems.at[unit])
    for copy in copies:
        copy.start()
    dp, share = main_ref.shape[0], main_ref.shape[2]
    w3, ff = inner[0].shape[1], inner[1].shape[1]
    w = inner[2].shape[1]

    def fill(target, begin, size, left, right):
        for j in range(dp):
            cols = slice(j * share, (j + 1) * share)
            total = sum(
                dot(left(unit)[...], right(unit)[:, cols], 0, 0) for unit in range(MB)
            )
            target[j, begin : begin + size] = total.astype(BF)

    fill(main_ref, 0, w3, lambda u: inner[6 * u], lambda u: inner[6 * u + 4])
    fill(main_ref, w3, ff, lambda u: inner[6 * u + 1], lambda u: inner[6 * u + 5])
    for copy in copies:
        copy.wait()
    fill(low_ref, 0, w, lambda u: inner[6 * u + 2], lambda u: c_all.at[u])
    fill(low_ref, w, ff, lambda u: inner[6 * u + 3], lambda u: c_all.at[u])


def weight_grads(index, c_blocks, inner, dp):
    blocks = len(c_blocks[0])
    w3, ff, w = (inner[0][i].shape[1] for i in range(3))
    flops = 2 * MB * TOK_MB * D * (w3 + 2 * ff + w)
    return pl.pallas_call(
        functools.partial(weights_kernel, blocks),
        in_specs=[SMEM] + [ANY] * (MB * blocks) + [VMEM] * (MB * 6),
        out_specs=[VMEM, VMEM],
        out_shape=[
            shape((dp, w3 + ff, D // dp), BF),
            shape((dp, w + ff, D // dp), BF),
        ],
        scratch_shapes=[
            pltpu.VMEM((MB, TOK_MB, D), BF),
            pltpu.SemaphoreType.DMA((MB, blocks)),
        ],
        compiler_params=pltpu.CompilerParams(vmem_limit_bytes=LIMIT),
        cost_estimate=pl.CostEstimate(flops=2 * flops, bytes_accessed=24 << 20, transcendentals=0),
        name="weight_grads",
    )(index, *[b for unit in c_blocks for b in unit], *[v for unit in inner for v in unit])


def norm_back_kernel(x_ref, own_ref, other_ref, cot_ref, out_ref):
    grad_hat = own_ref[...].astype(F32) + other_ref[...].astype(F32)
    hat, scale = normalize(x_ref[...])
    mean = jnp.mean(grad_hat, axis=-1, keepdims=True)
    along = jnp.mean(grad_hat * hat, axis=-1, keepdims=True)
    grad = cot_ref[...].astype(F32) + (grad_hat - mean - hat * along) * scale
    out_ref[...] = grad.astype(out_ref.dtype)


def norm_back(x_rows, own, other, cot_rows, dtype):
    return pl.pallas_call(
        norm_back_kernel,
        in_specs=[VMEM] * 4,
        out_specs=VMEM,
        out_shape=shape(x_rows.shape, dtype),
        compiler_params=pltpu.CompilerParams(vmem_limit_bytes=LIMIT),
        cost_estimate=pl.CostEstimate(
            flops=20 * x_rows.size, bytes_accessed=4 << 20, transcendentals=0
        ),
        name="norm_back",
    )(x_rows, own, other, cot_rows)


def angles_for(lengths_row, w):
    finish = jnp.cumsum(lengths_row)
    places = jnp.arange(TOK_MB, dtype=jnp.int32)
    after = (places[:, None] >= finish[None, :]).astype(jnp.int32)
    starts = jnp.sum(after * lengths_row[None, :], axis=1)
    position = (places - starts).astype(F32)
    inverse_freq = 10000.0 ** (-jnp.arange(ROT // 2, dtype=F32) * 2.0 / ROT)
    phase = position[:, None] * inverse_freq[None, :]
    cosine, sine = jnp.cos(phase), jnp.sin(phase)
    rest = HD - ROT
    table_cos = jnp.concatenate([cosine, cosine, jnp.ones((TOK_MB, rest), F32)], axis=1)
    table_sin = jnp.concatenate([-sine, sine, jnp.zeros((TOK_MB, rest), F32)], axis=1)
    return starts, jnp.tile(table_cos, (1, w // HD)), jnp.tile(table_sin, (1, w // HD))


def body(
    boundary,
    lengths,
    gains,
    biases,
    qkv_weight,
    qkv_bias,
    out_weight,
    up_weight,
    up_bias,
    down_weight,
):
    stage = lax.axis_index("pipe")
    at_first = stage == 0
    dp = lax.axis_size("dp")
    tensor = lax.axis_size("tensor")
    index = lax.axis_index("tensor").astype(jnp.int32)[None]
    share = D // dp
    width = qkv_weight.shape[3] // 2
    ff = up_weight.shape[2] // 2
    heads = width // HD
    w = max(width, 128)

    def split(mine, other):
        return jnp.where(at_first, mine, other), jnp.where(at_first, other, mine)

    def half(value, which, axis):
        size = value.shape[axis] // 2
        return lax.dynamic_slice_in_dim(value, which * size, size, axis)

    def padded(value, axis):
        if w == width:
            return value
        pads = [(0, 0)] * value.ndim
        pads[axis] = (0, w - width)
        return jnp.pad(value, pads)

    def packs(which):
        qkv = padded(half(qkv_weight[0], which, 2), 2).reshape(share, 3 * w)
        main = jnp.concatenate([qkv, half(up_weight[0], which, 1)], axis=1)
        low = jnp.concatenate(
            [padded(half(out_weight[0], which, 0), 0), half(down_weight[0], which, 0)], axis=0
        )
        return main, low

    main_mine, low_mine = packs(stage)
    main_sent, low_sent = packs(1 - stage)
    mains = split(main_mine, swap(main_sent, "pipe", 0))
    lows = split(low_mine, swap(low_sent, "pipe", 0))

    piece = gains.shape[2]
    small = jnp.concatenate([gains[0].reshape(-1), biases[0].reshape(-1)])
    small = gather_tensor(small).reshape(-1)
    small = jnp.concatenate([small, qkv_bias[0].reshape(-1), up_bias[0]])
    small = jnp.stack(split(small, swap(small, "pipe", 0)))
    small = lax.all_gather(small, "dp", axis=0)
    small = jnp.moveaxis(small, 0, 1).astype(F32)
    norms = small[:, :, : tensor * 6 * piece].reshape(2, dp, tensor, 6, piece)
    norms = norms.transpose(0, 3, 2, 1, 4).reshape(2, 6, D)
    rest = small[:, :, tensor * 6 * piece :]
    qkv_biases = rest[:, :, : 3 * piece].reshape(2, dp, 3, piece)
    qkv_biases = qkv_biases.transpose(0, 2, 1, 3).reshape(2, 3, 2 * width)
    qkv_biases = padded(half(qkv_biases, stage, 2), 2).reshape(2, 1, 3 * w)
    up_biases = half(rest[:, :, 3 * piece :].reshape(2, 1, 2 * ff), stage, 2)

    layers = []
    for layer in range(2):
        main = lax.all_gather(mains[layer], "dp", axis=0, tiled=True)
        low = lax.all_gather(lows[layer], "dp", axis=0)
        layers.append(
            dict(
                w=w,
                heads=heads,
                qkv=main[:, : 3 * w],
                up=main[:, 3 * w :],
                low=low,
                norms=norms[layer],
                qkv_bias=qkv_biases[layer],
                up_bias=up_biases[layer],
            )
        )

    tiles = boundary[0, :, 0]
    angles = [angles_for(lengths[unit, 0], w) for unit in range(MB)]
    x_rows, cot_rows = [], []
    for unit in range(MB):
        x_own, cot_own = split(tiles[unit], swap(tiles[unit], "pipe", 0))
        x_rows.append(x_own)
        cot_rows.append(cot_own)
    x_blocks = [gather_blocks(rows) for rows in x_rows]
    c_blocks = [gather_blocks(rows) for rows in cot_rows]

    def forward(blocks, layer, unit):
        kept = project(index, blocks, layers[layer], angles[unit])
        keep, send, context, logs = attend(index, kept, layers[layer], angles[unit])
        return scatter_tensor(keep, send), [*kept, context, logs]

    def finish(rows, value, layer):
        own, other = sum_pipe(value)
        bias = layers[layer]["norms"]
        return rows.astype(F32) + own.astype(F32) + other.astype(F32) + (bias[4] + bias[5])

    kept = [[None] * MB, [None] * MB]
    middle_rows, middle_blocks, outputs = [], [None] * MB, []
    for unit in range(MB):
        value, kept[0][unit] = forward(x_blocks[unit], 0, unit)
        middle_rows.append(finish(x_rows[unit], value, 0).astype(BF))
    back = [[None] * MB, [None] * MB]
    cot0_rows, ends = [], []
    for unit in range(MB):
        middle_blocks[unit] = gather_blocks(middle_rows[unit])
        value, kept[1][unit] = forward(middle_blocks[unit], 1, unit)
        outputs.append(finish(middle_rows[unit], value, 1))
        keep, send, *back[1][unit] = backward(
            index, c_blocks[unit], middle_blocks[unit], kept[1][unit], layers[1], angles[unit]
        )
        own, other = sum_pipe(scatter_tensor(keep, send))
        cot0_rows.append(norm_back(middle_rows[unit], own, other, cot_rows[unit], BF))

    def grads_of(layer, blocks):
        inner = []
        for unit in range(MB):
            grad_raw, grad_pre = back[layer][unit][:2]
            first, second = kept[layer][unit][:2]
            hidden, context = kept[layer][unit][5], kept[layer][unit][7]
            inner.append([grad_raw, grad_pre, context, hidden, first, second])
        main, low = weight_grads(index, blocks, inner, dp)
        main = lax.psum_scatter(main, "dp", scatter_dimension=0)
        low = lax.psum_scatter(low, "dp", scatter_dimension=0)
        return main, low

    reduced = [None, grads_of(1, c_blocks)]
    cot0_blocks = []
    for unit in range(MB):
        cot0_blocks.append(gather_blocks(cot0_rows[unit]))
        keep, send, *back[0][unit] = backward(
            index, cot0_blocks[unit], x_blocks[unit], kept[0][unit], layers[0], angles[unit]
        )
        own, other = sum_pipe(scatter_tensor(keep, send))
        ends.append(norm_back(x_rows[unit], own, other, cot0_rows[unit], F32))
    reduced[0] = grads_of(0, cot0_blocks)
    ends = jnp.stack([jnp.where(at_first, ends[unit], outputs[unit]) for unit in range(MB)])

    def join(parts, axis):
        keep = jnp.where(at_first, parts[0], parts[1])
        other = swap(jnp.where(at_first, parts[1], parts[0]), "pipe", 0)
        return jnp.concatenate(split(keep, other), axis=axis)

    main = join([reduced[layer][0][None] for layer in range(2)], 0)
    low = join([reduced[layer][1][None] for layer in range(2)], 0)
    grad_qkv = main[:, : 3 * w].reshape(2, 3, w, share)[:, :, :width]
    grad_qkv = grad_qkv.transpose(3, 1, 0, 2).reshape(share, 3, 2 * width).astype(F32)
    grad_up = main[:, 3 * w :].reshape(2 * ff, share).T.astype(F32)
    grad_out = low[:, :width].reshape(2 * width, share).astype(F32)
    grad_down = low[:, w:].reshape(2 * ff, share).astype(F32)

    own_rows = [
        jnp.sum(jnp.stack([row.astype(F32) for row in rows]), axis=(0, 1))
        for rows in (cot0_rows, cot_rows)
    ]
    once = jnp.where(at_first, 1.0, 0.0)
    tails, raw_sums, pre_sums = [], [], []
    for layer in range(2):
        sums = [sum(back[layer][unit][i] for unit in range(MB)) for i in range(2, 5)]
        tails.append(jnp.concatenate([sums[0][:4], own_rows[layer][None] * once]))
        raw_sums.append(sums[1].reshape(3, w)[:, :width])
        pre_sums.append(sums[2][0])
    mine = jnp.where(at_first, tails[0], tails[1])
    mine = mine + swap(jnp.where(at_first, tails[1], tails[0]), "pipe", 0)
    mine = mine.reshape(5, tensor, D // tensor).transpose(1, 0, 2)
    place = lax.axis_index("tensor")
    for bit in range(bits_of("tensor")):
        own = (place >> bit) & 1
        pairs = mine.reshape((mine.shape[0] // 2, 2) + mine.shape[1:])
        mine = pick(pairs, own, 1) + swap(pick(pairs, 1 - own, 1), "tensor", bit)
    mine = mine[0].reshape(5, dp, piece).transpose(1, 0, 2).reshape(dp, 5 * piece)
    flat_qkv = join(raw_sums, 1)
    flat_qkv = flat_qkv.reshape(3, dp, piece).transpose(1, 0, 2).reshape(dp, 3 * piece)
    flat_up = join(pre_sums, 0).reshape(dp, -1)
    vector = scatter_line(jnp.concatenate([mine, flat_qkv, flat_up], axis=1), "dp", F32)
    norm_grads = vector[: 5 * piece].reshape(5, piece)
    grad_gains = norm_grads[:2]
    grad_biases = jnp.concatenate([norm_grads[2:5], norm_grads[4:5]])
    grad_qkv_bias = vector[5 * piece : 8 * piece].reshape(3, piece)
    grad_up_bias = vector[8 * piece :]
    return (
        ends[None, :, None],
        grad_gains[None],
        grad_biases[None],
        grad_qkv[None],
        grad_qkv_bias[None],
        grad_out[None],
        grad_up[None],
        grad_up_bias[None],
        grad_down[None],
    )


def solution(mesh):
    placed = (
        P("pipe", None, "dp", "tensor", None),
        P(None, "dp", None),
        P("pipe", None, ("tensor", "dp")),
        P("pipe", None, ("tensor", "dp")),
        P("pipe", "dp", None, "tensor"),
        P("pipe", None, ("tensor", "dp")),
        P("pipe", "tensor", "dp"),
        P("pipe", "dp", "tensor"),
        P("pipe", ("tensor", "dp")),
        P("pipe", "tensor", "dp"),
    )
    return jax.shard_map(
        body,
        mesh=mesh,
        in_specs=placed,
        out_specs=(placed[0],) + placed[2:],
        check_vma=False,
    )
```

```python
import functools

import jax
import jax.numpy as jnp
from jax import lax
from jax.experimental import pallas as pl
from jax.experimental.pallas import tpu as pltpu
from jax.sharding import PartitionSpec as P

D = 1024
H = 16
HD = 64
ROT = 16
MB = 2
TOK_MB = 1280
EPS = 1e-05
CHUNK = 256
FLOPS = 10**11
BF = jnp.bfloat16
F32 = jnp.float32
ANY = pl.BlockSpec(memory_space=pl.ANY)
VMEM = pl.BlockSpec(memory_space=pltpu.VMEM)
SMEM = pl.BlockSpec(memory_space=pltpu.SMEM)


def dot(left, right, left_dim, right_dim):
    return lax.dot_general(
        left, right, (((left_dim,), (right_dim,)), ((), ())), preferred_element_type=F32
    )


def shape(dims, dtype):
    return jax.ShapeDtypeStruct(dims, dtype)


def swap(value, axis, bit):
    count = lax.axis_size(axis)
    return lax.ppermute(value, axis, [(i, i ^ (1 << bit)) for i in range(count)])


def bits_of(axis):
    return lax.axis_size(axis).bit_length() - 1


def pick(value, index, axis):
    return lax.dynamic_index_in_dim(value, index, axis, keepdims=False)


def gather_blocks(value):
    blocks = {0: value}
    for bit in reversed(range(bits_of("tensor"))):
        for s in list(blocks):
            blocks[s | (1 << bit)] = swap(blocks[s], "tensor", bit)
    return [blocks[s] for s in range(len(blocks))]


def gather_tensor(value):
    index = lax.axis_index("tensor")
    value = value[None]
    for bit in reversed(range(bits_of("tensor"))):
        other = swap(value, "tensor", bit)
        mine = ((index >> bit) & 1) == 0
        low = jnp.where(mine, value, other)
        high = jnp.where(mine, other, value)
        value = jnp.stack([low, high], axis=1).reshape((-1,) + value.shape[1:])
    return value


def after(value, *others):
    return lax.optimization_barrier((value, *others))[0]


def line_parts(value, axis):
    count = lax.axis_size(axis)
    left, right = [value], [value]
    for hop in range(1, count):
        left.append(lax.ppermute(left[-1], axis, [(j, j + 1) for j in range(hop - 1, count - 1)]))
        right.append(lax.ppermute(right[-1], axis, [(j + 1, j) for j in range(count - hop)]))
    return left + right[1:]


def gather_direct(value, axis):
    count = lax.axis_size(axis)
    index = lax.axis_index(axis)
    found = [value]
    for hop in range(1, count):
        found.append(lax.ppermute(value, axis, [(j, (j + hop) % count) for j in range(count)]))
    turned = jnp.stack(found[::-1] * 2)
    return lax.dynamic_slice_in_dim(turned, count - 1 - index, count, 0)


def scatter_direct(value, axis):
    count = lax.axis_size(axis)
    index = lax.axis_index(axis)
    total = pick(value, index, 0)
    for hop in range(1, count):
        sent = pick(value, (index + hop) % count, 0)
        total = total + lax.ppermute(sent, axis, [(j, (j + hop) % count) for j in range(count)])
    return total


def copies_of_blocks(index, blocks, target, sems):
    copies = []
    for s, block in enumerate(blocks):
        rows = block.shape[0]
        where = pl.multiple_of((index ^ s) * rows, rows)
        copies.append(pltpu.make_async_copy(block, target.at[pl.ds(where, rows)], sems.at[s]))
    return copies


def copies_to_halves(index, source, keep, send, sems, rows):
    copies = []
    own = index & 1
    for block in range(source.shape[0] // rows):
        part = source.at[pl.ds(block * rows, rows)]
        copies.append(
            (
                own == block & 1,
                pltpu.make_async_copy(part, keep.at[block >> 1], sems.at[block]),
                pltpu.make_async_copy(part, send.at[block >> 1], sems.at[block]),
            )
        )
    return copies


def start_half(copy):
    is_kept, to_keep, to_send = copy

    @pl.when(is_kept)
    def _():
        to_keep.start()

    @pl.when(jnp.logical_not(is_kept))
    def _():
        to_send.start()


def normalize(rows):
    rows = rows.astype(F32)
    centered = rows - jnp.mean(rows, axis=-1, keepdims=True)
    scale = lax.rsqrt(jnp.mean(centered * centered, axis=-1, keepdims=True) + EPS)
    return centered * scale, scale


def gelu_pair(values):
    share = 0.5 * (1.0 + lax.erf(values * 0.7071067811865476))
    density = jnp.exp(-0.5 * values * values) * 0.3989422804014327
    return values * share, share + values * density


def rotate(values, table_cos, table_sin, sign):
    width = values.shape[1]
    half = ROT // 2
    lanes = lax.broadcasted_iota(jnp.int32, values.shape, 1) % HD
    partner = jnp.where(
        lanes < half, pltpu.roll(values, width - half, 1), pltpu.roll(values, half, 1)
    )
    return values * table_cos + partner * (table_sin * sign)


def unpack_table(packed, sign):
    width = packed.shape[1]
    lanes = lax.broadcasted_iota(jnp.int32, packed.shape, 1) % HD
    table_cos = jnp.where(lanes < ROT, packed, 1.0)
    table_sin = jnp.where(lanes < ROT, pltpu.roll(packed, width - ROT, 1) * sign, 0.0)
    return table_cos, table_sin


def rotate(values, table_cos, table_sin):
    width = values.shape[1]
    half = ROT // 2
    lanes = lax.broadcasted_iota(jnp.int32, values.shape, 1) % HD
    partner = jnp.where(
        lanes < half, pltpu.roll(values, width - half, 1), pltpu.roll(values, half, 1)
    )
    return values * table_cos + partner * table_sin


def chunks():
    return [slice(begin, begin + CHUNK) for begin in range(0, TOK_MB, CHUNK)]


class Order:
    def __init__(self):
        self.last = []

    def hold(self, *values):
        self.last = [*self.last, *values]

    def call(self, kernel, name, vmem, in_specs, out_specs, out_shape, scratch, args, **more):
        count = len(args)
        deps = self.last

        def outer(*refs):
            kernel(*refs[:count], *refs[count + len(deps) :])

        results = pl.pallas_call(
            outer,
            in_specs=in_specs + [ANY] * len(deps),
            out_specs=out_specs,
            out_shape=out_shape,
            scratch_shapes=scratch,
            compiler_params=pltpu.CompilerParams(vmem_limit_bytes=vmem << 20),
            cost_estimate=pl.CostEstimate(
                flops=FLOPS, bytes_accessed=1024, transcendentals=0
            ),
            name=name,
            **more,
        )(*args, *deps)
        self.last = [min(results, key=lambda result: result.size)]
        return results

    def pause(self):
        def nothing(out_ref):
            out_ref[...] = jnp.zeros_like(out_ref)

        self.call(nothing, "pause", 2, [], [VMEM], [shape((8, 128), F32)], [], [])


def loads_of_weights(source, row, target, sems, first=0):
    dp, _, share = source.shape
    rows = target.shape[0]
    return [
        pltpu.make_async_copy(
            source.at[j, pl.ds(row, rows)],
            target.at[:, pl.ds(j * share, share)],
            sems.at[first + j],
        )
        for j in range(dp)
    ]


def start_all(copies):
    for copy in copies:
        copy.start()


def wait_all(copies):
    for copy in copies:
        copy.wait()


class Leaving:
    def __init__(self, index, source, keep, send, sems):
        self.rows = keep.shape[1]
        self.copies = copies_to_halves(index, source, keep, send, sems, self.rows)
        self.done = 0

    def reached(self, end):
        while self.done < len(self.copies) and (self.done + 1) * self.rows <= end:
            start_half(self.copies[self.done])
            self.done += 1

    def wait(self):
        for copy in self.copies:
            copy[1].wait()


def masked(scores, starts, begin):
    key = lax.broadcasted_iota(jnp.int32, scores.shape, 0)
    query = lax.broadcasted_iota(jnp.int32, scores.shape, 1) + begin
    return jnp.where((key <= query) & (key >= starts), scores, -1e30)


def head_only(values, head):
    lanes = lax.broadcasted_iota(jnp.int32, values.shape, 1)
    inside = (lanes >= head * HD) & (lanes < (head + 1) * HD)
    return jnp.where(inside, values, jnp.zeros_like(values))


def turned_back(parts, w):
    rest = w - len(parts) * HD
    if rest:
        parts = parts + [jnp.zeros((rest, parts[0].shape[1]), F32)]
    return jnp.concatenate(parts, axis=0).T


def do_project(w, x_all, main, norms_ref, bias_ref, table_ref, q_ref, k_ref, v_ref, hidden_ref, slope_ref):
    for at in chunks():
        hat, _ = normalize(x_all[at])
        first = (hat * norms_ref[0:1] + norms_ref[2:3]).astype(BF)
        second = (hat * norms_ref[1:2] + norms_ref[3:4]).astype(BF)
        raw = dot(first, main[: 3 * w], 1, 1) + bias_ref[:, : 3 * w]
        table_cos, table_sin = unpack_table(table_ref[at], 1.0)
        q_ref[at] = rotate(raw[:, :w], table_cos, table_sin).astype(BF)
        k_ref[at] = rotate(raw[:, w : 2 * w], table_cos, table_sin).astype(BF)
        v_ref[at] = raw[:, 2 * w :].astype(BF)
        hidden, slope = gelu_pair(dot(second, main[3 * w :], 1, 1) + bias_ref[:, 3 * w :])
        hidden_ref[at] = hidden.astype(BF)
        slope_ref[at] = slope.astype(BF)


def do_attend(heads, w, starts_ref, q_ref, k_ref, v_ref, hidden_ref, low, loads, context_ref, logs_ref, v_turned, partial, leaving):
    v_turned[...] = v_ref[...].T
    logs_ref[...] = jnp.zeros_like(logs_ref)
    for at in chunks():
        starts = starts_ref[:, at]
        queries = q_ref[at] * BF(HD**-0.5)
        turned = []
        for head in range(heads):
            s = dot(k_ref[: at.stop], head_only(queries, head), 1, 1)
            s = masked(s, starts, at.start)
            top = jnp.max(s, axis=0, keepdims=True)
            e = jnp.exp(s - top)
            total = jnp.sum(e, axis=0, keepdims=True)
            part = v_turned[head * HD : (head + 1) * HD, : at.stop]
            turned.append(dot(part, e.astype(BF), 1, 0) / total)
            logs_ref[head : head + 1, at] = top + jnp.log(total)
        context = turned_back(turned, w).astype(BF)
        context_ref[at] = context
        if at.start == 0:
            wait_all(loads)
        total = dot(context, low[:w], 1, 0) + dot(hidden_ref[at], low[w:], 1, 0)
        partial[at] = total.astype(BF)
        leaving.reached(at.stop)


def do_enter(w, c_all, low, slope_ref, grad_context, pre_ref, sum_ref):
    total = jnp.zeros(sum_ref.shape, F32)
    for at in chunks():
        both = dot(c_all[at], low[...], 1, 1)
        grad_context[at] = both[:, :w].astype(BF)
        grad_pre = (both[:, w:] * slope_ref[at].astype(F32)).astype(BF)
        pre_ref[at] = grad_pre
        total = total + jnp.sum(grad_pre.astype(F32), axis=0, keepdims=True)
    sum_ref[...] = total


def do_backward(
    heads,
    w,
    starts_ref,
    q_ref,
    k_ref,
    v_ref,
    context_ref,
    logs_ref,
    grad_context,
    pre_ref,
    x_loads,
    x_all,
    main,
    norms_ref,
    table_ref,
    raw_ref,
    vectors_ref,
    sum_ref,
    k_turned,
    grad_q,
    grad_k,
    grad_v,
    partial,
    leaving,
):
    k_turned[...] = (k_ref[...] * BF(HD**-0.5)).T
    grad_k[...] = jnp.zeros_like(grad_k)
    grad_v[...] = jnp.zeros_like(grad_v)
    for at in chunks():
        starts = starts_ref[:, at]
        queries = q_ref[at] * BF(HD**-0.5)
        grads = grad_context[at]
        products = (grads.astype(F32) * context_ref[at].astype(F32)).T
        to_k = to_v = 0.0
        turned = []
        for head in range(heads):
            lanes = slice(head * HD, (head + 1) * HD)
            q, g = head_only(queries, head), head_only(grads, head)
            weighted = jnp.sum(products[lanes], axis=0, keepdims=True)
            s = masked(dot(k_ref[: at.stop], q, 1, 1), starts, at.start)
            p = jnp.exp(s - logs_ref[head : head + 1, at])
            grad_p = dot(v_ref[: at.stop], g, 1, 1)
            grad_s = (p * (grad_p - weighted)).astype(BF)
            to_k = to_k + dot(grad_s, q, 1, 0)
            to_v = to_v + dot(p.astype(BF), g, 1, 0)
            turned.append(dot(k_turned[lanes, : at.stop], grad_s, 1, 0))
        grad_k[: at.stop] += to_k
        grad_v[: at.stop] += to_v
        grad_q[at] = turned_back(turned, w)
    wait_all(x_loads)
    sums = [jnp.zeros((1, D), F32) for _ in range(4)]
    raw_sum = jnp.zeros(sum_ref.shape, F32)
    for at in chunks():
        table_cos, table_sin = unpack_table(table_ref[at], -1.0)
        grad_raw = jnp.concatenate(
            [
                rotate(grad_q[at], table_cos, table_sin),
                rotate(grad_k[at], table_cos, table_sin),
                grad_v[at],
            ],
            axis=1,
        ).astype(BF)
        raw_ref[at] = grad_raw
        raw_sum = raw_sum + jnp.sum(grad_raw.astype(F32), axis=0, keepdims=True)
        grad_first = dot(grad_raw, main[: 3 * w], 1, 0)
        grad_second = dot(pre_ref[at], main[3 * w :], 1, 0)
        hat, _ = normalize(x_all[at])
        for i, term in enumerate(
            (grad_first * hat, grad_second * hat, grad_first, grad_second)
        ):
            sums[i] = sums[i] + jnp.sum(term, axis=0, keepdims=True)
        partial[at] = (grad_first * norms_ref[0:1] + grad_second * norms_ref[1:2]).astype(BF)
        leaving.reached(at.stop)
    vectors_ref[...] = jnp.concatenate(sums + [jnp.zeros((4, D), F32)], axis=0)
    sum_ref[...] = raw_sum


def rows_of(*widths):
    return [shape((TOK_MB, width), BF) for width in widths]


def halves_of(blocks):
    return [shape((blocks // 2, TOK_MB // blocks, D), BF)] * 2


def held(*widths):
    return [pltpu.VMEM((TOK_MB, width), BF) for width in widths]


def dma(*counts):
    return [pltpu.SemaphoreType.DMA((count,)) for count in counts]


def project_kernel(blocks, w, row, *refs):
    index_ref = refs[0]
    x_refs = refs[1 : 1 + blocks]
    main_ref, norms_ref, bias_ref, table_ref = refs[1 + blocks : 5 + blocks]
    outs = refs[5 + blocks : 10 + blocks]
    x_all, main, x_sems, main_sems = refs[10 + blocks :]
    loads = copies_of_blocks(index_ref[0], x_refs, x_all, x_sems)
    loads += loads_of_weights(main_ref, row, main, main_sems)
    start_all(loads)
    wait_all(loads)
    do_project(w, x_all, main, norms_ref, bias_ref, table_ref, *outs)


def project(order, index, x_blocks, weights, angles):
    blocks = len(x_blocks)
    w, ff = weights["w"], weights["ff"]
    main, row = weights["main"]
    return order.call(
        functools.partial(project_kernel, blocks, w, row),
        "project",
        24,
        [SMEM] + [ANY] * (blocks + 1) + [VMEM] * 3,
        [VMEM] * 5,
        rows_of(w, w, w, ff, ff),
        held(D) + [pltpu.VMEM((3 * w + ff, D), BF)] + dma(blocks, main.shape[0]),
        [index, *x_blocks, main, weights["norms"], weights["bias"], angles[1]],
    )


def attend_kernel(heads, w, row, *refs):
    index_ref, starts_ref, q_ref, k_ref, v_ref, hidden_ref, low_ref = refs[:7]
    keep_ref, send_ref, context_ref, logs_ref = refs[7:11]
    low, partial, v_turned, low_sems, out_sems = refs[11:]
    loads = loads_of_weights(low_ref, row, low, low_sems)
    start_all(loads)
    leaving = Leaving(index_ref[0], partial, keep_ref, send_ref, out_sems)
    do_attend(
        heads,
        w,
        starts_ref,
        q_ref,
        k_ref,
        v_ref,
        hidden_ref,
        low,
        loads,
        context_ref,
        logs_ref,
        v_turned,
        partial,
        leaving,
    )
    leaving.wait()


def attend(order, index, blocks, kept, weights, angles):
    w, heads, ff = weights["w"], weights["heads"], weights["ff"]
    low, row = weights["low"]
    return order.call(
        functools.partial(attend_kernel, heads, w, row),
        "attend",
        28,
        [SMEM] + [VMEM] * 5 + [ANY],
        [ANY, ANY, VMEM, VMEM],
        halves_of(blocks) + rows_of(w) + [shape((8, TOK_MB), F32)],
        [pltpu.VMEM((w + ff, D), BF)]
        + held(D)
        + [pltpu.VMEM((w, TOK_MB), BF)]
        + dma(low.shape[0], blocks),
        [index, angles[0], *kept[:4], low],
    )


def enter_kernel(blocks, w, row, *refs):
    index_ref = refs[0]
    c_refs = refs[1 : 1 + blocks]
    low_ref, slope_ref = refs[1 + blocks : 3 + blocks]
    context_ref, pre_ref, sum_ref = refs[3 + blocks : 6 + blocks]
    c_all, low, c_sems, low_sems = refs[6 + blocks :]
    loads = loads_of_weights(low_ref, row, low, low_sems)
    loads += copies_of_blocks(index_ref[0], c_refs, c_all, c_sems)
    start_all(loads)
    wait_all(loads)
    do_enter(w, c_all, low, slope_ref, context_ref, pre_ref, sum_ref)


def enter(order, index, c_blocks, kept, weights):
    w, ff = weights["w"], weights["ff"]
    low, row = weights["low"]
    blocks = len(c_blocks)
    return order.call(
        functools.partial(enter_kernel, blocks, w, row),
        "enter",
        20,
        [SMEM] + [ANY] * (blocks + 1) + [VMEM],
        [VMEM] * 3,
        rows_of(w, ff) + [shape((1, ff), F32)],
        held(D) + [pltpu.VMEM((w + ff, D), BF)] + dma(blocks, low.shape[0]),
        [index, *c_blocks, low, kept[4]],
    )


def scratch_of_backward(w):
    return [pltpu.VMEM((w, TOK_MB), BF)] + [pltpu.VMEM((TOK_MB, w), F32)] * 3


def backward_kernel(blocks, heads, w, row, *refs):
    index_ref = refs[0]
    x_refs = refs[1 : 1 + blocks]
    inner = refs[1 + blocks : 9 + blocks]
    main_ref, norms_ref, table_ref = refs[9 + blocks : 12 + blocks]
    keep_ref, send_ref, *outs = refs[12 + blocks : 17 + blocks]
    x_all, main, partial, *scratch, x_sems, main_sems, out_sems = refs[17 + blocks :]
    loads = copies_of_blocks(index_ref[0], x_refs, x_all, x_sems)
    loads += loads_of_weights(main_ref, row, main, main_sems)
    start_all(loads)
    leaving = Leaving(index_ref[0], partial, keep_ref, send_ref, out_sems)
    do_backward(
        heads, w, *inner, loads, x_all, main, norms_ref, table_ref, *outs, *scratch, partial, leaving
    )
    leaving.wait()


def backward(order, index, x_blocks, kept, entered, weights, angles):
    queries, keys, values, _, _, context, logs = kept
    blocks = len(x_blocks)
    w, heads, ff = weights["w"], weights["heads"], weights["ff"]
    main, row = weights["main"]
    return order.call(
        functools.partial(backward_kernel, blocks, heads, w, row),
        "backward",
        36,
        [SMEM] + [ANY] * blocks + [VMEM] * 8 + [ANY] + [VMEM] * 2,
        [ANY, ANY] + [VMEM] * 3,
        halves_of(blocks) + rows_of(3 * w) + [shape((8, D), F32), shape((1, 3 * w), F32)],
        held(D)
        + [pltpu.VMEM((3 * w + ff, D), BF)]
        + held(D)
        + scratch_of_backward(w)
        + dma(blocks, main.shape[0], blocks),
        [
            index,
            *x_blocks,
            angles[0],
            queries,
            keys,
            values,
            context,
            logs,
            entered[0],
            entered[1],
            main,
            weights["norms"],
            angles[1],
        ],
    )


def whole_backward_kernel(blocks, heads, w, main_row, low_row, *refs):
    index_ref = refs[0]
    c_refs = refs[1 : 1 + blocks]
    x_refs = refs[1 + blocks : 1 + 2 * blocks]
    starts_ref, q_ref, k_ref, v_ref, context_ref, logs_ref, slope_ref = refs[
        1 + 2 * blocks : 8 + 2 * blocks
    ]
    main_ref, low_ref, norms_ref, table_ref = refs[8 + 2 * blocks : 12 + 2 * blocks]
    keep_ref, send_ref, pre_ref, pre_sum_ref, *outs = refs[12 + 2 * blocks : 19 + 2 * blocks]
    c_all, x_all, main, low, partial, grad_context, *scratch = refs[19 + 2 * blocks : 29 + 2 * blocks]
    c_sems, x_sems, main_sems, low_sems, out_sems = refs[29 + 2 * blocks :]
    loads = loads_of_weights(low_ref, low_row, low, low_sems)
    loads += copies_of_blocks(index_ref[0], c_refs, c_all, c_sems)
    later = copies_of_blocks(index_ref[0], x_refs, x_all, x_sems)
    later += loads_of_weights(main_ref, main_row, main, main_sems)
    start_all(loads + later)
    leaving = Leaving(index_ref[0], partial, keep_ref, send_ref, out_sems)
    wait_all(loads)
    do_enter(w, c_all, low, slope_ref, grad_context, pre_ref, pre_sum_ref)
    do_backward(
        heads,
        w,
        starts_ref,
        q_ref,
        k_ref,
        v_ref,
        context_ref,
        logs_ref,
        grad_context,
        pre_ref,
        later,
        x_all,
        main,
        norms_ref,
        table_ref,
        *outs,
        *scratch,
        partial,
        leaving,
    )
    leaving.wait()


def whole_backward(order, index, c_blocks, x_blocks, kept, weights, angles):
    queries, keys, values, _, slope, context, logs = kept
    blocks = len(x_blocks)
    w, heads, ff = weights["w"], weights["heads"], weights["ff"]
    main, main_row = weights["main"]
    low, low_row = weights["low"]
    dp = main.shape[0]
    return order.call(
        functools.partial(whole_backward_kernel, blocks, heads, w, main_row, low_row),
        "whole_backward",
        42,
        [SMEM] + [ANY] * (2 * blocks) + [VMEM] * 7 + [ANY] * 2 + [VMEM] * 2,
        [ANY, ANY] + [VMEM] * 5,
        halves_of(blocks)
        + rows_of(ff)
        + [shape((1, ff), F32)]
        + rows_of(3 * w)
        + [shape((8, D), F32), shape((1, 3 * w), F32)],
        held(D, D)
        + [pltpu.VMEM((3 * w + ff, D), BF), pltpu.VMEM((w + ff, D), BF)]
        + held(D, w)
        + scratch_of_backward(w)
        + dma(blocks, blocks, dp, dp, blocks),
        [
            index,
            *c_blocks,
            *x_blocks,
            angles[0],
            queries,
            keys,
            values,
            context,
            logs,
            slope,
            main,
            low,
            weights["norms"],
            angles[1],
        ],
    )


def layer_kernel(blocks, heads, w, main_row, low_row, *refs):
    index_ref = refs[0]
    c_refs = refs[1 : 1 + blocks]
    x_refs = refs[1 + blocks : 1 + 2 * blocks]
    starts_ref, main_ref, low_ref, norms_ref, bias_ref, table_ref = refs[
        1 + 2 * blocks : 7 + 2 * blocks
    ]
    (y_keep, y_send, u_keep, u_send, hidden_ref, context_ref, pre_ref, pre_sum_ref, *outs) = refs[
        7 + 2 * blocks : 18 + 2 * blocks
    ]
    (c_all, x_all, main, low, y_all, u_all, q_ref, k_ref, v_ref, slope_ref, grad_context) = refs[
        18 + 2 * blocks : 29 + 2 * blocks
    ]
    logs_ref, v_turned, *scratch = refs[29 + 2 * blocks : 35 + 2 * blocks]
    c_sems, x_sems, main_sems, low_sems, y_sems, u_sems = refs[35 + 2 * blocks :]
    index = index_ref[0]
    loads = copies_of_blocks(index, x_refs, x_all, x_sems)
    loads += loads_of_weights(main_ref, main_row, main, main_sems)
    low_loads = loads_of_weights(low_ref, low_row, low, low_sems)
    c_loads = copies_of_blocks(index, c_refs, c_all, c_sems)
    start_all(loads + low_loads + c_loads)
    y_leaving = Leaving(index, y_all, y_keep, y_send, y_sems)
    u_leaving = Leaving(index, u_all, u_keep, u_send, u_sems)
    wait_all(loads)
    do_project(
        w, x_all, main, norms_ref, bias_ref, table_ref, q_ref, k_ref, v_ref, hidden_ref, slope_ref
    )
    do_attend(
        heads,
        w,
        starts_ref,
        q_ref,
        k_ref,
        v_ref,
        hidden_ref,
        low,
        low_loads,
        context_ref,
        logs_ref,
        v_turned,
        y_all,
        y_leaving,
    )
    wait_all(c_loads)
    do_enter(w, c_all, low, slope_ref, grad_context, pre_ref, pre_sum_ref)
    do_backward(
        heads,
        w,
        starts_ref,
        q_ref,
        k_ref,
        v_ref,
        context_ref,
        logs_ref,
        grad_context,
        pre_ref,
        [],
        x_all,
        main,
        norms_ref,
        table_ref,
        *outs,
        *scratch,
        u_all,
        u_leaving,
    )
    y_leaving.wait()
    u_leaving.wait()


def whole_layer(order, index, c_blocks, x_blocks, weights, angles):
    blocks = len(x_blocks)
    w, heads, ff = weights["w"], weights["heads"], weights["ff"]
    main, main_row = weights["main"]
    low, low_row = weights["low"]
    dp = main.shape[0]
    return order.call(
        functools.partial(layer_kernel, blocks, heads, w, main_row, low_row),
        "whole_layer",
        60,
        [SMEM] + [ANY] * (2 * blocks) + [VMEM] + [ANY] * 2 + [VMEM] * 3,
        [ANY] * 4 + [VMEM] * 7,
        halves_of(blocks)
        + halves_of(blocks)
        + rows_of(ff, w, ff)
        + [shape((1, ff), F32)]
        + rows_of(3 * w)
        + [shape((8, D), F32), shape((1, 3 * w), F32)],
        held(D, D)
        + [pltpu.VMEM((3 * w + ff, D), BF), pltpu.VMEM((w + ff, D), BF)]
        + held(D, D, w, w, w, ff, w)
        + [pltpu.VMEM((8, TOK_MB), F32), pltpu.VMEM((w, TOK_MB), BF)]
        + scratch_of_backward(w)
        + dma(blocks, blocks, dp, dp, blocks, blocks),
        [
            index,
            *c_blocks,
            *x_blocks,
            angles[0],
            main,
            low,
            weights["norms"],
            weights["bias"],
            angles[1],
        ],
    )


def fill(target, begin, lefts, rights):
    dp, _, share = target.shape
    size = lefts[0].shape[1]
    for j in range(dp):
        cols = slice(j * share, (j + 1) * share)
        total = sum(dot(left[...], right[:, cols], 0, 0) for left, right in zip(lefts, rights))
        target[j, begin : begin + size] = total.astype(BF)


def grads_kernel(blocks, plan, *refs):
    index_ref, norms_ref = refs[:2]
    with_cot = None in plan
    normed = sorted({which for which in plan if which is not None})
    sets = with_cot + bool(normed)
    count = MB * blocks
    c_refs = refs[2 : 2 + count * with_cot]
    x_refs = refs[2 + count * with_cot : 2 + count * sets]
    lefts = refs[2 + count * sets : 2 + count * sets + MB * len(plan)]
    out_ref, *scratch = refs[2 + count * sets + MB * len(plan) :]
    sems = scratch.pop()
    index = index_ref[0]

    def loads(source, target, which):
        copies = []
        for unit in range(MB):
            part = source[unit * blocks : (unit + 1) * blocks]
            copies += copies_of_blocks(index, part, target.at[unit], sems.at[which, unit])
        return copies

    rights = {}
    c_loads, x_loads = [], []
    if with_cot:
        rights[None] = scratch[0]
        c_loads = loads(c_refs, scratch[0], 0)
    if normed:
        x_loads = loads(x_refs, scratch[with_cot], 1)
    start_all(c_loads + x_loads)
    for i, which in enumerate(normed):
        rights[which] = scratch[with_cot + i]
    begin = 0
    wait_all(c_loads)
    for i, which in enumerate(plan):
        if which is not None and x_loads:
            wait_all(x_loads)
            x_loads = []
            raw = scratch[with_cot]
            for unit in range(MB):
                for at in chunks():
                    hat, _ = normalize(raw[unit, at])
                    for norm in normed:
                        row = hat * norms_ref[norm : norm + 1] + norms_ref[2 + norm : 3 + norm]
                        rights[norm][unit, at] = row.astype(BF)
        part = lefts[i * MB : (i + 1) * MB]
        fill(out_ref, begin, part, [rights[which].at[unit] for unit in range(MB)])
        begin += part[0].shape[1]


def weight_grads(order, index, c_blocks, x_blocks, pieces, norms, dp):
    plan = [which for _, which in pieces]
    blocks = len(x_blocks[0])
    rows = []
    if None in plan:
        rows += [block for unit in c_blocks for block in unit]
    if any(which is not None for which in plan):
        rows += [block for unit in x_blocks for block in unit]
    lefts = [left for part, _ in pieces for left in part]
    size = sum(part[0].shape[1] for part, _ in pieces)
    buffers = len(set(plan))
    return order.call(
        functools.partial(grads_kernel, blocks, plan),
        "weight_grads",
        60,
        [SMEM, VMEM] + [ANY] * len(rows) + [VMEM] * len(lefts),
        [VMEM],
        [shape((dp, size, D // dp), BF)],
        [pltpu.VMEM((MB, TOK_MB, D), BF)] * buffers
        + [pltpu.SemaphoreType.DMA((2, MB, blocks))],
        [index, norms, *rows, *lefts],
    )[0]


def pack_kernel(width, w, stage_ref, qkv_ref, up_ref, out_ref, down_ref, *refs):
    at_first = stage_ref[0] == 0
    ff = down_ref.shape[0] // 2
    mains, lows = refs[:2], refs[2:]

    def put(target, begin, size, low, high):
        target[0][begin : begin + size] = jnp.where(at_first, low, high)
        target[1][begin : begin + size] = jnp.where(at_first, high, low)

    if w != width:
        for ref in refs:
            ref[...] = jnp.zeros_like(ref)
    for i in range(3):
        turned = qkv_ref[i].T
        put(mains, i * w, width, turned[:width], turned[width:])
    turned = up_ref[...].T
    put(mains, 3 * w, ff, turned[:ff], turned[ff:])
    put(lows, 0, width, out_ref[:width], out_ref[width:])
    put(lows, w, ff, down_ref[:ff], down_ref[ff:])


def pack(order, stage, qkv, up, out, down, w):
    width = out.shape[0] // 2
    ff = down.shape[0] // 2
    share = out.shape[1]
    return order.call(
        functools.partial(pack_kernel, width, w),
        "pack",
        24,
        [SMEM] + [VMEM] * 4,
        [VMEM] * 4,
        [shape((3 * w + ff, share), BF)] * 2 + [shape((w + ff, share), BF)] * 2,
        [],
        [stage, qkv, up, out, down],
    )


def assemble_kernel(count, index_ref, *refs):
    parts, out_ref, sems = refs[: 2 * count - 1], refs[-2], refs[-1]
    index = index_ref[0]
    copies = [(index >= 0, pltpu.make_async_copy(parts[0], out_ref.at[index], sems.at[0]))]
    for hop in range(1, count):
        for sign, number in ((-1, hop), (1, count - 1 + hop)):
            place = index + sign * hop
            inside = (place >= 0) & (place < count)
            target = out_ref.at[jnp.clip(place, 0, count - 1)]
            copies.append(
                (inside, pltpu.make_async_copy(parts[number], target, sems.at[number]))
            )
    for inside, copy in copies:
        pl.when(inside)(copy.start)
    for inside, copy in copies:
        pl.when(inside)(copy.wait)


def assemble(order, index, parts):
    count = (len(parts) + 1) // 2
    return order.call(
        functools.partial(assemble_kernel, count),
        "assemble",
        4,
        [SMEM] + [ANY] * len(parts),
        [ANY],
        [shape((count, *parts[0].shape), BF)],
        dma(len(parts)),
        [index, *parts],
    )[0]


def by_stage_kernel(stage_ref, mine_ref, other_ref, *refs):
    at_first = stage_ref[0] == 0
    mine, other = mine_ref[...], other_ref[...]
    refs[-2][...] = jnp.where(at_first, mine, other)
    second = jnp.where(at_first, other, mine)
    if len(refs) > 2:
        rows = refs[0].shape[0]
        refs[-1][:rows] = refs[0][...]
        refs[-1][rows:] = second
    else:
        refs[-1][...] = second


def by_stage(order, stage, mine, other, above=()):
    rows = mine.shape[0] + sum(value.shape[0] for value in above)
    return order.call(
        by_stage_kernel,
        "by_stage",
        16,
        [SMEM] + [VMEM] * (2 + len(above)),
        [VMEM] * 2,
        [shape(mine.shape, BF), shape((rows, mine.shape[1]), BF)],
        [],
        [stage, mine, other, *above],
    )


def unpack_outer_kernel(width, w, ff, *refs):
    stage_ref, mine0, mine1, from0, from1, up_ref, out_ref, down_ref = refs
    at_first = stage_ref[0] == 0

    def halves(begin, size):
        rows = slice(begin, begin + size)
        low = jnp.where(at_first, mine0[rows], from1[rows])
        high = jnp.where(at_first, from0[rows], mine1[rows])
        return low.astype(F32), high.astype(F32)

    out_ref[:width], out_ref[width:] = halves(0, width)
    down_ref[:ff], down_ref[ff:] = halves(w, ff)
    low, high = halves(w + ff, ff)
    up_ref[:, :ff] = low.T
    up_ref[:, ff:] = high.T


def unpack_inner_kernel(width, w, stage_ref, mine0, mine1, from0, from1, qkv_ref):
    at_first = stage_ref[0] == 0
    for i in range(3):
        rows = slice(i * w, i * w + width)
        low = jnp.where(at_first, mine0[rows], from1[rows]).astype(F32)
        high = jnp.where(at_first, from0[rows], mine1[rows]).astype(F32)
        qkv_ref[i] = jnp.concatenate([low, high], axis=0).T


def unpack(kernel, order, stage, parts, out_shape):
    return order.call(
        kernel,
        "unpack",
        24,
        [SMEM] + [VMEM] * 4,
        [VMEM] * len(out_shape),
        out_shape,
        [],
        [stage, *parts],
    )


def picked_kernel(bit, flip, pairs, plains, *refs):
    index_ref = refs[0]
    out_ref, held, sems = refs[1 + pairs + plains :]
    want = (index_ref[0] >> bit) & 1
    if flip:
        want = 1 - want
    copies = []
    for i in range(pairs + plains):
        for j in range(out_ref.shape[0]):
            source = refs[1 + i].at[j, want] if i < pairs else refs[1 + i].at[j]
            copies.append(pltpu.make_async_copy(source, held.at[i, j], sems.at[i, j]))
    for copy in copies:
        copy.start()
    for copy in copies:
        copy.wait()
    total = held[0].astype(F32)
    for i in range(1, pairs + plains):
        total = total + held[i].astype(F32)
    out_ref[...] = total.astype(BF)


def picked_sum(order, where, bit, flip, pairs, plains=()):
    dims = (pairs[0].shape[0],) + pairs[0].shape[2:]
    terms = [*pairs, *plains]
    return order.call(
        functools.partial(picked_kernel, bit, flip, len(pairs), len(plains)),
        "picked_sum",
        20,
        [SMEM] + [ANY] * len(terms),
        [VMEM],
        [shape(dims, BF)],
        [
            pltpu.VMEM((len(terms), *dims), BF),
            pltpu.SemaphoreType.DMA((len(terms), dims[0])),
        ],
        [where, *terms],
    )[0]


class Sum:
    def __init__(self, where, keep, send):
        self.where = where
        self.terms = [keep, swap(send, "tensor", 0)]

    def send(self, order):
        place = lax.axis_index("tensor")
        last = bits_of("tensor") - 1
        for bit in range(1, last + 1):
            pairs = [
                term.reshape((term.shape[0] // 2, 2) + term.shape[1:]) for term in self.terms
            ]
            sent = picked_sum(order, self.where, bit, True, pairs)
            self.received = swap(sent, "tensor", bit)
            if bit < last:
                own = (place >> bit) & 1
                self.terms = [pick(pair, own, 1) for pair in pairs] + [self.received]
        self.pairs = pairs
        return self

    def cross(self, order):
        last = bits_of("tensor") - 1
        self.own = picked_sum(order, self.where, last, False, self.pairs, [self.received])[0]
        self.other = swap(self.own, "pipe", 0)
        return self


def add_rows_kernel(x_ref, own_ref, other_ref, norms_ref, out_ref):
    bias = norms_ref[4:5] + norms_ref[5:6]
    total = x_ref[...].astype(F32) + own_ref[...].astype(F32) + other_ref[...].astype(F32)
    out_ref[...] = (total + bias).astype(out_ref.dtype)


def add_rows(order, x_rows, summed, weights):
    return order.call(
        add_rows_kernel,
        "add_rows",
        12,
        [VMEM] * 4,
        [VMEM],
        [shape(x_rows.shape, BF)],
        [],
        [x_rows, summed.own, summed.other, weights["norms"]],
    )[0]


def norm_back_rows(x_ref, own_ref, other_ref, cot_ref):
    grad_hat = own_ref[...].astype(F32) + other_ref[...].astype(F32)
    hat, scale = normalize(x_ref[...])
    mean = jnp.mean(grad_hat, axis=-1, keepdims=True)
    along = jnp.mean(grad_hat * hat, axis=-1, keepdims=True)
    return cot_ref[...].astype(F32) + (grad_hat - mean - hat * along) * scale


def norm_back_kernel(x_ref, own_ref, other_ref, cot_ref, out_ref):
    out_ref[...] = norm_back_rows(x_ref, own_ref, other_ref, cot_ref).astype(BF)


def norm_back(order, x_rows, summed, cot_rows):
    return order.call(
        norm_back_kernel,
        "norm_back",
        16,
        [VMEM] * 4,
        [VMEM],
        [shape(x_rows.shape, BF)],
        [],
        [x_rows, summed.own, summed.other, cot_rows],
    )[0]


def ends_kernel(unit, stage_ref, x_ref, own_ref, other_ref, cot_ref, *refs):
    middle_ref, y_own_ref, y_other_ref, norms_ref = refs[:4]
    ends_ref, token_ref, held, sem = refs[-4:]
    token_ref[...] = jnp.zeros_like(token_ref)

    @pl.when(stage_ref[0] == 0)
    def _():
        held[...] = norm_back_rows(x_ref, own_ref, other_ref, cot_ref)

    @pl.when(stage_ref[0] != 0)
    def _():
        add_rows_kernel(middle_ref, y_own_ref, y_other_ref, norms_ref, held)

    copy = pltpu.make_async_copy(held, ends_ref.at[unit], sem)
    copy.start()
    copy.wait()


def write_ends(order, unit, stage, ends, x_rows, summed, cot_rows, middle_rows, y_sum, weights):
    args = [
        stage,
        x_rows,
        summed.own,
        summed.other,
        cot_rows,
        middle_rows,
        y_sum.own,
        y_sum.other,
        weights["norms"],
    ]
    more = {}
    if ends is not None:
        more = dict(input_output_aliases={len(args): 0})
        args.append(ends)
    return order.call(
        functools.partial(ends_kernel, unit),
        "ends",
        20,
        [SMEM] + [VMEM] * 8 + [ANY] * len(more),
        [ANY, VMEM],
        [shape((MB, *x_rows.shape), F32), shape((8, 128), F32)],
        [pltpu.VMEM(x_rows.shape, F32), pltpu.SemaphoreType.DMA],
        args,
        **more,
    )[0]


def angles_for(lengths_row, w):
    finish = jnp.cumsum(lengths_row)
    places = jnp.arange(TOK_MB, dtype=jnp.int32)
    after = (places[:, None] >= finish[None, :]).astype(jnp.int32)
    starts = jnp.sum(after * lengths_row[None, :], axis=1)
    position = (places - starts).astype(F32)
    inverse_freq = 10000.0 ** (-jnp.arange(ROT // 2, dtype=F32) * 2.0 / ROT)
    phase = position[:, None] * inverse_freq[None, :]
    cosine, sine = jnp.cos(phase), jnp.sin(phase)
    rest = jnp.zeros((TOK_MB, HD - 2 * ROT), F32)
    table = jnp.concatenate([cosine, cosine, -sine, sine, rest], axis=1)
    return starts[None], jnp.tile(table, (1, w // HD))


def body(
    boundary,
    lengths,
    gains,
    biases,
    qkv_weight,
    qkv_bias,
    out_weight,
    up_weight,
    up_bias,
    down_weight,
):
    stage = lax.axis_index("pipe")
    at_first = stage == 0
    dp = lax.axis_size("dp")
    tensor = lax.axis_size("tensor")
    index = lax.axis_index("tensor").astype(jnp.int32)[None]
    stage_word = stage.astype(jnp.int32)[None]
    order = Order()
    share = D // dp
    width = qkv_weight.shape[3] // 2
    ff = up_weight.shape[2] // 2
    heads = width // HD
    w = max(width, 128)
    cut = 3 * w + ff

    def split(mine, other):
        return jnp.where(at_first, mine, other), jnp.where(at_first, other, mine)

    def half(value, which, axis):
        size = value.shape[axis] // 2
        return lax.dynamic_slice_in_dim(value, which * size, size, axis)

    def padded(value, axis):
        if w == width:
            return value
        pads = [(0, 0)] * value.ndim
        pads[axis] = (0, w - width)
        return jnp.pad(value, pads)

    tiles = boundary[0, :, 0]
    angles = [angles_for(lengths[unit, 0], w) for unit in range(MB)]
    main_mine, main_sent, low_mine, low_sent = pack(
        order,
        stage_word,
        jnp.moveaxis(qkv_weight[0], 1, 0),
        up_weight[0],
        out_weight[0],
        down_weight[0],
        w,
    )
    main_other = swap(main_sent, "pipe", 0)
    low_other = swap(after(low_sent, main_other), "pipe", 0)
    tile_other = swap(after(tiles[0], low_other), "pipe", 0)
    order.pause()
    main_0, main_1 = by_stage(order, stage_word, main_mine, main_other)
    order.pause()
    low_0, both_1 = by_stage(order, stage_word, low_mine, low_other, [main_1])
    low_parts = line_parts(low_0, "dp")

    piece = gains.shape[2]
    small = jnp.concatenate([gains[0].reshape(-1), biases[0].reshape(-1)])
    small = gather_tensor(after(small, main_0)).reshape(-1)
    small = jnp.concatenate([small, qkv_bias[0].reshape(-1), up_bias[0]])
    small = jnp.stack(split(small, swap(small, "pipe", 0)))
    small = gather_direct(small, "dp")
    small = jnp.moveaxis(small, 0, 1).astype(F32)
    norms = small[:, :, : tensor * 6 * piece].reshape(2, dp, tensor, 6, piece)
    norms = norms.transpose(0, 3, 2, 1, 4).reshape(2, 6, D)
    rest = small[:, :, tensor * 6 * piece :]
    qkv_biases = rest[:, :, : 3 * piece].reshape(2, dp, 3, piece)
    qkv_biases = qkv_biases.transpose(0, 2, 1, 3).reshape(2, 3, 2 * width)
    qkv_biases = padded(half(qkv_biases, stage, 2), 2).reshape(2, 1, 3 * w)
    up_biases = half(rest[:, :, 3 * piece :].reshape(2, 1, 2 * ff), stage, 2)
    main_biases = jnp.concatenate([qkv_biases, up_biases], axis=2)

    layers = [
        dict(w=w, ff=ff, heads=heads, norms=norms[layer], bias=main_biases[layer])
        for layer in range(2)
    ]
    main_0 = lax.all_gather(main_0, "dp", axis=0)
    both_1 = lax.all_gather(after(both_1, main_0, *low_parts[1:]), "dp", axis=0)
    layers[0].update(main=(main_0, 0))
    layers[1].update(main=(both_1, 0), low=(both_1, cut))
    x_rows, cot_rows, x_blocks, c_blocks = [], [], [], []

    def take_tile(other):
        rows, cot = by_stage(order, stage_word, tiles[len(x_rows)], other)
        x_rows.append(rows)
        cot_rows.append(cot)
        x_blocks.append(gather_blocks(rows))

    order.hold(*[value for pair in angles for value in pair])
    order.pause()
    take_tile(tile_other)
    tile_other = swap(after(tiles[1], tile_other), "pipe", 0)
    order.hold(norms, main_biases)
    order.pause()
    take_tile(tile_other)
    order.pause()
    c_blocks.append(gather_blocks(after(cot_rows[0], x_blocks[1][tensor // 2])))

    units = range(MB)
    kept = [[None] * MB, [None] * MB]
    entered = [[None] * MB, [None] * MB]
    back = [[None] * MB, [None] * MB]

    def across(value, source):
        return lax.ppermute(value, "pipe", [(source, 1 - source)])

    class VectorSums:
        def __init__(self, cot_a, cot_b):
            own = [
                sum(jnp.sum(rows.astype(F32), axis=0) for rows in pair)
                for pair in ((cot_a, cot_b), cot_rows)
            ]
            once = jnp.where(at_first, 1.0, 0.0)
            packs = []
            for layer in range(2):
                rows = sum(back[layer][unit][1] for unit in units)[:4]
                raw = sum(back[layer][unit][2] for unit in units).reshape(3, w)[:, :width]
                pre = sum(entered[layer][unit][2] for unit in units)
                flat = [rows.reshape(-1), own[layer] * once, raw.reshape(-1), pre[0]]
                packs.append(jnp.concatenate(flat))
            self.mine = jnp.where(at_first, packs[0], packs[1])
            self.other = jnp.where(at_first, packs[1], packs[0])

        def across(self):
            self.received = swap(self.other, "pipe", 0)
            return self.received

        def along_tensor(self):
            rows = 5 * D
            norm = (self.mine[:rows] + self.received[:rows]).reshape(5, tensor, D // tensor)
            norm = norm.transpose(1, 0, 2)
            place = lax.axis_index("tensor")
            for bit in range(bits_of("tensor")):
                own = (place >> bit) & 1
                pairs = norm.reshape((norm.shape[0] // 2, 2) + norm.shape[1:])
                norm = pick(pairs, own, 1) + swap(pick(pairs, 1 - own, 1), "tensor", bit)
            norm = norm[0].reshape(5, dp, piece).transpose(1, 0, 2).reshape(dp, 5 * piece)
            low, high = split(self.mine[rows:], self.received[rows:])
            raw = jnp.stack([low[: 3 * width], high[: 3 * width]]).reshape(2, 3, width)
            raw = raw.transpose(1, 0, 2).reshape(3, dp, piece).transpose(1, 0, 2)
            pre = jnp.concatenate([low[3 * width :], high[3 * width :]]).reshape(dp, -1)
            self.parts = jnp.concatenate([norm, raw.reshape(dp, 3 * piece), pre], axis=1)
            return self.parts

        def along_dp(self):
            self.total = scatter_direct(self.parts, "dp")
            return self.total

        def results(self):
            norm = self.total[: 5 * piece].reshape(5, piece)
            raw = self.total[5 * piece : 8 * piece].reshape(3, piece)
            return norm, raw, self.total[8 * piece :]

    def run_project(layer, unit, blocks):
        kept[layer][unit] = project(order, index, blocks, layers[layer], angles[unit])

    def run_attend(layer, unit):
        keep, send, *rest = attend(
            order, index, tensor, kept[layer][unit], layers[layer], angles[unit]
        )
        kept[layer][unit] = [*kept[layer][unit], *rest]
        return Sum(index, keep, send)

    def run_backward(layer, unit, cots, blocks):
        keep, send, pre, pre_sum, *back[layer][unit] = whole_backward(
            order, index, cots, blocks, kept[layer][unit], layers[layer], angles[unit]
        )
        entered[layer][unit] = [None, pre, pre_sum]
        return Sum(index, keep, send)

    def run_layer(unit, blocks):
        y_keep, y_send, u_keep, u_send, hidden, context, pre, pre_sum, *rest = whole_layer(
            order, index, c_blocks[unit], blocks, layers[1], angles[unit]
        )
        kept[1][unit] = [None, None, None, hidden, None, context, None]
        entered[1][unit] = [None, pre, pre_sum]
        back[1][unit] = rest
        return Sum(index, y_keep, y_send), Sum(index, u_keep, u_send)

    def reduced(layer, names, cots, rows):
        lefts = dict(
            out=([kept[layer][unit][5] for unit in units], None),
            down=([kept[layer][unit][3] for unit in units], None),
            up=([entered[layer][unit][1] for unit in units], 1),
            qkv=([back[layer][unit] and back[layer][unit][0] for unit in units], 0),
        )
        pieces = [lefts[name] for name in names]
        value = weight_grads(order, index, cots, rows, pieces, layers[layer]["norms"], dp)
        return lax.psum_scatter(value, "dp", scatter_dimension=0)

    run_project(0, 0, x_blocks[0])
    dp_index = lax.axis_index("dp").astype(jnp.int32)[None]
    layers[0].update(low=(assemble(order, dp_index, low_parts), 0))
    sum_a = run_attend(0, 0)
    run_project(0, 1, x_blocks[1])
    order.hold(*c_blocks[0])
    sum_a.send(order)
    sum_b = run_attend(0, 1)
    sum_a.cross(order)
    sum_b.send(order)
    middle_a = add_rows(order, x_rows[0], sum_a, layers[0])
    blocks_a = gather_blocks(after(middle_a, sum_b.received))
    sum_b.cross(order)
    order.pause()
    middle_b = add_rows(order, x_rows[1], sum_b, layers[0])
    blocks_b = gather_blocks(after(middle_b, blocks_a[-1]))
    c_blocks.append(gather_blocks(after(cot_rows[1], blocks_b[tensor // 2])))
    middle_blocks = [blocks_a, blocks_b]

    y_a, sum_a = run_layer(0, blocks_a)
    order.pause()
    sum_a.send(order)
    run_project(1, 1, blocks_b)
    y_b = run_attend(1, 1)
    sum_a.cross(order)
    order.hold(*c_blocks[1])
    y_a.send(order)
    sum_b = run_backward(1, 1, c_blocks[1], blocks_b)
    cot_a = norm_back(order, middle_a, sum_a, cot_rows[0])
    sum_b.send(order)
    y_a.cross(order)
    grads_1 = reduced(1, ("out", "down", "up", "qkv"), c_blocks, middle_blocks)
    sum_b.cross(order)
    cot_blocks = [gather_blocks(after(cot_a, sum_b.own))]
    order.hold(y_a.other)
    order.pause()
    cot_b = norm_back(order, middle_b, sum_b, cot_rows[1])
    cot_blocks.append(gather_blocks(after(cot_b, cot_blocks[0][-1])))

    sum_a = run_backward(0, 0, cot_blocks[0], x_blocks[0])
    order.pause()
    entered[0][1] = enter(order, index, cot_blocks[1], kept[0][1], layers[0])
    sum_a.send(order)
    order.hold(grads_1)
    outer_0 = reduced(0, ("out", "down", "up"), cot_blocks, x_blocks)
    sum_a.cross(order)
    y_b.send(order)
    from_1 = across(grads_1, 0)
    keep, send, *back[0][1] = backward(
        order, index, x_blocks[1], kept[0][1], entered[0][1], layers[0], angles[1]
    )
    sum_b = Sum(index, keep, send)
    order.hold(from_1)
    y_b.cross(order)
    sum_b.send(order)
    vectors = VectorSums(cot_a, cot_b)
    order.pause()
    inner_0 = reduced(0, ("qkv",), cot_blocks, x_blocks)
    order.hold(vectors.across())
    ends = write_ends(
        order, 0, stage_word, None, x_rows[0], sum_a, cot_a, middle_a, y_a, layers[1]
    )
    order.hold(vectors.along_tensor())
    sum_b.cross(order)
    from_outer = across(outer_0, 1)
    order.hold(vectors.along_dp())
    order.pause()
    ends = write_ends(
        order, 1, stage_word, ends, x_rows[1], sum_b, cot_b, middle_b, y_b, layers[1]
    )

    inner_1, outer_1 = grads_1[w + 2 * ff :], grads_1[: w + 2 * ff]
    grad_up, grad_out, grad_down = unpack(
        functools.partial(unpack_outer_kernel, width, w, ff),
        order,
        stage_word,
        [outer_0, outer_1, from_outer, from_1[: w + 2 * ff]],
        [
            shape((share, 2 * ff), F32),
            shape((2 * width, share), F32),
            shape((2 * ff, share), F32),
        ],
    )
    grad_qkv = unpack(
        functools.partial(unpack_inner_kernel, width, w),
        order,
        stage_word,
        [inner_0, inner_1, across(inner_0, 1), from_1[w + 2 * ff :]],
        [shape((3, share, 2 * width), F32)],
    )[0]
    grad_qkv = jnp.moveaxis(grad_qkv, 0, 1)

    norm_grads, grad_qkv_bias, grad_up_bias = vectors.results()
    grad_gains = norm_grads[:2]
    grad_biases = jnp.concatenate([norm_grads[2:5], norm_grads[4:5]])
    return (
        ends[None, :, None],
        grad_gains[None],
        grad_biases[None],
        grad_qkv[None],
        grad_qkv_bias[None],
        grad_out[None],
        grad_up[None],
        grad_up_bias[None],
        grad_down[None],
    )


def solution(mesh):
    placed = (
        P("pipe", None, "dp", "tensor", None),
        P(None, "dp", None),
        P("pipe", None, ("tensor", "dp")),
        P("pipe", None, ("tensor", "dp")),
        P("pipe", "dp", None, "tensor"),
        P("pipe", None, ("tensor", "dp")),
        P("pipe", "tensor", "dp"),
        P("pipe", "dp", "tensor"),
        P("pipe", ("tensor", "dp")),
        P("pipe", "tensor", "dp"),
    )
    return jax.shard_map(
        body,
        mesh=mesh,
        in_specs=placed,
        out_specs=(placed[0],) + placed[2:],
        check_vma=False,
    )
```

```python
import functools

import jax
import jax.numpy as jnp
from jax import lax
from jax.experimental import pallas as pl
from jax.experimental.pallas import tpu as pltpu
from jax.sharding import PartitionSpec as P

D = 1024
H = 16
HD = 64
ROT = 16
MB = 2
TOK_MB = 1280
EPS = 1e-05
CHUNK = 256
FLOPS = 10**11
BF = jnp.bfloat16
F32 = jnp.float32
ANY = pl.BlockSpec(memory_space=pl.ANY)
VMEM = pl.BlockSpec(memory_space=pltpu.VMEM)
SMEM = pl.BlockSpec(memory_space=pltpu.SMEM)


def dot(left, right, left_dim, right_dim):
    return lax.dot_general(
        left, right, (((left_dim,), (right_dim,)), ((), ())), preferred_element_type=F32
    )


def shape(dims, dtype):
    return jax.ShapeDtypeStruct(dims, dtype)


def swap(value, axis, bit):
    count = lax.axis_size(axis)
    return lax.ppermute(value, axis, [(i, i ^ (1 << bit)) for i in range(count)])


def bits_of(axis):
    return lax.axis_size(axis).bit_length() - 1


def pick(value, index, axis):
    return lax.dynamic_index_in_dim(value, index, axis, keepdims=False)


def gather_blocks(value):
    blocks = {0: value}
    for bit in reversed(range(bits_of("tensor"))):
        found = [blocks[s] for s in blocks if s]
        for s in list(blocks):
            sent = after(blocks[s], *found) if found and s == 0 else blocks[s]
            blocks[s | (1 << bit)] = swap(sent, "tensor", bit)
    return [blocks[s] for s in range(len(blocks))]


def gather_tensor(value):
    index = lax.axis_index("tensor")
    value = value[None]
    for bit in reversed(range(bits_of("tensor"))):
        other = swap(value, "tensor", bit)
        mine = ((index >> bit) & 1) == 0
        low = jnp.where(mine, value, other)
        high = jnp.where(mine, other, value)
        value = jnp.stack([low, high], axis=1).reshape((-1,) + value.shape[1:])
    return value


def after(value, *others):
    return lax.optimization_barrier((value, *others))[0]


def gather_direct(value, axis):
    count = lax.axis_size(axis)
    index = lax.axis_index(axis)
    found = [value]
    for hop in range(1, count):
        found.append(lax.ppermute(value, axis, [(j, (j + hop) % count) for j in range(count)]))
    turned = jnp.stack(found[::-1] * 2)
    return lax.dynamic_slice_in_dim(turned, count - 1 - index, count, 0)


def scatter_direct(value, axis):
    count = lax.axis_size(axis)
    index = lax.axis_index(axis)
    total = pick(value, index, 0)
    for hop in range(1, count):
        sent = pick(value, (index + hop) % count, 0)
        total = total + lax.ppermute(sent, axis, [(j, (j + hop) % count) for j in range(count)])
    return total


def copies_of_blocks(index, blocks, target, sems):
    copies = []
    for s, block in enumerate(blocks):
        rows = block.shape[0]
        where = pl.multiple_of((index ^ s) * rows, rows)
        copies.append(pltpu.make_async_copy(block, target.at[pl.ds(where, rows)], sems.at[s]))
    return copies


def copies_to_halves(index, source, keep, send, sems, rows):
    copies = []
    own = index & 1
    for block in range(source.shape[0] // rows):
        part = source.at[pl.ds(block * rows, rows)]
        copies.append(
            (
                own == block & 1,
                pltpu.make_async_copy(part, keep.at[block >> 1], sems.at[block]),
                pltpu.make_async_copy(part, send.at[block >> 1], sems.at[block]),
            )
        )
    return copies


def start_half(copy):
    is_kept, to_keep, to_send = copy

    @pl.when(is_kept)
    def _():
        to_keep.start()

    @pl.when(jnp.logical_not(is_kept))
    def _():
        to_send.start()


def normalize(rows):
    rows = rows.astype(F32)
    centered = rows - jnp.mean(rows, axis=-1, keepdims=True)
    scale = lax.rsqrt(jnp.mean(centered * centered, axis=-1, keepdims=True) + EPS)
    return centered * scale, scale


def gelu_pair(values):
    share = 0.5 * (1.0 + lax.erf(values * 0.7071067811865476))
    density = jnp.exp(-0.5 * values * values) * 0.3989422804014327
    return values * share, share + values * density


def rotate(values, table_cos, table_sin, sign):
    width = values.shape[1]
    half = ROT // 2
    lanes = lax.broadcasted_iota(jnp.int32, values.shape, 1) % HD
    partner = jnp.where(
        lanes < half, pltpu.roll(values, width - half, 1), pltpu.roll(values, half, 1)
    )
    return values * table_cos + partner * (table_sin * sign)


def unpack_table(packed, sign):
    width = packed.shape[1]
    lanes = lax.broadcasted_iota(jnp.int32, packed.shape, 1) % HD
    table_cos = jnp.where(lanes < ROT, packed, 1.0)
    table_sin = jnp.where(lanes < ROT, pltpu.roll(packed, width - ROT, 1) * sign, 0.0)
    return table_cos, table_sin


def rotate(values, table_cos, table_sin):
    width = values.shape[1]
    half = ROT // 2
    lanes = lax.broadcasted_iota(jnp.int32, values.shape, 1) % HD
    partner = jnp.where(
        lanes < half, pltpu.roll(values, width - half, 1), pltpu.roll(values, half, 1)
    )
    return values * table_cos + partner * table_sin


def chunks():
    return [slice(begin, begin + CHUNK) for begin in range(0, TOK_MB, CHUNK)]


class Order:
    def __init__(self):
        self.last = []

    def hold(self, *values):
        self.last = [*self.last, *values]

    def call(self, kernel, name, vmem, in_specs, out_specs, out_shape, scratch, args, **more):
        count = len(args)
        deps = self.last

        def outer(*refs):
            kernel(*refs[:count], *refs[count + len(deps) :])

        results = pl.pallas_call(
            outer,
            in_specs=in_specs + [ANY] * len(deps),
            out_specs=out_specs,
            out_shape=out_shape,
            scratch_shapes=scratch,
            compiler_params=pltpu.CompilerParams(vmem_limit_bytes=vmem << 20),
            cost_estimate=pl.CostEstimate(
                flops=FLOPS, bytes_accessed=1024, transcendentals=0
            ),
            name=name,
            **more,
        )(*args, *deps)
        self.last = [min(results, key=lambda result: result.size)]
        return results

    def pause(self):
        def nothing(out_ref):
            out_ref[...] = jnp.zeros_like(out_ref)

        self.call(nothing, "pause", 2, [], [VMEM], [shape((8, 128), F32)], [], [])


def loads_of_weights(source, row, target, sems, first=0):
    dp, _, share = source.shape
    rows = target.shape[0]
    return [
        pltpu.make_async_copy(
            source.at[j, pl.ds(row, rows)],
            target.at[:, pl.ds(j * share, share)],
            sems.at[first + j],
        )
        for j in range(dp)
    ]


def start_all(copies):
    for copy in copies:
        copy.start()


def wait_all(copies):
    for copy in copies:
        copy.wait()


class Leaving:
    def __init__(self, index, source, keep, send, sems):
        self.rows = keep.shape[1]
        self.copies = copies_to_halves(index, source, keep, send, sems, self.rows)
        self.done = 0

    def reached(self, end):
        while self.done < len(self.copies) and (self.done + 1) * self.rows <= end:
            start_half(self.copies[self.done])
            self.done += 1

    def wait(self):
        for copy in self.copies:
            copy[1].wait()


def masked(scores, starts, begin):
    key = lax.broadcasted_iota(jnp.int32, scores.shape, 0)
    query = lax.broadcasted_iota(jnp.int32, scores.shape, 1) + begin
    return jnp.where((key <= query) & (key >= starts), scores, -1e30)


def head_only(values, head):
    lanes = lax.broadcasted_iota(jnp.int32, values.shape, 1)
    inside = (lanes >= head * HD) & (lanes < (head + 1) * HD)
    return jnp.where(inside, values, jnp.zeros_like(values))


def turned_back(parts, w):
    rest = w - len(parts) * HD
    if rest:
        parts = parts + [jnp.zeros((rest, parts[0].shape[1]), F32)]
    return jnp.concatenate(parts, axis=0).T


def do_project(w, x_all, main, norms_ref, bias_ref, table_ref, q_ref, k_ref, v_ref, hidden_ref, slope_ref):
    for at in chunks():
        hat, _ = normalize(x_all[at])
        first = (hat * norms_ref[0:1] + norms_ref[2:3]).astype(BF)
        second = (hat * norms_ref[1:2] + norms_ref[3:4]).astype(BF)
        raw = dot(first, main[: 3 * w], 1, 1) + bias_ref[:, : 3 * w]
        table_cos, table_sin = unpack_table(table_ref[at], 1.0)
        q_ref[at] = rotate(raw[:, :w], table_cos, table_sin).astype(BF)
        k_ref[at] = rotate(raw[:, w : 2 * w], table_cos, table_sin).astype(BF)
        v_ref[at] = raw[:, 2 * w :].astype(BF)
        hidden, slope = gelu_pair(dot(second, main[3 * w :], 1, 1) + bias_ref[:, 3 * w :])
        hidden_ref[at] = hidden.astype(BF)
        slope_ref[at] = slope.astype(BF)


def do_attend(heads, w, starts_ref, q_ref, k_ref, v_ref, hidden_ref, low, loads, context_ref, logs_ref, v_turned, partial, leaving):
    v_turned[...] = v_ref[...].T
    logs_ref[...] = jnp.zeros_like(logs_ref)
    for at in chunks():
        starts = starts_ref[:, at]
        queries = q_ref[at] * BF(HD**-0.5)
        turned = []
        for head in range(heads):
            s = dot(k_ref[: at.stop], head_only(queries, head), 1, 1)
            s = masked(s, starts, at.start)
            top = jnp.max(s, axis=0, keepdims=True)
            e = jnp.exp(s - top)
            total = jnp.sum(e, axis=0, keepdims=True)
            part = v_turned[head * HD : (head + 1) * HD, : at.stop]
            turned.append(dot(part, e.astype(BF), 1, 0) / total)
            logs_ref[head : head + 1, at] = top + jnp.log(total)
        context = turned_back(turned, w).astype(BF)
        context_ref[at] = context
        if at.start == 0:
            wait_all(loads)
        total = dot(context, low[:w], 1, 0) + dot(hidden_ref[at], low[w:], 1, 0)
        partial[at] = total.astype(BF)
        leaving.reached(at.stop)


def do_enter(w, c_all, low, slope_ref, grad_context, pre_ref, sum_ref):
    total = jnp.zeros(sum_ref.shape, F32)
    for at in chunks():
        both = dot(c_all[at], low[...], 1, 1)
        grad_context[at] = both[:, :w].astype(BF)
        grad_pre = (both[:, w:] * slope_ref[at].astype(F32)).astype(BF)
        pre_ref[at] = grad_pre
        total = total + jnp.sum(grad_pre.astype(F32), axis=0, keepdims=True)
    sum_ref[...] = total


def do_backward(
    heads,
    w,
    starts_ref,
    q_ref,
    k_ref,
    v_ref,
    context_ref,
    logs_ref,
    grad_context,
    pre_ref,
    x_loads,
    x_all,
    main,
    norms_ref,
    table_ref,
    raw_ref,
    vectors_ref,
    sum_ref,
    k_turned,
    grad_q,
    grad_k,
    grad_v,
    partial,
    leaving,
):
    k_turned[...] = (k_ref[...] * BF(HD**-0.5)).T
    grad_k[...] = jnp.zeros_like(grad_k)
    grad_v[...] = jnp.zeros_like(grad_v)
    for at in chunks():
        starts = starts_ref[:, at]
        queries = q_ref[at] * BF(HD**-0.5)
        grads = grad_context[at]
        products = (grads.astype(F32) * context_ref[at].astype(F32)).T
        to_k = to_v = 0.0
        turned = []
        for head in range(heads):
            lanes = slice(head * HD, (head + 1) * HD)
            q, g = head_only(queries, head), head_only(grads, head)
            weighted = jnp.sum(products[lanes], axis=0, keepdims=True)
            s = masked(dot(k_ref[: at.stop], q, 1, 1), starts, at.start)
            p = jnp.exp(s - logs_ref[head : head + 1, at])
            grad_p = dot(v_ref[: at.stop], g, 1, 1)
            grad_s = (p * (grad_p - weighted)).astype(BF)
            to_k = to_k + dot(grad_s, q, 1, 0)
            to_v = to_v + dot(p.astype(BF), g, 1, 0)
            turned.append(dot(k_turned[lanes, : at.stop], grad_s, 1, 0))
        grad_k[: at.stop] += to_k
        grad_v[: at.stop] += to_v
        grad_q[at] = turned_back(turned, w)
    wait_all(x_loads)
    sums = [jnp.zeros((1, D), F32) for _ in range(4)]
    raw_sum = jnp.zeros(sum_ref.shape, F32)
    for at in chunks():
        table_cos, table_sin = unpack_table(table_ref[at], -1.0)
        grad_raw = jnp.concatenate(
            [
                rotate(grad_q[at], table_cos, table_sin),
                rotate(grad_k[at], table_cos, table_sin),
                grad_v[at],
            ],
            axis=1,
        ).astype(BF)
        raw_ref[at] = grad_raw
        raw_sum = raw_sum + jnp.sum(grad_raw.astype(F32), axis=0, keepdims=True)
        grad_first = dot(grad_raw, main[: 3 * w], 1, 0)
        grad_second = dot(pre_ref[at], main[3 * w :], 1, 0)
        hat, _ = normalize(x_all[at])
        for i, term in enumerate(
            (grad_first * hat, grad_second * hat, grad_first, grad_second)
        ):
            sums[i] = sums[i] + jnp.sum(term, axis=0, keepdims=True)
        partial[at] = (grad_first * norms_ref[0:1] + grad_second * norms_ref[1:2]).astype(BF)
        leaving.reached(at.stop)
    vectors_ref[...] = jnp.concatenate(sums + [jnp.zeros((4, D), F32)], axis=0)
    sum_ref[...] = raw_sum


def rows_of(*widths):
    return [shape((TOK_MB, width), BF) for width in widths]


def halves_of(blocks):
    return [shape((blocks // 2, TOK_MB // blocks, D), BF)] * 2


def held(*widths):
    return [pltpu.VMEM((TOK_MB, width), BF) for width in widths]


def dma(*counts):
    return [pltpu.SemaphoreType.DMA((count,)) for count in counts]


def project_kernel(blocks, w, row, *refs):
    index_ref = refs[0]
    x_refs = refs[1 : 1 + blocks]
    main_ref, norms_ref, bias_ref, table_ref = refs[1 + blocks : 5 + blocks]
    outs = refs[5 + blocks : 10 + blocks]
    x_all, main, x_sems, main_sems = refs[10 + blocks :]
    loads = copies_of_blocks(index_ref[0], x_refs, x_all, x_sems)
    loads += loads_of_weights(main_ref, row, main, main_sems)
    start_all(loads)
    wait_all(loads)
    do_project(w, x_all, main, norms_ref, bias_ref, table_ref, *outs)


def project(order, index, x_blocks, weights, angles):
    blocks = len(x_blocks)
    w, ff = weights["w"], weights["ff"]
    main, row = weights["main"]
    return order.call(
        functools.partial(project_kernel, blocks, w, row),
        "project",
        24,
        [SMEM] + [ANY] * (blocks + 1) + [VMEM] * 3,
        [VMEM] * 5,
        rows_of(w, w, w, ff, ff),
        held(D) + [pltpu.VMEM((3 * w + ff, D), BF)] + dma(blocks, main.shape[0]),
        [index, *x_blocks, main, weights["norms"], weights["bias"], angles[1]],
    )


def attend_kernel(heads, w, row, *refs):
    index_ref, starts_ref, q_ref, k_ref, v_ref, hidden_ref, low_ref = refs[:7]
    keep_ref, send_ref, context_ref, logs_ref = refs[7:11]
    low, partial, v_turned, low_sems, out_sems = refs[11:]
    loads = loads_of_weights(low_ref, row, low, low_sems)
    start_all(loads)
    leaving = Leaving(index_ref[0], partial, keep_ref, send_ref, out_sems)
    do_attend(
        heads,
        w,
        starts_ref,
        q_ref,
        k_ref,
        v_ref,
        hidden_ref,
        low,
        loads,
        context_ref,
        logs_ref,
        v_turned,
        partial,
        leaving,
    )
    leaving.wait()


def attend(order, index, blocks, kept, weights, angles):
    w, heads, ff = weights["w"], weights["heads"], weights["ff"]
    low, row = weights["low"]
    return order.call(
        functools.partial(attend_kernel, heads, w, row),
        "attend",
        28,
        [SMEM] + [VMEM] * 5 + [ANY],
        [ANY, ANY, VMEM, VMEM],
        halves_of(blocks) + rows_of(w) + [shape((8, TOK_MB), F32)],
        [pltpu.VMEM((w + ff, D), BF)]
        + held(D)
        + [pltpu.VMEM((w, TOK_MB), BF)]
        + dma(low.shape[0], blocks),
        [index, angles[0], *kept[:4], low],
    )


def enter_kernel(blocks, w, row, *refs):
    index_ref = refs[0]
    c_refs = refs[1 : 1 + blocks]
    low_ref, slope_ref = refs[1 + blocks : 3 + blocks]
    context_ref, pre_ref, sum_ref = refs[3 + blocks : 6 + blocks]
    c_all, low, c_sems, low_sems = refs[6 + blocks :]
    loads = loads_of_weights(low_ref, row, low, low_sems)
    loads += copies_of_blocks(index_ref[0], c_refs, c_all, c_sems)
    start_all(loads)
    wait_all(loads)
    do_enter(w, c_all, low, slope_ref, context_ref, pre_ref, sum_ref)


def enter(order, index, c_blocks, kept, weights):
    w, ff = weights["w"], weights["ff"]
    low, row = weights["low"]
    blocks = len(c_blocks)
    return order.call(
        functools.partial(enter_kernel, blocks, w, row),
        "enter",
        60,
        [SMEM] + [ANY] * (blocks + 1) + [VMEM],
        [VMEM] * 3,
        rows_of(w, ff) + [shape((1, ff), F32)],
        held(D) + [pltpu.VMEM((w + ff, D), BF)] + dma(blocks, low.shape[0]),
        [index, *c_blocks, low, kept[4]],
    )


def scratch_of_backward(w):
    return [pltpu.VMEM((w, TOK_MB), BF)] + [pltpu.VMEM((TOK_MB, w), F32)] * 3


def backward_kernel(blocks, heads, w, row, *refs):
    index_ref = refs[0]
    x_refs = refs[1 : 1 + blocks]
    inner = refs[1 + blocks : 9 + blocks]
    main_ref, norms_ref, table_ref = refs[9 + blocks : 12 + blocks]
    keep_ref, send_ref, *outs = refs[12 + blocks : 17 + blocks]
    x_all, main, partial, *scratch, x_sems, main_sems, out_sems = refs[17 + blocks :]
    loads = copies_of_blocks(index_ref[0], x_refs, x_all, x_sems)
    loads += loads_of_weights(main_ref, row, main, main_sems)
    start_all(loads)
    leaving = Leaving(index_ref[0], partial, keep_ref, send_ref, out_sems)
    do_backward(
        heads, w, *inner, loads, x_all, main, norms_ref, table_ref, *outs, *scratch, partial, leaving
    )
    leaving.wait()


def backward(order, index, x_blocks, kept, entered, weights, angles):
    queries, keys, values, _, _, context, logs = kept
    blocks = len(x_blocks)
    w, heads, ff = weights["w"], weights["heads"], weights["ff"]
    main, row = weights["main"]
    return order.call(
        functools.partial(backward_kernel, blocks, heads, w, row),
        "backward",
        60,
        [SMEM] + [ANY] * blocks + [VMEM] * 8 + [ANY] + [VMEM] * 2,
        [ANY, ANY] + [VMEM] * 3,
        halves_of(blocks) + rows_of(3 * w) + [shape((8, D), F32), shape((1, 3 * w), F32)],
        held(D)
        + [pltpu.VMEM((3 * w + ff, D), BF)]
        + held(D)
        + scratch_of_backward(w)
        + dma(blocks, main.shape[0], blocks),
        [
            index,
            *x_blocks,
            angles[0],
            queries,
            keys,
            values,
            context,
            logs,
            entered[0],
            entered[1],
            main,
            weights["norms"],
            angles[1],
        ],
    )


def whole_backward_kernel(blocks, heads, w, main_row, low_row, *refs):
    index_ref = refs[0]
    c_refs = refs[1 : 1 + blocks]
    x_refs = refs[1 + blocks : 1 + 2 * blocks]
    starts_ref, q_ref, k_ref, v_ref, context_ref, logs_ref, slope_ref = refs[
        1 + 2 * blocks : 8 + 2 * blocks
    ]
    main_ref, low_ref, norms_ref, table_ref = refs[8 + 2 * blocks : 12 + 2 * blocks]
    keep_ref, send_ref, pre_ref, pre_sum_ref, *outs = refs[12 + 2 * blocks : 19 + 2 * blocks]
    c_all, x_all, main, low, partial, grad_context, *scratch = refs[19 + 2 * blocks : 29 + 2 * blocks]
    c_sems, x_sems, main_sems, low_sems, out_sems = refs[29 + 2 * blocks :]
    loads = loads_of_weights(low_ref, low_row, low, low_sems)
    loads += copies_of_blocks(index_ref[0], c_refs, c_all, c_sems)
    later = copies_of_blocks(index_ref[0], x_refs, x_all, x_sems)
    later += loads_of_weights(main_ref, main_row, main, main_sems)
    start_all(loads + later)
    leaving = Leaving(index_ref[0], partial, keep_ref, send_ref, out_sems)
    wait_all(loads)
    do_enter(w, c_all, low, slope_ref, grad_context, pre_ref, pre_sum_ref)
    do_backward(
        heads,
        w,
        starts_ref,
        q_ref,
        k_ref,
        v_ref,
        context_ref,
        logs_ref,
        grad_context,
        pre_ref,
        later,
        x_all,
        main,
        norms_ref,
        table_ref,
        *outs,
        *scratch,
        partial,
        leaving,
    )
    leaving.wait()


def whole_backward(order, index, c_blocks, x_blocks, kept, weights, angles):
    queries, keys, values, _, slope, context, logs = kept
    blocks = len(x_blocks)
    w, heads, ff = weights["w"], weights["heads"], weights["ff"]
    main, main_row = weights["main"]
    low, low_row = weights["low"]
    dp = main.shape[0]
    return order.call(
        functools.partial(whole_backward_kernel, blocks, heads, w, main_row, low_row),
        "whole_backward",
        60,
        [SMEM] + [ANY] * (2 * blocks) + [VMEM] * 7 + [ANY] * 2 + [VMEM] * 2,
        [ANY, ANY] + [VMEM] * 5,
        halves_of(blocks)
        + rows_of(ff)
        + [shape((1, ff), F32)]
        + rows_of(3 * w)
        + [shape((8, D), F32), shape((1, 3 * w), F32)],
        held(D, D)
        + [pltpu.VMEM((3 * w + ff, D), BF), pltpu.VMEM((w + ff, D), BF)]
        + held(D, w)
        + scratch_of_backward(w)
        + dma(blocks, blocks, dp, dp, blocks),
        [
            index,
            *c_blocks,
            *x_blocks,
            angles[0],
            queries,
            keys,
            values,
            context,
            logs,
            slope,
            main,
            low,
            weights["norms"],
            angles[1],
        ],
    )


def layer_kernel(blocks, heads, w, main_row, low_row, *refs):
    index_ref = refs[0]
    c_refs = refs[1 : 1 + blocks]
    x_refs = refs[1 + blocks : 1 + 2 * blocks]
    starts_ref, main_ref, low_ref, norms_ref, bias_ref, table_ref = refs[
        1 + 2 * blocks : 7 + 2 * blocks
    ]
    (y_keep, y_send, u_keep, u_send, hidden_ref, context_ref, pre_ref, pre_sum_ref, *outs) = refs[
        7 + 2 * blocks : 18 + 2 * blocks
    ]
    (c_all, x_all, main, low, y_all, u_all, q_ref, k_ref, v_ref, slope_ref, grad_context) = refs[
        18 + 2 * blocks : 29 + 2 * blocks
    ]
    logs_ref, v_turned, *scratch = refs[29 + 2 * blocks : 35 + 2 * blocks]
    c_sems, x_sems, main_sems, low_sems, y_sems, u_sems = refs[35 + 2 * blocks :]
    index = index_ref[0]
    loads = copies_of_blocks(index, x_refs, x_all, x_sems)
    loads += loads_of_weights(main_ref, main_row, main, main_sems)
    low_loads = loads_of_weights(low_ref, low_row, low, low_sems)
    c_loads = copies_of_blocks(index, c_refs, c_all, c_sems)
    start_all(loads + low_loads + c_loads)
    y_leaving = Leaving(index, y_all, y_keep, y_send, y_sems)
    u_leaving = Leaving(index, u_all, u_keep, u_send, u_sems)
    wait_all(loads)
    do_project(
        w, x_all, main, norms_ref, bias_ref, table_ref, q_ref, k_ref, v_ref, hidden_ref, slope_ref
    )
    do_attend(
        heads,
        w,
        starts_ref,
        q_ref,
        k_ref,
        v_ref,
        hidden_ref,
        low,
        low_loads,
        context_ref,
        logs_ref,
        v_turned,
        y_all,
        y_leaving,
    )
    wait_all(c_loads)
    do_enter(w, c_all, low, slope_ref, grad_context, pre_ref, pre_sum_ref)
    do_backward(
        heads,
        w,
        starts_ref,
        q_ref,
        k_ref,
        v_ref,
        context_ref,
        logs_ref,
        grad_context,
        pre_ref,
        [],
        x_all,
        main,
        norms_ref,
        table_ref,
        *outs,
        *scratch,
        u_all,
        u_leaving,
    )
    y_leaving.wait()
    u_leaving.wait()


def whole_layer(order, index, c_blocks, x_blocks, weights, angles):
    blocks = len(x_blocks)
    w, heads, ff = weights["w"], weights["heads"], weights["ff"]
    main, main_row = weights["main"]
    low, low_row = weights["low"]
    dp = main.shape[0]
    return order.call(
        functools.partial(layer_kernel, blocks, heads, w, main_row, low_row),
        "whole_layer",
        60,
        [SMEM] + [ANY] * (2 * blocks) + [VMEM] + [ANY] * 2 + [VMEM] * 3,
        [ANY] * 4 + [VMEM] * 7,
        halves_of(blocks)
        + halves_of(blocks)
        + rows_of(ff, w, ff)
        + [shape((1, ff), F32)]
        + rows_of(3 * w)
        + [shape((8, D), F32), shape((1, 3 * w), F32)],
        held(D, D)
        + [pltpu.VMEM((3 * w + ff, D), BF), pltpu.VMEM((w + ff, D), BF)]
        + held(D, D, w, w, w, ff, w)
        + [pltpu.VMEM((8, TOK_MB), F32), pltpu.VMEM((w, TOK_MB), BF)]
        + scratch_of_backward(w)
        + dma(blocks, blocks, dp, dp, blocks, blocks),
        [
            index,
            *c_blocks,
            *x_blocks,
            angles[0],
            main,
            low,
            weights["norms"],
            weights["bias"],
            angles[1],
        ],
    )


def grads_kernel(blocks, plan, extra, *refs):
    index_ref, norms_ref = refs[:2]
    with_cot = None in plan
    normed = sorted({which for which in plan if which is not None})
    count = MB * blocks
    row_refs = refs[2 : 2 + count]
    lefts = refs[2 + count : 2 + count + MB * len(plan)]
    rest = refs[2 + count + MB * len(plan) :]
    extra_ref, rest = (rest[0], rest[1:]) if extra else (None, rest)
    out_ref, total, *scratch = rest
    side_sems, sems = scratch.pop(), scratch.pop()
    sides, scratch = scratch[: MB * len(plan)], scratch[MB * len(plan) :]
    index = index_ref[0]
    dp, _, share = out_ref.shape
    loads = []
    for unit in range(MB):
        part = row_refs[unit * blocks : (unit + 1) * blocks]
        loads.append(copies_of_blocks(index, part, scratch[0].at[unit], sems.at[unit]))
        for i in range(len(plan)):
            left = lefts[i * MB + unit]
            loads[unit].append(
                pltpu.make_async_copy(left, sides[i * MB + unit], side_sems.at[i * MB + unit])
            )
        start_all(loads[unit])
    for unit in range(MB):
        wait_all(loads[unit])
        rights = {None: scratch[0]}
        if not with_cot:
            rights = dict(zip(normed, scratch))
            for at in chunks():
                hat, _ = normalize(scratch[0][unit, at])
                for norm in normed:
                    row = hat * norms_ref[norm : norm + 1] + norms_ref[2 + norm : 3 + norm]
                    rights[norm][unit, at] = row.astype(BF)
        begin = 0
        for i, which in enumerate(plan):
            left = sides[i * MB + unit]
            rows = slice(begin, begin + left.shape[1])
            part = dot(left[...], rights[which][unit], 0, 0)
            if unit:
                part = part + total[rows]
            if unit + 1 < MB:
                total[rows] = part
            else:
                for j in range(dp):
                    out_ref[j, rows] = part[:, j * share : (j + 1) * share].astype(BF)
            begin = rows.stop
    if extra:
        out_ref[:, begin:] = extra_ref[...]


def weight_grads(order, index, c_blocks, x_blocks, pieces, norms, dp, extra=()):
    plan = [which for _, which in pieces]
    blocks = len(x_blocks[0])
    rows = [block for unit in (c_blocks if None in plan else x_blocks) for block in unit]
    lefts = [left for part, _ in pieces for left in part]
    size = sum(part[0].shape[1] for part, _ in pieces) + sum(value.shape[1] for value in extra)
    buffers = len(set(plan))
    return order.call(
        functools.partial(grads_kernel, blocks, plan, bool(extra)),
        "weight_grads",
        60,
        [SMEM, VMEM] + [ANY] * (len(rows) + len(lefts)) + [VMEM] * len(extra),
        [VMEM],
        [shape((dp, size, D // dp), BF)],
        [pltpu.VMEM((size, D), F32)]
        + [pltpu.VMEM(left.shape, BF) for left in lefts]
        + [pltpu.VMEM((MB, TOK_MB, D), BF)] * buffers
        + [pltpu.SemaphoreType.DMA((MB, blocks)), pltpu.SemaphoreType.DMA((len(lefts),))],
        [index, norms, *rows, *lefts, *extra],
    )[0]


SMALL = 16


def put_halves(at_first, keep, send, begin, size, low, high):
    keep[begin : begin + size] = jnp.where(at_first, low, high)
    send[begin : begin + size] = jnp.where(at_first, high, low)


def pack_kernel(width, w, stage_ref, qkv_ref, up_ref, out_ref, down_ref, keep_ref, send_ref, *held):
    (qkv, up, out, down), sems = held[:4], held[4]
    sources = (qkv_ref, up_ref, out_ref, down_ref)
    loads = [
        pltpu.make_async_copy(source, target, sems.at[i])
        for i, (source, target) in enumerate(zip(sources, held))
    ]
    start_all(loads)
    at_first = stage_ref[0] == 0
    ff = up.shape[1] // 2
    if w != width:
        keep_ref[...] = jnp.zeros_like(keep_ref)
        send_ref[...] = jnp.zeros_like(send_ref)
    wait_all(loads)
    for i in range(3):
        turned = qkv[i].T
        put_halves(at_first, keep_ref, send_ref, i * w, width, turned[:width], turned[width:])
    turned = up[...].T
    put_halves(at_first, keep_ref, send_ref, 3 * w, ff, turned[:ff], turned[ff:])
    begin = 3 * w + ff
    put_halves(at_first, keep_ref, send_ref, begin, width, out[:width], out[width:])
    put_halves(at_first, keep_ref, send_ref, begin + w, ff, down[:ff], down[ff:])


def pack(order, stage, qkv, up, out, down, w):
    width, ff, share = qkv.shape[2] // 2, up.shape[1] // 2, up.shape[0]
    return order.call(
        functools.partial(pack_kernel, width, w),
        "pack",
        60,
        [SMEM] + [ANY] * 4,
        [VMEM] * 2,
        [shape((4 * w + 2 * ff, share), BF)] * 2,
        [pltpu.VMEM(value.shape, BF) for value in (qkv, up, out, down)] + dma(4),
        [stage, qkv, up, out, down],
    )


def by_stage_kernel(stage_ref, *refs):
    at_first = stage_ref[0] == 0
    pairs, (first_ref, second_ref) = refs[:-2], refs[-2:]
    begin = 0
    for mine_ref, other_ref in zip(pairs[::2], pairs[1::2]):
        rows = slice(begin, begin + mine_ref.shape[0])
        mine, other = mine_ref[...], other_ref[...]
        first_ref[rows] = jnp.where(at_first, mine, other)
        second_ref[rows] = jnp.where(at_first, other, mine)
        begin = rows.stop


def by_stage(order, stage, *pairs):
    rows = sum(mine.shape[0] for mine in pairs[::2])
    return order.call(
        by_stage_kernel,
        "by_stage",
        16,
        [SMEM] + [VMEM] * len(pairs),
        [VMEM] * 2,
        [shape((rows, pairs[0].shape[1]), BF)] * 2,
        [],
        [stage, *pairs],
    )


def both_halves(stage_ref, mine0, mine1, from0, from1, begin, size):
    at_first = stage_ref[0] == 0
    rows = slice(begin, begin + size)
    low = jnp.where(at_first, mine0[rows], from1[rows])
    high = jnp.where(at_first, from0[rows], mine1[rows])
    return low.astype(F32), high.astype(F32)


def unpack_outer_kernel(width, w, ff, *refs):
    parts, (out_ref, down_ref) = refs[:5], refs[5:]
    out_ref[:width], out_ref[width:] = both_halves(*parts, 0, width)
    down_ref[:ff], down_ref[ff:] = both_halves(*parts, w, ff)


def unpack_inner_kernel(width, w, ff, *refs):
    parts, (up_ref, qkv_ref) = refs[:5], refs[5:]
    low, high = both_halves(*parts, 0, ff)
    up_ref[:, :ff] = low.T
    up_ref[:, ff:] = high.T
    for i in range(3):
        low, high = both_halves(*parts, ff + i * w, width)
        qkv_ref[i] = jnp.concatenate([low, high], axis=0).T


def unpack(kernel, order, stage, parts, out_shape):
    return order.call(
        kernel,
        "unpack",
        24,
        [SMEM] + [VMEM] * 4,
        [VMEM] * len(out_shape),
        out_shape,
        [],
        [stage, *parts],
    )


def picked_kernel(bit, flip, pairs, plains, *refs):
    index_ref = refs[0]
    out_ref, held, sems = refs[1 + pairs + plains :]
    want = (index_ref[0] >> bit) & 1
    if flip:
        want = 1 - want
    copies = []
    for i in range(pairs + plains):
        for j in range(out_ref.shape[0]):
            source = refs[1 + i].at[j, want] if i < pairs else refs[1 + i].at[j]
            copies.append(pltpu.make_async_copy(source, held.at[i, j], sems.at[i, j]))
    for copy in copies:
        copy.start()
    for copy in copies:
        copy.wait()
    total = held[0].astype(F32)
    for i in range(1, pairs + plains):
        total = total + held[i].astype(F32)
    out_ref[...] = total.astype(BF)


def picked_sum(order, where, bit, flip, pairs, plains=()):
    dims = (pairs[0].shape[0],) + pairs[0].shape[2:]
    terms = [*pairs, *plains]
    return order.call(
        functools.partial(picked_kernel, bit, flip, len(pairs), len(plains)),
        "picked_sum",
        20,
        [SMEM] + [ANY] * len(terms),
        [VMEM],
        [shape(dims, BF)],
        [
            pltpu.VMEM((len(terms), *dims), BF),
            pltpu.SemaphoreType.DMA((len(terms), dims[0])),
        ],
        [where, *terms],
    )[0]


class Sum:
    def __init__(self, where, keep, send):
        self.where = where
        self.terms = [keep, swap(send, "tensor", 0)]

    def send(self, order, *others):
        place = lax.axis_index("tensor")
        last = bits_of("tensor") - 1
        for bit in range(1, last + 1):
            pairs = [
                term.reshape((term.shape[0] // 2, 2) + term.shape[1:]) for term in self.terms
            ]
            sent = picked_sum(order, self.where, bit, True, pairs)
            self.sent = sent
            self.received = swap(after(sent, *others) if others else sent, "tensor", bit)
            if bit < last:
                own = (place >> bit) & 1
                self.terms = [pick(pair, own, 1) for pair in pairs] + [self.received]
        self.pairs = pairs
        return self

    def cross(self, order):
        last = bits_of("tensor") - 1
        self.own = picked_sum(order, self.where, last, False, self.pairs, [self.received])[0]
        self.other = swap(self.own, "pipe", 0)
        return self


def add_rows_kernel(x_ref, own_ref, other_ref, norms_ref, out_ref):
    bias = norms_ref[4:5] + norms_ref[5:6]
    total = x_ref[...].astype(F32) + own_ref[...].astype(F32) + other_ref[...].astype(F32)
    out_ref[...] = (total + bias).astype(out_ref.dtype)


def add_rows(order, x_rows, summed, weights):
    return order.call(
        add_rows_kernel,
        "add_rows",
        12,
        [VMEM] * 4,
        [VMEM],
        [shape(x_rows.shape, BF)],
        [],
        [x_rows, summed.own, summed.other, weights["norms"]],
    )[0]


def norm_back_rows(x_ref, own_ref, other_ref, cot_ref):
    grad_hat = own_ref[...].astype(F32) + other_ref[...].astype(F32)
    hat, scale = normalize(x_ref[...])
    mean = jnp.mean(grad_hat, axis=-1, keepdims=True)
    along = jnp.mean(grad_hat * hat, axis=-1, keepdims=True)
    return cot_ref[...].astype(F32) + (grad_hat - mean - hat * along) * scale


def norm_back_kernel(x_ref, own_ref, other_ref, cot_ref, out_ref):
    out_ref[...] = norm_back_rows(x_ref, own_ref, other_ref, cot_ref).astype(BF)


def norm_back(order, x_rows, summed, cot_rows):
    return order.call(
        norm_back_kernel,
        "norm_back",
        16,
        [VMEM] * 4,
        [VMEM],
        [shape(x_rows.shape, BF)],
        [],
        [x_rows, summed.own, summed.other, cot_rows],
    )[0]


def ends_kernel(unit, stage_ref, x_ref, own_ref, other_ref, cot_ref, *refs):
    middle_ref, y_own_ref, y_other_ref, norms_ref = refs[:4]
    ends_ref, token_ref, held, sem = refs[-4:]
    token_ref[...] = jnp.zeros_like(token_ref)

    @pl.when(stage_ref[0] == 0)
    def _():
        held[...] = norm_back_rows(x_ref, own_ref, other_ref, cot_ref)

    @pl.when(stage_ref[0] != 0)
    def _():
        add_rows_kernel(middle_ref, y_own_ref, y_other_ref, norms_ref, held)

    copy = pltpu.make_async_copy(held, ends_ref.at[unit], sem)
    copy.start()
    copy.wait()


def write_ends(order, unit, stage, ends, x_rows, summed, cot_rows, middle_rows, y_sum, weights):
    args = [
        stage,
        x_rows,
        summed.own,
        summed.other,
        cot_rows,
        middle_rows,
        y_sum.own,
        y_sum.other,
        weights["norms"],
    ]
    more = {}
    if ends is not None:
        more = dict(input_output_aliases={len(args): 0})
        args.append(ends)
    return order.call(
        functools.partial(ends_kernel, unit),
        "ends",
        20,
        [SMEM] + [VMEM] * 8 + [ANY] * len(more),
        [ANY, VMEM],
        [shape((MB, *x_rows.shape), F32), shape((8, 128), F32)],
        [pltpu.VMEM(x_rows.shape, F32), pltpu.SemaphoreType.DMA],
        args,
        **more,
    )[0]


def angles_for(lengths_row, w):
    finish = jnp.cumsum(lengths_row)
    places = jnp.arange(TOK_MB, dtype=jnp.int32)
    after = (places[:, None] >= finish[None, :]).astype(jnp.int32)
    starts = jnp.sum(after * lengths_row[None, :], axis=1)
    position = (places - starts).astype(F32)
    inverse_freq = 10000.0 ** (-jnp.arange(ROT // 2, dtype=F32) * 2.0 / ROT)
    phase = position[:, None] * inverse_freq[None, :]
    cosine, sine = jnp.cos(phase), jnp.sin(phase)
    rest = jnp.zeros((TOK_MB, HD - 2 * ROT), F32)
    table = jnp.concatenate([cosine, cosine, -sine, sine, rest], axis=1)
    return starts[None], jnp.tile(table, (1, w // HD))


def body(
    boundary,
    lengths,
    gains,
    biases,
    qkv_weight,
    qkv_bias,
    out_weight,
    up_weight,
    up_bias,
    down_weight,
):
    stage = lax.axis_index("pipe")
    at_first = stage == 0
    dp = lax.axis_size("dp")
    tensor = lax.axis_size("tensor")
    index = lax.axis_index("tensor").astype(jnp.int32)[None]
    stage_word = stage.astype(jnp.int32)[None]
    order = Order()
    share = D // dp
    width = qkv_weight.shape[3] // 2
    ff = up_weight.shape[2] // 2
    heads = width // HD
    w = max(width, 128)
    cut = 3 * w + ff

    def split(mine, other):
        return jnp.where(at_first, mine, other), jnp.where(at_first, other, mine)

    def half(value, which, axis):
        size = value.shape[axis] // 2
        return lax.dynamic_slice_in_dim(value, which * size, size, axis)

    def padded(value, axis):
        if w == width:
            return value
        pads = [(0, 0)] * value.ndim
        pads[axis] = (0, w - width)
        return jnp.pad(value, pads)

    tiles = boundary[0, :, 0]
    angles = [angles_for(lengths[unit, 0], w) for unit in range(MB)]
    far = tensor // 2

    def gather_far(value):
        blocks = {0: value}
        for bit in reversed(range(1, bits_of("tensor"))):
            for s in list(blocks):
                blocks[s | (1 << bit)] = swap(blocks[s], "tensor", bit)
        return [blocks[s] for s in sorted(blocks)]

    piece = gains.shape[2]
    small = jnp.concatenate([gains[0], biases[0]])
    small = jnp.moveaxis(gather_tensor(small), 0, 1).reshape(6, share)
    flat = jnp.concatenate([qkv_bias[0].reshape(-1), up_bias[0]])
    flat = jnp.pad(flat, (0, (SMALL - 6) * share - flat.shape[0])).reshape(-1, share)
    small = jnp.concatenate([small, flat])

    mine, sent = pack(
        order,
        stage_word,
        jnp.moveaxis(qkv_weight[0], 1, 0),
        up_weight[0],
        out_weight[0],
        down_weight[0],
        w,
    )
    other = swap(sent, "pipe", 0)
    order.hold(small)
    order.pause()
    small_other = swap(small, "pipe", 0)
    def gather_near(order, blocks):
        found = [None] * tensor
        for i, rows in enumerate(blocks):
            found[2 * i] = rows
            found[2 * i + 1] = swap(after(rows, order.last[0]), "tensor", 0)
        return found

    order.pause()
    stack_0, stack_1 = by_stage(order, stage_word, mine, other, small, small_other)
    far_tiles = [gather_far(after(tile, order.last[0])) for tile in tiles]
    stack_0 = lax.all_gather(stack_0, "dp", axis=0)

    def vectors_of(gathered, row):
        small = gathered[:, row : row + SMALL].astype(F32)
        norms = small[:, :6].reshape(dp, 6, tensor, piece).transpose(1, 2, 0, 3).reshape(6, D)
        flat = small[:, 6:].reshape(dp, -1)
        raw = flat[:, : 3 * piece].reshape(dp, 3, piece).transpose(1, 0, 2)
        raw = padded(half(raw.reshape(3, 2 * width), stage, 1), 1).reshape(1, 3 * w)
        up = flat[:, 3 * piece : 3 * piece + up_bias.shape[1]].reshape(1, 2 * ff)
        return dict(norms=norms, bias=jnp.concatenate([raw, half(up, stage, 1)], axis=1))

    x_rows, cot_rows, x_blocks, c_blocks = [], [], [], []

    def take_tiles(unit):
        others = [swap(tile, "pipe", 0) for tile in far_tiles[unit]]
        order.pause()
        x_far, cot_far = [], []
        for mine, other in zip(far_tiles[unit], others):
            rows, cot = by_stage(order, stage_word, mine, other)
            x_far.append(rows)
            cot_far.append(cot)
        x_rows.append(x_far[0])
        cot_rows.append(cot_far[0])
        order.pause()
        x_blocks.append(gather_near(order, x_far))
        order.pause()
        order.hold(*x_blocks[unit])
        order.pause()
        c_blocks.append(gather_near(order, cot_far))
        order.pause()
        order.hold(*c_blocks[unit])

    order.hold(*[value for pair in angles for value in pair])
    order.pause()
    take_tiles(0)
    stack_1 = lax.all_gather(after(stack_1, x_rows[0]), "dp", axis=0)
    take_tiles(1)
    order.pause()
    row = 4 * w + 2 * ff
    layers = [
        dict(w=w, ff=ff, heads=heads, main=(stack, 0), low=(stack, cut))
        for stack in (stack_0, stack_1)
    ]
    layers[0].update(vectors_of(stack_0, row))

    units = range(MB)
    kept = [[None] * MB, [None] * MB]
    entered = [[None] * MB, [None] * MB]
    back = [[None] * MB, [None] * MB]

    def vector_rows(layer, cots):
        own = sum(jnp.sum(rows.astype(F32), axis=0) for rows in cots)
        own = own * jnp.where(at_first, 1.0, 0.0)
        rows = sum(back[layer][unit][1] for unit in units)[:4]
        rows = jnp.concatenate([rows, own[None]]).reshape(5, tensor, dp, piece)
        rows = rows.transpose(2, 0, 1, 3).reshape(dp, 5, share)
        raw = sum(back[layer][unit][2] for unit in units).reshape(3, w)[:, :width]
        raw = raw.reshape(3, dp // 2, piece).transpose(1, 0, 2).reshape(dp // 2, 3 * piece)
        pre = sum(entered[layer][unit][2] for unit in units).reshape(dp // 2, -1)
        pads = [jnp.pad(item, ((0, 0), (0, share - item.shape[1]))) for item in (raw, pre)]
        held = lax.dynamic_update_slice(
            jnp.zeros((dp, 2, share), F32), jnp.stack(pads, axis=1), (stage * (dp // 2), 0, 0)
        )
        return [jnp.pad(jnp.concatenate([rows, held], axis=1), ((0, 0), (0, SMALL - 7), (0, 0))).astype(BF)]

    def vectors_from(rows_0, rows_1):
        both = jnp.stack([rows_0, rows_1]).astype(F32)
        norm = both[:, :5].reshape(2, 5, tensor, piece).transpose(2, 0, 1, 3)
        place = lax.axis_index("tensor")
        total = pick(norm, place, 0)
        for s in range(1, tensor):
            pairs = [(i, i ^ s) for i in range(tensor)]
            total = total + lax.ppermute(pick(norm, place ^ s, 0), "tensor", pairs)
        flat = jnp.concatenate([total.reshape(2, -1), both[:, 5:7].reshape(2, -1)], axis=1)
        mine = jnp.where(at_first, flat[0], flat[1])
        total = mine + swap(jnp.where(at_first, flat[1], flat[0]), "pipe", 0)
        norm = total[: 5 * piece].reshape(5, piece)
        raw = total[5 * piece : 5 * piece + 3 * piece].reshape(3, piece)
        begin = 5 * piece + share
        return norm, raw, total[begin : begin + up_bias.shape[1]]

    def run_project(layer, unit, blocks):
        kept[layer][unit] = project(order, index, blocks, layers[layer], angles[unit])

    def run_attend(layer, unit):
        keep, send, *rest = attend(
            order, index, tensor, kept[layer][unit], layers[layer], angles[unit]
        )
        kept[layer][unit] = [*kept[layer][unit], *rest]
        return Sum(index, keep, send)

    def run_backward(layer, unit, cots, blocks):
        keep, send, pre, pre_sum, *back[layer][unit] = whole_backward(
            order, index, cots, blocks, kept[layer][unit], layers[layer], angles[unit]
        )
        entered[layer][unit] = [None, pre, pre_sum]
        return Sum(index, keep, send)

    def run_layer(unit, blocks):
        y_keep, y_send, u_keep, u_send, hidden, context, pre, pre_sum, *rest = whole_layer(
            order, index, c_blocks[unit], blocks, layers[1], angles[unit]
        )
        kept[1][unit] = [None, None, None, hidden, None, context, None]
        entered[1][unit] = [None, pre, pre_sum]
        back[1][unit] = rest
        return Sum(index, y_keep, y_send), Sum(index, u_keep, u_send)

    def reduced(layer, names, cots, rows, extra=()):
        sources = dict(
            out=(kept, 5, None), down=(kept, 3, None), up=(entered, 1, 1), qkv=(back, 0, 0)
        )
        pieces = []
        for name in names:
            held_in, place, which = sources[name]
            pieces.append(([held_in[layer][unit][place] for unit in units], which))
        norms = layers[layer]["norms"]
        value = weight_grads(order, index, cots, rows, pieces, norms, dp, extra)
        return lax.psum_scatter(value, "dp", scatter_dimension=0)

    run_project(0, 0, x_blocks[0])
    sum_a = run_attend(0, 0)
    order.pause()
    sum_a.send(order)
    run_project(0, 1, x_blocks[1])
    sum_b = run_attend(0, 1)
    sum_a.cross(order)
    sum_b.send(order)
    middle_a = add_rows(order, x_rows[0], sum_a, layers[0])
    far_a = gather_far(middle_a)
    sum_b.cross(order)
    order.pause()
    blocks_a = gather_near(order, far_a)
    order.hold(stack_1)
    middle_b = add_rows(order, x_rows[1], sum_b, layers[0])
    far_b = gather_far(middle_b)
    layers[1].update(vectors_of(after(stack_1, middle_b), row))

    y_a, sum_a = run_layer(0, blocks_a)
    order.pause()
    blocks_b = gather_near(order, far_b)
    middle_blocks = [blocks_a, blocks_b]
    order.hold(y_a.terms[1])
    sum_a.send(order)
    run_project(1, 1, blocks_b)
    y_b = run_attend(1, 1)
    sum_a.cross(order)
    order.hold(y_b.terms[1])
    y_a.send(order)
    y_b.send(order)
    sum_b = run_backward(1, 1, c_blocks[1], blocks_b)
    cot_a = norm_back(order, middle_a, sum_a, cot_rows[0])
    sum_b.send(order)
    y_a.cross(order)
    outer_1 = reduced(1, ("out", "down"), c_blocks, middle_blocks)
    sum_b.cross(order)
    far_a = gather_far(after(cot_a, order.last[0]))
    inner_1 = reduced(1, ("up", "qkv"), c_blocks, middle_blocks, vector_rows(1, cot_rows))
    cot_blocks = [gather_near(order, far_a)]
    y_b.cross(order)
    cot_b = norm_back(order, middle_b, sum_b, cot_rows[1])
    far_b = gather_far(cot_b)

    order.hold(outer_1, y_a.other)
    order.pause()
    from_outer_1 = swap(outer_1, "pipe", 0)
    sum_a = run_backward(0, 0, cot_blocks[0], x_blocks[0])
    cot_blocks.append(gather_near(order, far_b))
    order.pause()
    outer_0 = reduced(0, ("out", "down"), cot_blocks, x_blocks)
    sum_a.send(order)
    order.hold(from_outer_1, inner_1, y_b.other)
    entered[0][1] = enter(order, index, cot_blocks[1], kept[0][1], layers[0])
    from_inner_1 = swap(inner_1, "pipe", 0)
    keep, send, *back[0][1] = backward(
        order, index, x_blocks[1], kept[0][1], entered[0][1], layers[0], angles[1]
    )
    sum_b = Sum(index, keep, send)
    order.hold(from_inner_1)
    inner_0 = reduced(0, ("up", "qkv"), cot_blocks, x_blocks, vector_rows(0, (cot_a, cot_b)))
    from_outer_0 = swap(after(outer_0, order.last[0]), "pipe", 0)
    order.pause()
    sum_b.send(order)
    sum_a.cross(order)
    order.pause()
    sum_b.cross(order)
    ends = write_ends(
        order, 0, stage_word, None, x_rows[0], sum_a, cot_a, middle_a, y_a, layers[1]
    )
    order.hold(from_outer_0)
    grad_out, grad_down = unpack(
        functools.partial(unpack_outer_kernel, width, w, ff),
        order,
        stage_word,
        [outer_0, outer_1, from_outer_0, from_outer_1],
        [shape((2 * width, share), F32), shape((2 * ff, share), F32)],
    )
    order.hold(inner_0)
    ends = write_ends(
        order, 1, stage_word, ends, x_rows[1], sum_b, cot_b, middle_b, y_b, layers[1]
    )
    last = 3 * w + ff
    from_inner_0 = swap(inner_0, "pipe", 0)
    vectors = vectors_from(inner_0[last:], inner_1[last:])
    order.hold(from_inner_0)
    grad_up, grad_qkv = unpack(
        functools.partial(unpack_inner_kernel, width, w, ff),
        order,
        stage_word,
        [inner_0, inner_1, from_inner_0, from_inner_1],
        [shape((share, 2 * ff), F32), shape((3, share, 2 * width), F32)],
    )
    grad_qkv = jnp.moveaxis(grad_qkv, 0, 1)
    norm_grads, grad_qkv_bias, grad_up_bias = vectors
    grad_gains = norm_grads[:2]
    grad_biases = jnp.concatenate([norm_grads[2:5], norm_grads[4:5]])
    return (
        ends[None, :, None],
        grad_gains[None],
        grad_biases[None],
        grad_qkv[None],
        grad_qkv_bias[None],
        grad_out[None],
        grad_up[None],
        grad_up_bias[None],
        grad_down[None],
    )


def solution(mesh):
    placed = (
        P("pipe", None, "dp", "tensor", None),
        P(None, "dp", None),
        P("pipe", None, ("tensor", "dp")),
        P("pipe", None, ("tensor", "dp")),
        P("pipe", "dp", None, "tensor"),
        P("pipe", None, ("tensor", "dp")),
        P("pipe", "tensor", "dp"),
        P("pipe", "dp", "tensor"),
        P("pipe", ("tensor", "dp")),
        P("pipe", "tensor", "dp"),
    )
    return jax.shard_map(
        body,
        mesh=mesh,
        in_specs=placed,
        out_specs=(placed[0],) + placed[2:],
        check_vma=False,
    )
```

```python
import functools

import jax
import jax.numpy as jnp
from jax import lax
from jax.experimental import pallas as pl
from jax.experimental.pallas import tpu as pltpu
from jax.sharding import PartitionSpec as P

D = 1024
H = 16
HD = 64
ROT = 16
MB = 2
TOK_MB = 1280
EPS = 1e-05
CHUNK = 256
FLOPS = 10**11
BF = jnp.bfloat16
F32 = jnp.float32
ANY = pl.BlockSpec(memory_space=pl.ANY)
VMEM = pl.BlockSpec(memory_space=pltpu.VMEM)
SMEM = pl.BlockSpec(memory_space=pltpu.SMEM)


def dot(left, right, left_dim, right_dim):
    return lax.dot_general(
        left, right, (((left_dim,), (right_dim,)), ((), ())), preferred_element_type=F32
    )


def shape(dims, dtype):
    return jax.ShapeDtypeStruct(dims, dtype)


def swap(value, axis, bit):
    count = lax.axis_size(axis)
    return lax.ppermute(value, axis, [(i, i ^ (1 << bit)) for i in range(count)])


def bits_of(axis):
    return lax.axis_size(axis).bit_length() - 1


def pick(value, index, axis):
    return lax.dynamic_index_in_dim(value, index, axis, keepdims=False)


def gather_blocks(value):
    blocks = {0: value}
    for bit in reversed(range(bits_of("tensor"))):
        found = [blocks[s] for s in blocks if s]
        for s in list(blocks):
            sent = after(blocks[s], *found) if found and s == 0 else blocks[s]
            blocks[s | (1 << bit)] = swap(sent, "tensor", bit)
    return [blocks[s] for s in range(len(blocks))]


def gather_tensor(value):
    index = lax.axis_index("tensor")
    value = value[None]
    for bit in reversed(range(bits_of("tensor"))):
        other = swap(value, "tensor", bit)
        mine = ((index >> bit) & 1) == 0
        low = jnp.where(mine, value, other)
        high = jnp.where(mine, other, value)
        value = jnp.stack([low, high], axis=1).reshape((-1,) + value.shape[1:])
    return value


def after(value, *others):
    return lax.optimization_barrier((value, *others))[0]


def gather_direct(value, axis):
    count = lax.axis_size(axis)
    index = lax.axis_index(axis)
    found = [value]
    for hop in range(1, count):
        found.append(lax.ppermute(value, axis, [(j, (j + hop) % count) for j in range(count)]))
    turned = jnp.stack(found[::-1] * 2)
    return lax.dynamic_slice_in_dim(turned, count - 1 - index, count, 0)


def scatter_direct(value, axis):
    count = lax.axis_size(axis)
    index = lax.axis_index(axis)
    total = pick(value, index, 0)
    for hop in range(1, count):
        sent = pick(value, (index + hop) % count, 0)
        total = total + lax.ppermute(sent, axis, [(j, (j + hop) % count) for j in range(count)])
    return total


def copies_of_blocks(index, blocks, target, sems):
    copies = []
    for s, block in enumerate(blocks):
        rows = block.shape[0]
        where = pl.multiple_of((index ^ s) * rows, rows)
        copies.append(pltpu.make_async_copy(block, target.at[pl.ds(where, rows)], sems.at[s]))
    return copies


def copies_to_halves(index, source, keep, send, sems, rows):
    copies = []
    own = index & 1
    for block in range(source.shape[0] // rows):
        part = source.at[pl.ds(block * rows, rows)]
        copies.append(
            (
                own == block & 1,
                pltpu.make_async_copy(part, keep.at[block >> 1], sems.at[block]),
                pltpu.make_async_copy(part, send.at[block >> 1], sems.at[block]),
            )
        )
    return copies


def start_half(copy):
    is_kept, to_keep, to_send = copy

    @pl.when(is_kept)
    def _():
        to_keep.start()

    @pl.when(jnp.logical_not(is_kept))
    def _():
        to_send.start()


def normalize(rows):
    rows = rows.astype(F32)
    centered = rows - jnp.mean(rows, axis=-1, keepdims=True)
    scale = lax.rsqrt(jnp.mean(centered * centered, axis=-1, keepdims=True) + EPS)
    return centered * scale, scale


def gelu_pair(values):
    share = 0.5 * (1.0 + lax.erf(values * 0.7071067811865476))
    density = jnp.exp(-0.5 * values * values) * 0.3989422804014327
    return values * share, share + values * density


def rotate(values, table_cos, table_sin, sign):
    width = values.shape[1]
    half = ROT // 2
    lanes = lax.broadcasted_iota(jnp.int32, values.shape, 1) % HD
    partner = jnp.where(
        lanes < half, pltpu.roll(values, width - half, 1), pltpu.roll(values, half, 1)
    )
    return values * table_cos + partner * (table_sin * sign)


def unpack_table(packed, sign):
    width = packed.shape[1]
    lanes = lax.broadcasted_iota(jnp.int32, packed.shape, 1) % HD
    table_cos = jnp.where(lanes < ROT, packed, 1.0)
    table_sin = jnp.where(lanes < ROT, pltpu.roll(packed, width - ROT, 1) * sign, 0.0)
    return table_cos, table_sin


def rotate(values, table_cos, table_sin):
    width = values.shape[1]
    half = ROT // 2
    lanes = lax.broadcasted_iota(jnp.int32, values.shape, 1) % HD
    partner = jnp.where(
        lanes < half, pltpu.roll(values, width - half, 1), pltpu.roll(values, half, 1)
    )
    return values * table_cos + partner * table_sin


def chunks():
    return [slice(begin, begin + CHUNK) for begin in range(0, TOK_MB, CHUNK)]


class Order:
    def __init__(self):
        self.last = []

    def hold(self, *values):
        self.last = [*self.last, *values]

    def call(self, kernel, name, vmem, in_specs, out_specs, out_shape, scratch, args, **more):
        count = len(args)
        deps = self.last

        def outer(*refs):
            kernel(*refs[:count], *refs[count + len(deps) :])

        results = pl.pallas_call(
            outer,
            in_specs=in_specs + [ANY] * len(deps),
            out_specs=out_specs,
            out_shape=out_shape,
            scratch_shapes=scratch,
            compiler_params=pltpu.CompilerParams(vmem_limit_bytes=vmem << 20),
            cost_estimate=pl.CostEstimate(
                flops=FLOPS, bytes_accessed=1024, transcendentals=0
            ),
            name=name,
            **more,
        )(*args, *deps)
        self.last = [min(results, key=lambda result: result.size)]
        return results

    def pause(self):
        def nothing(out_ref):
            out_ref[...] = jnp.zeros_like(out_ref)

        self.call(nothing, "pause", 2, [], [VMEM], [shape((8, 128), F32)], [], [])


def loads_of_weights(source, row, target, sems, first=0):
    dp, _, share = source.shape
    rows = target.shape[0]
    return [
        pltpu.make_async_copy(
            source.at[j, pl.ds(row, rows)],
            target.at[:, pl.ds(j * share, share)],
            sems.at[first + j],
        )
        for j in range(dp)
    ]


def start_all(copies):
    for copy in copies:
        copy.start()


def wait_all(copies):
    for copy in copies:
        copy.wait()


class Leaving:
    def __init__(self, index, source, keep, send, sems):
        self.rows = keep.shape[1]
        self.copies = copies_to_halves(index, source, keep, send, sems, self.rows)
        self.done = 0

    def reached(self, end):
        while self.done < len(self.copies) and (self.done + 1) * self.rows <= end:
            start_half(self.copies[self.done])
            self.done += 1

    def wait(self):
        for copy in self.copies:
            copy[1].wait()


def masked(scores, starts, begin):
    key = lax.broadcasted_iota(jnp.int32, scores.shape, 0)
    query = lax.broadcasted_iota(jnp.int32, scores.shape, 1) + begin
    return jnp.where((key <= query) & (key >= starts), scores, -1e30)


def head_only(values, head):
    lanes = lax.broadcasted_iota(jnp.int32, values.shape, 1)
    inside = (lanes >= head * HD) & (lanes < (head + 1) * HD)
    return jnp.where(inside, values, jnp.zeros_like(values))


def turned_back(parts, w):
    rest = w - len(parts) * HD
    if rest:
        parts = parts + [jnp.zeros((rest, parts[0].shape[1]), F32)]
    return jnp.concatenate(parts, axis=0).T


def do_project(w, x_all, main, norms_ref, bias_ref, table_ref, q_ref, k_ref, v_ref, hidden_ref, slope_ref):
    for at in chunks():
        hat, _ = normalize(x_all[at])
        first = (hat * norms_ref[0:1] + norms_ref[2:3]).astype(BF)
        second = (hat * norms_ref[1:2] + norms_ref[3:4]).astype(BF)
        raw = dot(first, main[: 3 * w], 1, 1) + bias_ref[:, : 3 * w]
        table_cos, table_sin = unpack_table(table_ref[at], 1.0)
        q_ref[at] = rotate(raw[:, :w], table_cos, table_sin).astype(BF)
        k_ref[at] = rotate(raw[:, w : 2 * w], table_cos, table_sin).astype(BF)
        v_ref[at] = raw[:, 2 * w :].astype(BF)
        hidden, slope = gelu_pair(dot(second, main[3 * w :], 1, 1) + bias_ref[:, 3 * w :])
        hidden_ref[at] = hidden.astype(BF)
        slope_ref[at] = slope.astype(BF)


def do_attend(heads, w, starts_ref, q_ref, k_ref, v_ref, hidden_ref, low, loads, context_ref, logs_ref, v_turned, partial, leaving):
    v_turned[...] = v_ref[...].T
    logs_ref[...] = jnp.zeros_like(logs_ref)
    for at in chunks():
        starts = starts_ref[:, at]
        queries = q_ref[at] * BF(HD**-0.5)
        turned = []
        for head in range(heads):
            s = dot(k_ref[: at.stop], head_only(queries, head), 1, 1)
            s = masked(s, starts, at.start)
            top = jnp.max(s, axis=0, keepdims=True)
            e = jnp.exp(s - top)
            total = jnp.sum(e, axis=0, keepdims=True)
            part = v_turned[head * HD : (head + 1) * HD, : at.stop]
            turned.append(dot(part, e.astype(BF), 1, 0) / total)
            logs_ref[head : head + 1, at] = top + jnp.log(total)
        context = turned_back(turned, w).astype(BF)
        context_ref[at] = context
        if at.start == 0:
            wait_all(loads)
        total = dot(context, low[:w], 1, 0) + dot(hidden_ref[at], low[w:], 1, 0)
        partial[at] = total.astype(BF)
        leaving.reached(at.stop)


def do_enter(w, products, slope_ref, grad_context, pre_ref, sum_ref):
    total = jnp.zeros(sum_ref.shape, F32)
    for at in chunks():
        both = products(at)
        grad_context[at] = both[:, :w].astype(BF)
        grad_pre = (both[:, w:] * slope_ref[at].astype(F32)).astype(BF)
        pre_ref[at] = grad_pre
        total = total + jnp.sum(grad_pre.astype(F32), axis=0, keepdims=True)
    sum_ref[...] = total


def cotangent_kernel(blocks, row, *refs):
    index_ref = refs[0]
    c_refs = refs[1 : 1 + blocks]
    low_ref, out_ref, c_all, low, c_sems, low_sems = refs[1 + blocks :]
    loads = loads_of_weights(low_ref, row, low, low_sems)
    loads += copies_of_blocks(index_ref[0], c_refs, c_all, c_sems)
    start_all(loads)
    wait_all(loads)
    for at in chunks():
        out_ref[at] = dot(c_all[at], low[...], 1, 1)


def cotangent(order, index, c_blocks, weights):
    w, ff = weights["w"], weights["ff"]
    low, row = weights["low"]
    blocks = len(c_blocks)
    return order.call(
        functools.partial(cotangent_kernel, blocks, row),
        "cotangent",
        24,
        [SMEM] + [ANY] * (blocks + 1),
        [VMEM],
        [shape((TOK_MB, w + ff), F32)],
        held(D) + [pltpu.VMEM((w + ff, D), BF)] + dma(blocks, low.shape[0]),
        [index, *c_blocks, low],
    )[0]


def do_backward(
    heads,
    w,
    starts_ref,
    q_ref,
    k_ref,
    v_ref,
    context_ref,
    logs_ref,
    grad_context,
    pre_ref,
    x_loads,
    x_all,
    main,
    norms_ref,
    table_ref,
    raw_ref,
    vectors_ref,
    sum_ref,
    k_turned,
    grad_q,
    grad_k,
    grad_v,
    partial,
    leaving,
):
    k_turned[...] = (k_ref[...] * BF(HD**-0.5)).T
    grad_k[...] = jnp.zeros_like(grad_k)
    grad_v[...] = jnp.zeros_like(grad_v)
    for at in chunks():
        starts = starts_ref[:, at]
        queries = q_ref[at] * BF(HD**-0.5)
        grads = grad_context[at]
        products = (grads.astype(F32) * context_ref[at].astype(F32)).T
        to_k = to_v = 0.0
        turned = []
        for head in range(heads):
            lanes = slice(head * HD, (head + 1) * HD)
            q, g = head_only(queries, head), head_only(grads, head)
            weighted = jnp.sum(products[lanes], axis=0, keepdims=True)
            s = masked(dot(k_ref[: at.stop], q, 1, 1), starts, at.start)
            p = jnp.exp(s - logs_ref[head : head + 1, at])
            grad_p = dot(v_ref[: at.stop], g, 1, 1)
            grad_s = (p * (grad_p - weighted)).astype(BF)
            to_k = to_k + dot(grad_s, q, 1, 0)
            to_v = to_v + dot(p.astype(BF), g, 1, 0)
            turned.append(dot(k_turned[lanes, : at.stop], grad_s, 1, 0))
        grad_k[: at.stop] += to_k
        grad_v[: at.stop] += to_v
        grad_q[at] = turned_back(turned, w)
    wait_all(x_loads)
    sums = [jnp.zeros((1, D), F32) for _ in range(4)]
    raw_sum = jnp.zeros(sum_ref.shape, F32)
    for at in chunks():
        table_cos, table_sin = unpack_table(table_ref[at], -1.0)
        grad_raw = jnp.concatenate(
            [
                rotate(grad_q[at], table_cos, table_sin),
                rotate(grad_k[at], table_cos, table_sin),
                grad_v[at],
            ],
            axis=1,
        ).astype(BF)
        raw_ref[at] = grad_raw
        raw_sum = raw_sum + jnp.sum(grad_raw.astype(F32), axis=0, keepdims=True)
        grad_first = dot(grad_raw, main[: 3 * w], 1, 0)
        grad_second = dot(pre_ref[at], main[3 * w :], 1, 0)
        hat, _ = normalize(x_all[at])
        for i, term in enumerate(
            (grad_first * hat, grad_second * hat, grad_first, grad_second)
        ):
            sums[i] = sums[i] + jnp.sum(term, axis=0, keepdims=True)
        partial[at] = (grad_first * norms_ref[0:1] + grad_second * norms_ref[1:2]).astype(BF)
        leaving.reached(at.stop)
    vectors_ref[...] = jnp.concatenate(sums + [jnp.zeros((4, D), F32)], axis=0)
    sum_ref[...] = raw_sum


def rows_of(*widths):
    return [shape((TOK_MB, width), BF) for width in widths]


def halves_of(blocks):
    return [shape((blocks // 2, TOK_MB // blocks, D), BF)] * 2


def held(*widths):
    return [pltpu.VMEM((TOK_MB, width), BF) for width in widths]


def dma(*counts):
    return [pltpu.SemaphoreType.DMA((count,)) for count in counts]


def project_kernel(blocks, w, row, *refs):
    index_ref = refs[0]
    x_refs = refs[1 : 1 + blocks]
    main_ref, norms_ref, bias_ref, table_ref = refs[1 + blocks : 5 + blocks]
    outs = refs[5 + blocks : 10 + blocks]
    x_all, main, x_sems, main_sems = refs[10 + blocks :]
    loads = copies_of_blocks(index_ref[0], x_refs, x_all, x_sems)
    loads += loads_of_weights(main_ref, row, main, main_sems)
    start_all(loads)
    wait_all(loads)
    do_project(w, x_all, main, norms_ref, bias_ref, table_ref, *outs)


def project(order, index, x_blocks, weights, angles):
    blocks = len(x_blocks)
    w, ff = weights["w"], weights["ff"]
    main, row = weights["main"]
    return order.call(
        functools.partial(project_kernel, blocks, w, row),
        "project",
        24,
        [SMEM] + [ANY] * (blocks + 1) + [VMEM] * 3,
        [VMEM] * 5,
        rows_of(w, w, w, ff, ff),
        held(D) + [pltpu.VMEM((3 * w + ff, D), BF)] + dma(blocks, main.shape[0]),
        [index, *x_blocks, main, weights["norms"], weights["bias"], angles[1]],
    )


def attend_kernel(heads, w, row, *refs):
    index_ref, starts_ref, q_ref, k_ref, v_ref, hidden_ref, low_ref = refs[:7]
    keep_ref, send_ref, context_ref, logs_ref = refs[7:11]
    low, partial, v_turned, low_sems, out_sems = refs[11:]
    loads = loads_of_weights(low_ref, row, low, low_sems)
    start_all(loads)
    leaving = Leaving(index_ref[0], partial, keep_ref, send_ref, out_sems)
    do_attend(
        heads,
        w,
        starts_ref,
        q_ref,
        k_ref,
        v_ref,
        hidden_ref,
        low,
        loads,
        context_ref,
        logs_ref,
        v_turned,
        partial,
        leaving,
    )
    leaving.wait()


def attend(order, index, blocks, kept, weights, angles):
    w, heads, ff = weights["w"], weights["heads"], weights["ff"]
    low, row = weights["low"]
    return order.call(
        functools.partial(attend_kernel, heads, w, row),
        "attend",
        28,
        [SMEM] + [VMEM] * 5 + [ANY],
        [ANY, ANY, VMEM, VMEM],
        halves_of(blocks) + rows_of(w) + [shape((8, TOK_MB), F32)],
        [pltpu.VMEM((w + ff, D), BF)]
        + held(D)
        + [pltpu.VMEM((w, TOK_MB), BF)]
        + dma(low.shape[0], blocks),
        [index, angles[0], *kept[:4], low],
    )


def enter_kernel(blocks, w, row, *refs):
    index_ref = refs[0]
    c_refs = refs[1 : 1 + blocks]
    low_ref, slope_ref = refs[1 + blocks : 3 + blocks]
    context_ref, pre_ref, sum_ref = refs[3 + blocks : 6 + blocks]
    c_all, low, c_sems, low_sems = refs[6 + blocks :]
    loads = loads_of_weights(low_ref, row, low, low_sems)
    loads += copies_of_blocks(index_ref[0], c_refs, c_all, c_sems)
    start_all(loads)
    wait_all(loads)
    do_enter(
        w, lambda at: dot(c_all[at], low[...], 1, 1), slope_ref, context_ref, pre_ref, sum_ref
    )


def enter(order, index, c_blocks, kept, weights):
    w, ff = weights["w"], weights["ff"]
    low, row = weights["low"]
    blocks = len(c_blocks)
    return order.call(
        functools.partial(enter_kernel, blocks, w, row),
        "enter",
        60,
        [SMEM] + [ANY] * (blocks + 1) + [VMEM],
        [VMEM] * 3,
        rows_of(w, ff) + [shape((1, ff), F32)],
        held(D) + [pltpu.VMEM((w + ff, D), BF)] + dma(blocks, low.shape[0]),
        [index, *c_blocks, low, kept[4]],
    )


def scratch_of_backward(w):
    return [pltpu.VMEM((w, TOK_MB), BF)] + [pltpu.VMEM((TOK_MB, w), F32)] * 3


def backward_kernel(blocks, heads, w, row, *refs):
    index_ref = refs[0]
    x_refs = refs[1 : 1 + blocks]
    inner = refs[1 + blocks : 9 + blocks]
    main_ref, norms_ref, table_ref = refs[9 + blocks : 12 + blocks]
    keep_ref, send_ref, *outs = refs[12 + blocks : 17 + blocks]
    x_all, main, partial, *scratch, x_sems, main_sems, out_sems = refs[17 + blocks :]
    loads = copies_of_blocks(index_ref[0], x_refs, x_all, x_sems)
    loads += loads_of_weights(main_ref, row, main, main_sems)
    start_all(loads)
    leaving = Leaving(index_ref[0], partial, keep_ref, send_ref, out_sems)
    do_backward(
        heads, w, *inner, loads, x_all, main, norms_ref, table_ref, *outs, *scratch, partial, leaving
    )
    leaving.wait()


def backward(order, index, x_blocks, kept, entered, weights, angles):
    queries, keys, values, _, _, context, logs = kept
    blocks = len(x_blocks)
    w, heads, ff = weights["w"], weights["heads"], weights["ff"]
    main, row = weights["main"]
    return order.call(
        functools.partial(backward_kernel, blocks, heads, w, row),
        "backward",
        60,
        [SMEM] + [ANY] * blocks + [VMEM] * 8 + [ANY] + [VMEM] * 2,
        [ANY, ANY] + [VMEM] * 3,
        halves_of(blocks) + rows_of(3 * w) + [shape((8, D), F32), shape((1, 3 * w), F32)],
        held(D)
        + [pltpu.VMEM((3 * w + ff, D), BF)]
        + held(D)
        + scratch_of_backward(w)
        + dma(blocks, main.shape[0], blocks),
        [
            index,
            *x_blocks,
            angles[0],
            queries,
            keys,
            values,
            context,
            logs,
            entered[0],
            entered[1],
            main,
            weights["norms"],
            angles[1],
        ],
    )


def products_of(ready, index, source_refs, low_ref, low_row, c_all, low, c_sems, low_sems):
    if ready:
        loads = [pltpu.make_async_copy(source_refs[0], c_all, c_sems.at[0])]
        return loads, lambda at: c_all[at]
    loads = loads_of_weights(low_ref, low_row, low, low_sems)
    loads += copies_of_blocks(index, source_refs, c_all, c_sems)
    return loads, lambda at: dot(c_all[at], low[...], 1, 1)


def whole_backward_kernel(blocks, given, heads, w, main_row, low_row, *refs):
    index_ref = refs[0]
    c_refs = refs[1 : 1 + given]
    refs = refs[1 + given :]
    x_refs = refs[:blocks]
    starts_ref, q_ref, k_ref, v_ref, context_ref, logs_ref, slope_ref = refs[blocks : 7 + blocks]
    main_ref, low_ref, norms_ref, table_ref = refs[7 + blocks : 11 + blocks]
    keep_ref, send_ref, pre_ref, pre_sum_ref, *outs = refs[11 + blocks : 18 + blocks]
    c_all, x_all, main, low, partial, grad_context, *scratch = refs[18 + blocks : 28 + blocks]
    c_sems, x_sems, main_sems, low_sems, out_sems = refs[28 + blocks :]
    loads, products = products_of(
        given < blocks, index_ref[0], c_refs, low_ref, low_row, c_all, low, c_sems, low_sems
    )
    later = copies_of_blocks(index_ref[0], x_refs, x_all, x_sems)
    later += loads_of_weights(main_ref, main_row, main, main_sems)
    start_all(loads + later)
    leaving = Leaving(index_ref[0], partial, keep_ref, send_ref, out_sems)
    wait_all(loads)
    do_enter(w, products, slope_ref, grad_context, pre_ref, pre_sum_ref)
    do_backward(
        heads,
        w,
        starts_ref,
        q_ref,
        k_ref,
        v_ref,
        context_ref,
        logs_ref,
        grad_context,
        pre_ref,
        later,
        x_all,
        main,
        norms_ref,
        table_ref,
        *outs,
        *scratch,
        partial,
        leaving,
    )
    leaving.wait()


def held_cotangent(c_blocks, blocks):
    if len(c_blocks) < blocks:
        return [pltpu.VMEM(c_blocks[0].shape, F32)]
    return held(D)


def whole_backward(order, index, c_blocks, x_blocks, kept, weights, angles):
    queries, keys, values, _, slope, context, logs = kept
    blocks = len(x_blocks)
    w, heads, ff = weights["w"], weights["heads"], weights["ff"]
    main, main_row = weights["main"]
    low, low_row = weights["low"]
    dp = main.shape[0]
    return order.call(
        functools.partial(
            whole_backward_kernel, blocks, len(c_blocks), heads, w, main_row, low_row
        ),
        "whole_backward",
        60,
        [SMEM] + [ANY] * (len(c_blocks) + blocks) + [VMEM] * 7 + [ANY] * 2 + [VMEM] * 2,
        [ANY, ANY] + [VMEM] * 5,
        halves_of(blocks)
        + rows_of(ff)
        + [shape((1, ff), F32)]
        + rows_of(3 * w)
        + [shape((8, D), F32), shape((1, 3 * w), F32)],
        held_cotangent(c_blocks, blocks)
        + held(D)
        + [pltpu.VMEM((3 * w + ff, D), BF), pltpu.VMEM((w + ff, D), BF)]
        + held(D, w)
        + scratch_of_backward(w)
        + dma(blocks, blocks, dp, dp, blocks),
        [
            index,
            *c_blocks,
            *x_blocks,
            angles[0],
            queries,
            keys,
            values,
            context,
            logs,
            slope,
            main,
            low,
            weights["norms"],
            angles[1],
        ],
    )


def layer_kernel(blocks, heads, w, main_row, low_row, *refs):
    index_ref = refs[0]
    c_ref = refs[1]
    refs = refs[2:]
    x_refs = refs[:blocks]
    starts_ref, main_ref, low_ref, norms_ref, bias_ref, table_ref = refs[blocks : 6 + blocks]
    (y_keep, y_send, u_keep, u_send, hidden_ref, context_ref, pre_ref, pre_sum_ref, *outs) = refs[
        6 + blocks : 17 + blocks
    ]
    (c_all, x_all, main, low, y_all, u_all, q_ref, k_ref, v_ref, slope_ref, grad_context) = refs[
        17 + blocks : 28 + blocks
    ]
    logs_ref, v_turned, *scratch = refs[28 + blocks : 34 + blocks]
    c_sems, x_sems, main_sems, low_sems, y_sems, u_sems = refs[34 + blocks :]
    index = index_ref[0]
    loads = copies_of_blocks(index, x_refs, x_all, x_sems)
    loads += loads_of_weights(main_ref, main_row, main, main_sems)
    low_loads = loads_of_weights(low_ref, low_row, low, low_sems)
    c_loads = [pltpu.make_async_copy(c_ref, c_all, c_sems.at[0])]
    start_all(loads + low_loads + c_loads)
    y_leaving = Leaving(index, y_all, y_keep, y_send, y_sems)
    u_leaving = Leaving(index, u_all, u_keep, u_send, u_sems)
    wait_all(loads)
    do_project(
        w, x_all, main, norms_ref, bias_ref, table_ref, q_ref, k_ref, v_ref, hidden_ref, slope_ref
    )
    do_attend(
        heads,
        w,
        starts_ref,
        q_ref,
        k_ref,
        v_ref,
        hidden_ref,
        low,
        low_loads,
        context_ref,
        logs_ref,
        v_turned,
        y_all,
        y_leaving,
    )
    wait_all(c_loads)
    do_enter(w, lambda at: c_all[at], slope_ref, grad_context, pre_ref, pre_sum_ref)
    do_backward(
        heads,
        w,
        starts_ref,
        q_ref,
        k_ref,
        v_ref,
        context_ref,
        logs_ref,
        grad_context,
        pre_ref,
        [],
        x_all,
        main,
        norms_ref,
        table_ref,
        *outs,
        *scratch,
        u_all,
        u_leaving,
    )
    y_leaving.wait()
    u_leaving.wait()


def whole_layer(order, index, products, x_blocks, weights, angles):
    blocks = len(x_blocks)
    w, heads, ff = weights["w"], weights["heads"], weights["ff"]
    main, main_row = weights["main"]
    low, low_row = weights["low"]
    dp = main.shape[0]
    return order.call(
        functools.partial(layer_kernel, blocks, heads, w, main_row, low_row),
        "whole_layer",
        60,
        [SMEM] + [ANY] * (1 + blocks) + [VMEM] + [ANY] * 2 + [VMEM] * 3,
        [ANY] * 4 + [VMEM] * 7,
        halves_of(blocks)
        + halves_of(blocks)
        + rows_of(ff, w, ff)
        + [shape((1, ff), F32)]
        + rows_of(3 * w)
        + [shape((8, D), F32), shape((1, 3 * w), F32)],
        [pltpu.VMEM(products.shape, F32)]
        + held(D)
        + [pltpu.VMEM((3 * w + ff, D), BF), pltpu.VMEM((w + ff, D), BF)]
        + held(D, D, w, w, w, ff, w)
        + [pltpu.VMEM((8, TOK_MB), F32), pltpu.VMEM((w, TOK_MB), BF)]
        + scratch_of_backward(w)
        + dma(1, blocks, dp, dp, blocks, blocks),
        [
            index,
            products,
            *x_blocks,
            angles[0],
            main,
            low,
            weights["norms"],
            weights["bias"],
            angles[1],
        ],
    )


def put_vectors(out_ref, begin, stage_ref, vec_a, vec_b, raw_a, raw_b, pre_a, pre_b, own_ref, order_ref, raw_order, pre_order):
    dp, _, share = out_ref.shape
    half = dp // 2
    rows = [vec_a[:4] + vec_b[:4], own_ref[...], jnp.zeros((3, vec_a.shape[1]), F32)]
    norms = dot(jnp.concatenate(rows, axis=0).astype(BF), order_ref[...], 1, 0)

    def moved(first, second, order):
        value = (first[...] + second[...]).astype(BF)
        return dot(jnp.broadcast_to(value, (8, value.shape[1])), order[...], 1, 0)[:1]

    raw, pre = moved(raw_a, raw_b, raw_order), moved(pre_a, pre_b, pre_order)
    for j in range(dp):
        mine = jnp.where(stage_ref[0] == j // half, 1.0, 0.0)
        cols = slice(j % half * share, (j % half + 1) * share)
        block = [
            norms[:5, j * share : (j + 1) * share],
            raw[:, cols] * mine,
            pre[:, cols] * mine,
            jnp.zeros((SMALL - 7, share), F32),
        ]
        out_ref[j, begin : begin + SMALL] = jnp.concatenate(block, axis=0).astype(BF)


def grads_kernel(blocks, plan, extra, *refs):
    index_ref, norms_ref = refs[:2]
    with_cot = None in plan
    normed = sorted({which for which in plan if which is not None})
    count = MB * blocks
    row_refs = refs[2 : 2 + count]
    lefts = refs[2 + count : 2 + count + MB * len(plan)]
    rest = refs[2 + count + MB * len(plan) :]
    extras, rest = rest[:extra], rest[extra:]
    out_ref, total, *scratch = rest
    side_sems, sems = scratch.pop(), scratch.pop()
    sides, scratch = scratch[: MB * len(plan)], scratch[MB * len(plan) :]
    index = index_ref[0]
    dp, _, share = out_ref.shape
    loads = []
    for unit in range(MB):
        part = row_refs[unit * blocks : (unit + 1) * blocks]
        loads.append(copies_of_blocks(index, part, scratch[0].at[unit], sems.at[unit]))
        for i in range(len(plan)):
            left = lefts[i * MB + unit]
            loads[unit].append(
                pltpu.make_async_copy(left, sides[i * MB + unit], side_sems.at[i * MB + unit])
            )
        start_all(loads[unit])
    for unit in range(MB):
        wait_all(loads[unit])
        rights = {None: scratch[0]}
        if not with_cot:
            rights = dict(zip(normed, scratch))
            for at in chunks():
                hat, _ = normalize(scratch[0][unit, at])
                for norm in normed:
                    row = hat * norms_ref[norm : norm + 1] + norms_ref[2 + norm : 3 + norm]
                    rights[norm][unit, at] = row.astype(BF)
        begin = 0
        for i, which in enumerate(plan):
            left = sides[i * MB + unit]
            rows = slice(begin, begin + left.shape[1])
            part = dot(left[...], rights[which][unit], 0, 0)
            if unit:
                part = part + total[rows]
            if unit + 1 < MB:
                total[rows] = part
            else:
                for j in range(dp):
                    out_ref[j, rows] = part[:, j * share : (j + 1) * share].astype(BF)
            begin = rows.stop
    if extra:
        put_vectors(out_ref, begin, *extras)


def weight_grads(order, index, c_blocks, x_blocks, pieces, norms, dp, extra=()):
    plan = [which for _, which in pieces]
    blocks = len(x_blocks[0])
    rows = [block for unit in (c_blocks if None in plan else x_blocks) for block in unit]
    lefts = [left for part, _ in pieces for left in part]
    size = sum(part[0].shape[1] for part, _ in pieces) + (SMALL if extra else 0)
    buffers = len(set(plan))
    return order.call(
        functools.partial(grads_kernel, blocks, plan, len(extra)),
        "weight_grads",
        60,
        [SMEM, VMEM] + [ANY] * (len(rows) + len(lefts)) + [SMEM, *[VMEM] * (len(extra) - 1)][: len(extra)],
        [VMEM],
        [shape((dp, size, D // dp), BF)],
        [pltpu.VMEM((size, D), F32)]
        + [pltpu.VMEM(left.shape, BF) for left in lefts]
        + [pltpu.VMEM((MB, TOK_MB, D), BF)] * buffers
        + [pltpu.SemaphoreType.DMA((MB, blocks)), pltpu.SemaphoreType.DMA((len(lefts),))],
        [index, norms, *rows, *lefts, *extra],
    )[0]


SMALL = 16


def put_halves(at_first, keep, send, begin, size, low, high):
    keep[begin : begin + size] = jnp.where(at_first, low, high)
    send[begin : begin + size] = jnp.where(at_first, high, low)


def pack_kernel(width, w, stage_ref, qkv_ref, up_ref, out_ref, down_ref, keep_ref, send_ref, *held):
    (qkv, up, out, down), sems = held[:4], held[4]
    sources = (qkv_ref, up_ref, out_ref, down_ref)
    loads = [
        pltpu.make_async_copy(source, target, sems.at[i])
        for i, (source, target) in enumerate(zip(sources, held))
    ]
    start_all(loads)
    at_first = stage_ref[0] == 0
    ff = up.shape[1] // 2
    if w != width:
        keep_ref[...] = jnp.zeros_like(keep_ref)
        send_ref[...] = jnp.zeros_like(send_ref)
    wait_all(loads)
    for i in range(3):
        turned = qkv[i].T
        put_halves(at_first, keep_ref, send_ref, i * w, width, turned[:width], turned[width:])
    turned = up[...].T
    put_halves(at_first, keep_ref, send_ref, 3 * w, ff, turned[:ff], turned[ff:])
    begin = 3 * w + ff
    put_halves(at_first, keep_ref, send_ref, begin, width, out[:width], out[width:])
    put_halves(at_first, keep_ref, send_ref, begin + w, ff, down[:ff], down[ff:])


def pack(order, stage, qkv, up, out, down, w):
    width, ff, share = qkv.shape[2] // 2, up.shape[1] // 2, up.shape[0]
    return order.call(
        functools.partial(pack_kernel, width, w),
        "pack",
        60,
        [SMEM] + [ANY] * 4,
        [VMEM] * 2,
        [shape((4 * w + 2 * ff, share), BF)] * 2,
        [pltpu.VMEM(value.shape, BF) for value in (qkv, up, out, down)] + dma(4),
        [stage, qkv, up, out, down],
    )


def by_stage_kernel(stage_ref, *refs):
    at_first = stage_ref[0] == 0
    pairs, (first_ref, second_ref) = refs[:-2], refs[-2:]
    begin = 0
    for mine_ref, other_ref in zip(pairs[::2], pairs[1::2]):
        rows = slice(begin, begin + mine_ref.shape[0])
        mine, other = mine_ref[...], other_ref[...]
        first_ref[rows] = jnp.where(at_first, mine, other)
        second_ref[rows] = jnp.where(at_first, other, mine)
        begin = rows.stop


def by_stage(order, stage, *pairs):
    rows = sum(mine.shape[0] for mine in pairs[::2])
    return order.call(
        by_stage_kernel,
        "by_stage",
        16,
        [SMEM] + [VMEM] * len(pairs),
        [VMEM] * 2,
        [shape((rows, pairs[0].shape[1]), BF)] * 2,
        [],
        [stage, *pairs],
    )


def both_halves(stage_ref, mine0, mine1, from0, from1, begin, size):
    at_first = stage_ref[0] == 0
    rows = slice(begin, begin + size)
    low = jnp.where(at_first, mine0[rows], from1[rows])
    high = jnp.where(at_first, from0[rows], mine1[rows])
    return low.astype(F32), high.astype(F32)


def unpack_outer_kernel(width, w, ff, *refs):
    parts, (out_ref, down_ref) = refs[:5], refs[5:]
    out_ref[:width], out_ref[width:] = both_halves(*parts, 0, width)
    down_ref[:ff], down_ref[ff:] = both_halves(*parts, w, ff)


def unpack_inner_kernel(width, w, ff, *refs):
    parts, (up_ref, qkv_ref) = refs[:5], refs[5:]
    low, high = both_halves(*parts, 0, ff)
    up_ref[:, :ff] = low.T
    up_ref[:, ff:] = high.T
    for i in range(3):
        low, high = both_halves(*parts, ff + i * w, width)
        qkv_ref[i] = jnp.concatenate([low, high], axis=0).T


def unpack(kernel, order, stage, parts, out_shape):
    return order.call(
        kernel,
        "unpack",
        24,
        [SMEM] + [VMEM] * 4,
        [VMEM] * len(out_shape),
        out_shape,
        [],
        [stage, *parts],
    )


def picked_kernel(bit, flip, pairs, plains, *refs):
    index_ref = refs[0]
    out_ref, held, sems = refs[1 + pairs + plains :]
    want = (index_ref[0] >> bit) & 1
    if flip:
        want = 1 - want
    copies = []
    for i in range(pairs + plains):
        for j in range(out_ref.shape[0]):
            source = refs[1 + i].at[j, want] if i < pairs else refs[1 + i].at[j]
            copies.append(pltpu.make_async_copy(source, held.at[i, j], sems.at[i, j]))
    for copy in copies:
        copy.start()
    for copy in copies:
        copy.wait()
    total = held[0].astype(F32)
    for i in range(1, pairs + plains):
        total = total + held[i].astype(F32)
    out_ref[...] = total.astype(BF)


def picked_sum(order, where, bit, flip, pairs, plains=()):
    dims = (pairs[0].shape[0],) + pairs[0].shape[2:]
    terms = [*pairs, *plains]
    return order.call(
        functools.partial(picked_kernel, bit, flip, len(pairs), len(plains)),
        "picked_sum",
        20,
        [SMEM] + [ANY] * len(terms),
        [VMEM],
        [shape(dims, BF)],
        [
            pltpu.VMEM((len(terms), *dims), BF),
            pltpu.SemaphoreType.DMA((len(terms), dims[0])),
        ],
        [where, *terms],
    )[0]


class Sum:
    def __init__(self, where, keep, send):
        self.where = where
        self.terms = [keep, swap(send, "tensor", 0)]

    def send(self, order, *others):
        place = lax.axis_index("tensor")
        last = bits_of("tensor") - 1
        for bit in range(1, last + 1):
            pairs = [
                term.reshape((term.shape[0] // 2, 2) + term.shape[1:]) for term in self.terms
            ]
            sent = picked_sum(order, self.where, bit, True, pairs)
            self.sent = sent
            self.received = swap(after(sent, *others) if others else sent, "tensor", bit)
            if bit < last:
                own = (place >> bit) & 1
                self.terms = [pick(pair, own, 1) for pair in pairs] + [self.received]
        self.pairs = pairs
        return self

    def cross(self, order):
        last = bits_of("tensor") - 1
        self.own = picked_sum(order, self.where, last, False, self.pairs, [self.received])[0]
        self.other = swap(self.own, "pipe", 0)
        return self


def add_rows_kernel(x_ref, own_ref, other_ref, norms_ref, out_ref):
    bias = norms_ref[4:5] + norms_ref[5:6]
    total = x_ref[...].astype(F32) + own_ref[...].astype(F32) + other_ref[...].astype(F32)
    out_ref[...] = (total + bias).astype(out_ref.dtype)


def add_rows(order, x_rows, summed, weights):
    return order.call(
        add_rows_kernel,
        "add_rows",
        12,
        [VMEM] * 4,
        [VMEM],
        [shape(x_rows.shape, BF)],
        [],
        [x_rows, summed.own, summed.other, weights["norms"]],
    )[0]


def norm_back_rows(x_ref, own_ref, other_ref, cot_ref):
    grad_hat = own_ref[...].astype(F32) + other_ref[...].astype(F32)
    hat, scale = normalize(x_ref[...])
    mean = jnp.mean(grad_hat, axis=-1, keepdims=True)
    along = jnp.mean(grad_hat * hat, axis=-1, keepdims=True)
    return cot_ref[...].astype(F32) + (grad_hat - mean - hat * along) * scale


def norm_back_kernel(x_ref, own_ref, other_ref, cot_ref, out_ref):
    out_ref[...] = norm_back_rows(x_ref, own_ref, other_ref, cot_ref).astype(BF)


def norm_back(order, x_rows, summed, cot_rows):
    return order.call(
        norm_back_kernel,
        "norm_back",
        16,
        [VMEM] * 4,
        [VMEM],
        [shape(x_rows.shape, BF)],
        [],
        [x_rows, summed.own, summed.other, cot_rows],
    )[0]


def ends_kernel(unit, stage_ref, x_ref, own_ref, other_ref, cot_ref, *refs):
    middle_ref, y_own_ref, y_other_ref, norms_ref = refs[:4]
    ends_ref, token_ref, held, sem = refs[-4:]
    token_ref[...] = jnp.zeros_like(token_ref)

    @pl.when(stage_ref[0] == 0)
    def _():
        held[...] = norm_back_rows(x_ref, own_ref, other_ref, cot_ref)

    @pl.when(stage_ref[0] != 0)
    def _():
        add_rows_kernel(middle_ref, y_own_ref, y_other_ref, norms_ref, held)

    copy = pltpu.make_async_copy(held, ends_ref.at[unit], sem)
    copy.start()
    copy.wait()


def write_ends(order, unit, stage, ends, x_rows, summed, cot_rows, middle_rows, y_sum, weights):
    args = [
        stage,
        x_rows,
        summed.own,
        summed.other,
        cot_rows,
        middle_rows,
        y_sum.own,
        y_sum.other,
        weights["norms"],
    ]
    more = {}
    if ends is not None:
        more = dict(input_output_aliases={len(args): 0})
        args.append(ends)
    return order.call(
        functools.partial(ends_kernel, unit),
        "ends",
        20,
        [SMEM] + [VMEM] * 8 + [ANY] * len(more),
        [ANY, VMEM],
        [shape((MB, *x_rows.shape), F32), shape((8, 128), F32)],
        [pltpu.VMEM(x_rows.shape, F32), pltpu.SemaphoreType.DMA],
        args,
        **more,
    )[0]


def angles_for(lengths_row, w):
    finish = jnp.cumsum(lengths_row)
    places = jnp.arange(TOK_MB, dtype=jnp.int32)
    after = (places[:, None] >= finish[None, :]).astype(jnp.int32)
    starts = jnp.sum(after * lengths_row[None, :], axis=1)
    position = (places - starts).astype(F32)
    inverse_freq = 10000.0 ** (-jnp.arange(ROT // 2, dtype=F32) * 2.0 / ROT)
    phase = position[:, None] * inverse_freq[None, :]
    cosine, sine = jnp.cos(phase), jnp.sin(phase)
    rest = jnp.zeros((TOK_MB, HD - 2 * ROT), F32)
    table = jnp.concatenate([cosine, cosine, -sine, sine, rest], axis=1)
    return starts[None], jnp.tile(table, (1, w // HD))


def body(
    boundary,
    lengths,
    gains,
    biases,
    qkv_weight,
    qkv_bias,
    out_weight,
    up_weight,
    up_bias,
    down_weight,
):
    stage = lax.axis_index("pipe")
    at_first = stage == 0
    dp = lax.axis_size("dp")
    tensor = lax.axis_size("tensor")
    index = lax.axis_index("tensor").astype(jnp.int32)[None]
    stage_word = stage.astype(jnp.int32)[None]
    order = Order()
    share = D // dp
    width = qkv_weight.shape[3] // 2
    ff = up_weight.shape[2] // 2
    heads = width // HD
    w = max(width, 128)
    cut = 3 * w + ff

    def split(mine, other):
        return jnp.where(at_first, mine, other), jnp.where(at_first, other, mine)

    def half(value, which, axis):
        size = value.shape[axis] // 2
        return lax.dynamic_slice_in_dim(value, which * size, size, axis)

    def padded(value, axis):
        if w == width:
            return value
        pads = [(0, 0)] * value.ndim
        pads[axis] = (0, w - width)
        return jnp.pad(value, pads)

    tiles = boundary[0, :, 0]
    angles = [angles_for(lengths[unit, 0], w) for unit in range(MB)]
    far = tensor // 2

    def gather_far(value):
        blocks = {0: value}
        for bit in reversed(range(1, bits_of("tensor"))):
            for s in list(blocks):
                blocks[s | (1 << bit)] = swap(blocks[s], "tensor", bit)
        return [blocks[s] for s in sorted(blocks)]

    piece = gains.shape[2]
    small = jnp.concatenate([gains[0], biases[0]])
    small = jnp.moveaxis(gather_tensor(small), 0, 1).reshape(6, share)
    flat = jnp.concatenate([qkv_bias[0].reshape(-1), up_bias[0]])
    flat = jnp.pad(flat, (0, (SMALL - 6) * share - flat.shape[0])).reshape(-1, share)
    small = jnp.concatenate([small, flat])

    mine, sent = pack(
        order,
        stage_word,
        jnp.moveaxis(qkv_weight[0], 1, 0),
        up_weight[0],
        out_weight[0],
        down_weight[0],
        w,
    )
    other = swap(sent, "pipe", 0)
    order.hold(small)
    order.pause()
    small_other = swap(small, "pipe", 0)
    def gather_near(order, blocks):
        found = [None] * tensor
        for i, rows in enumerate(blocks):
            found[2 * i] = rows
            found[2 * i + 1] = swap(after(rows, order.last[0]), "tensor", 0)
        return found

    order.pause()
    stack_0, stack_1 = by_stage(order, stage_word, mine, other, small, small_other)
    far_tiles = [gather_far(after(tile, order.last[0])) for tile in tiles]
    stack_0 = lax.all_gather(stack_0, "dp", axis=0)

    def vectors_of(gathered, row):
        small = gathered[:, row : row + SMALL].astype(F32)
        norms = small[:, :6].reshape(dp, 6, tensor, piece).transpose(1, 2, 0, 3).reshape(6, D)
        flat = small[:, 6:].reshape(dp, -1)
        raw = flat[:, : 3 * piece].reshape(dp, 3, piece).transpose(1, 0, 2)
        raw = padded(half(raw.reshape(3, 2 * width), stage, 1), 1).reshape(1, 3 * w)
        up = flat[:, 3 * piece : 3 * piece + up_bias.shape[1]].reshape(1, 2 * ff)
        return dict(norms=norms, bias=jnp.concatenate([raw, half(up, stage, 1)], axis=1))

    x_rows, cot_rows, x_blocks, c_blocks = [], [], [], []

    def take_tiles(unit):
        others = [swap(tile, "pipe", 0) for tile in far_tiles[unit]]
        order.pause()
        x_far, cot_far = [], []
        for mine, other in zip(far_tiles[unit], others):
            rows, cot = by_stage(order, stage_word, mine, other)
            x_far.append(rows)
            cot_far.append(cot)
        x_rows.append(x_far[0])
        cot_rows.append(cot_far[0])
        order.pause()
        x_blocks.append(gather_near(order, x_far))
        order.pause()
        order.hold(*x_blocks[unit])
        order.pause()
        c_blocks.append(gather_near(order, cot_far))
        order.pause()
        order.hold(*c_blocks[unit])

    order.hold(*[value for pair in angles for value in pair])
    order.pause()
    take_tiles(0)
    stack_1 = lax.all_gather(after(stack_1, x_rows[0]), "dp", axis=0)
    take_tiles(1)
    order.pause()
    row = 4 * w + 2 * ff
    layers = [
        dict(w=w, ff=ff, heads=heads, main=(stack, 0), low=(stack, cut))
        for stack in (stack_0, stack_1)
    ]
    layers[0].update(vectors_of(stack_0, row))

    units = range(MB)
    kept = [[None] * MB, [None] * MB]
    entered = [[None] * MB, [None] * MB]
    back = [[None] * MB, [None] * MB]

    def picks(sources, count):
        return (jnp.arange(count)[:, None] == sources[None, :]).astype(BF)

    column = jnp.arange(D)
    order_norms = picks(
        column % share // piece * (D // tensor) + column // share * piece + column % piece, D
    )
    column = jnp.arange(dp // 2 * share)
    group, place = column // share, column % share
    order_raw = picks(
        jnp.where(place < 3 * piece, place // piece * w + group * piece + place % piece, -1), 3 * w
    )
    up_piece = 2 * ff // dp
    order_pre = picks(jnp.where(place < up_piece, group * up_piece + place, -1), ff)

    def vector_rows(layer, cots):
        own = sum(jnp.sum(rows.astype(F32), axis=0) for rows in cots)
        own = own * jnp.where(at_first, 1.0, 0.0)
        sources = ((back, 1), (back, 2), (entered, 2))
        parts = [source[layer][unit][at] for source, at in sources for unit in units]
        return [stage_word, *parts, own[None], order_norms, order_raw, order_pre]

    def vectors_from(rows_0, rows_1):
        both = jnp.stack([rows_0, rows_1]).astype(F32)
        norm = both[:, :5].reshape(2, 5, tensor, piece).transpose(2, 0, 1, 3)
        place = lax.axis_index("tensor")
        total = pick(norm, place, 0)
        for s in range(1, tensor):
            pairs = [(i, i ^ s) for i in range(tensor)]
            total = total + lax.ppermute(pick(norm, place ^ s, 0), "tensor", pairs)
        flat = jnp.concatenate([total.reshape(2, -1), both[:, 5:7].reshape(2, -1)], axis=1)
        mine = jnp.where(at_first, flat[0], flat[1])
        total = mine + swap(jnp.where(at_first, flat[1], flat[0]), "pipe", 0)
        norm = total[: 5 * piece].reshape(5, piece)
        raw = total[5 * piece : 5 * piece + 3 * piece].reshape(3, piece)
        begin = 5 * piece + share
        return norm, raw, total[begin : begin + up_bias.shape[1]]

    def run_project(layer, unit, blocks):
        kept[layer][unit] = project(order, index, blocks, layers[layer], angles[unit])

    def run_attend(layer, unit):
        keep, send, *rest = attend(
            order, index, tensor, kept[layer][unit], layers[layer], angles[unit]
        )
        kept[layer][unit] = [*kept[layer][unit], *rest]
        return Sum(index, keep, send)

    def run_backward(layer, unit, cots, blocks):
        keep, send, pre, pre_sum, *back[layer][unit] = whole_backward(
            order, index, cots, blocks, kept[layer][unit], layers[layer], angles[unit]
        )
        entered[layer][unit] = [None, pre, pre_sum]
        return Sum(index, keep, send)

    def run_layer(unit, blocks):
        y_keep, y_send, u_keep, u_send, hidden, context, pre, pre_sum, *rest = whole_layer(
            order, index, products[unit], blocks, layers[1], angles[unit]
        )
        kept[1][unit] = [None, None, None, hidden, None, context, None]
        entered[1][unit] = [None, pre, pre_sum]
        back[1][unit] = rest
        return Sum(index, y_keep, y_send), Sum(index, u_keep, u_send)

    def reduced(layer, names, cots, rows, extra=()):
        sources = dict(
            out=(kept, 5, None), down=(kept, 3, None), up=(entered, 1, 1), qkv=(back, 0, 0)
        )
        pieces = []
        for name in names:
            held_in, place, which = sources[name]
            pieces.append(([held_in[layer][unit][place] for unit in units], which))
        norms = layers[layer]["norms"]
        value = weight_grads(order, index, cots, rows, pieces, norms, dp, extra)
        return lax.psum_scatter(value, "dp", scatter_dimension=0)

    run_project(0, 0, x_blocks[0])
    sum_a = run_attend(0, 0)
    order.pause()
    sum_a.send(order)
    run_project(0, 1, x_blocks[1])
    sum_b = run_attend(0, 1)
    sum_a.cross(order)
    sum_b.send(order)
    middle_a = add_rows(order, x_rows[0], sum_a, layers[0])
    far_a = gather_far(middle_a)
    sum_b.cross(order)
    layers[1].update(vectors_of(after(stack_1, order.last[0]), row))
    products = [cotangent(order, index, c_blocks[unit], layers[1]) for unit in units]
    blocks_a = gather_near(order, far_a)
    order.hold(stack_1)
    middle_b = add_rows(order, x_rows[1], sum_b, layers[0])
    far_b = gather_far(middle_b)

    y_a, sum_a = run_layer(0, blocks_a)
    order.pause()
    blocks_b = gather_near(order, far_b)
    middle_blocks = [blocks_a, blocks_b]
    order.hold(y_a.terms[1])
    sum_a.send(order)
    run_project(1, 1, blocks_b)
    y_b = run_attend(1, 1)
    sum_a.cross(order)
    order.hold(y_b.terms[1])
    y_a.send(order)
    y_b.send(order)
    sum_b = run_backward(1, 1, [products[1]], blocks_b)
    cot_a = norm_back(order, middle_a, sum_a, cot_rows[0])
    sum_b.send(order)
    y_a.cross(order)
    outer_1 = reduced(1, ("out", "down"), c_blocks, middle_blocks)
    sum_b.cross(order)
    far_a = gather_far(after(cot_a, order.last[0]))
    inner_1 = reduced(1, ("up", "qkv"), c_blocks, middle_blocks, vector_rows(1, cot_rows))
    cot_blocks = [gather_near(order, far_a)]
    y_b.cross(order)
    cot_b = norm_back(order, middle_b, sum_b, cot_rows[1])
    far_b = gather_far(cot_b)

    order.hold(outer_1, y_a.other)
    order.pause()
    from_outer_1 = swap(outer_1, "pipe", 0)
    sum_a = run_backward(0, 0, cot_blocks[0], x_blocks[0])
    cot_blocks.append(gather_near(order, far_b))
    order.pause()
    outer_0 = reduced(0, ("out", "down"), cot_blocks, x_blocks)
    sum_a.send(order)
    order.hold(from_outer_1, inner_1, y_b.other)
    order.pause()
    from_inner_1 = swap(inner_1, "pipe", 0)
    sum_b = run_backward(0, 1, cot_blocks[1], x_blocks[1])
    order.hold(from_inner_1)
    inner_0 = reduced(0, ("up", "qkv"), cot_blocks, x_blocks, vector_rows(0, (cot_a, cot_b)))
    from_outer_0 = swap(after(outer_0, order.last[0]), "pipe", 0)
    order.pause()
    sum_b.send(order)
    sum_a.cross(order)
    order.pause()
    sum_b.cross(order)
    ends = write_ends(
        order, 0, stage_word, None, x_rows[0], sum_a, cot_a, middle_a, y_a, layers[1]
    )
    order.hold(from_outer_0)
    grad_out, grad_down = unpack(
        functools.partial(unpack_outer_kernel, width, w, ff),
        order,
        stage_word,
        [outer_0, outer_1, from_outer_0, from_outer_1],
        [shape((2 * width, share), F32), shape((2 * ff, share), F32)],
    )
    order.hold(inner_0)
    ends = write_ends(
        order, 1, stage_word, ends, x_rows[1], sum_b, cot_b, middle_b, y_b, layers[1]
    )
    last = 3 * w + ff
    from_inner_0 = swap(inner_0, "pipe", 0)
    vectors = vectors_from(inner_0[last:], inner_1[last:])
    order.hold(from_inner_0)
    grad_up, grad_qkv = unpack(
        functools.partial(unpack_inner_kernel, width, w, ff),
        order,
        stage_word,
        [inner_0, inner_1, from_inner_0, from_inner_1],
        [shape((share, 2 * ff), F32), shape((3, share, 2 * width), F32)],
    )
    grad_qkv = jnp.moveaxis(grad_qkv, 0, 1)
    norm_grads, grad_qkv_bias, grad_up_bias = vectors
    grad_gains = norm_grads[:2]
    grad_biases = jnp.concatenate([norm_grads[2:5], norm_grads[4:5]])
    return (
        ends[None, :, None],
        grad_gains[None],
        grad_biases[None],
        grad_qkv[None],
        grad_qkv_bias[None],
        grad_out[None],
        grad_up[None],
        grad_up_bias[None],
        grad_down[None],
    )


def solution(mesh):
    placed = (
        P("pipe", None, "dp", "tensor", None),
        P(None, "dp", None),
        P("pipe", None, ("tensor", "dp")),
        P("pipe", None, ("tensor", "dp")),
        P("pipe", "dp", None, "tensor"),
        P("pipe", None, ("tensor", "dp")),
        P("pipe", "tensor", "dp"),
        P("pipe", "dp", "tensor"),
        P("pipe", ("tensor", "dp")),
        P("pipe", "tensor", "dp"),
    )
    return jax.shard_map(
        body,
        mesh=mesh,
        in_specs=placed,
        out_specs=(placed[0],) + placed[2:],
        check_vma=False,
    )
```

```python
import functools

import jax
import jax.numpy as jnp
from jax import lax
from jax.experimental import pallas as pl
from jax.experimental.pallas import tpu as pltpu
from jax.sharding import PartitionSpec as P

D = 1024
H = 16
HD = 64
ROT = 16
MB = 2
TOK_MB = 1280
EPS = 1e-05
CHUNK = 256
FLOPS = 10**11
BF = jnp.bfloat16
F32 = jnp.float32
ANY = pl.BlockSpec(memory_space=pl.ANY)
VMEM = pl.BlockSpec(memory_space=pltpu.VMEM)
SMEM = pl.BlockSpec(memory_space=pltpu.SMEM)


def dot(left, right, left_dim, right_dim):
    return lax.dot_general(
        left, right, (((left_dim,), (right_dim,)), ((), ())), preferred_element_type=F32
    )


def shape(dims, dtype):
    return jax.ShapeDtypeStruct(dims, dtype)


def swap(value, axis, bit):
    count = lax.axis_size(axis)
    return lax.ppermute(value, axis, [(i, i ^ (1 << bit)) for i in range(count)])


def bits_of(axis):
    return lax.axis_size(axis).bit_length() - 1


def pick(value, index, axis):
    return lax.dynamic_index_in_dim(value, index, axis, keepdims=False)


def gather_blocks(value):
    blocks = {0: value}
    for bit in reversed(range(bits_of("tensor"))):
        found = [blocks[s] for s in blocks if s]
        for s in list(blocks):
            sent = after(blocks[s], *found) if found and s == 0 else blocks[s]
            blocks[s | (1 << bit)] = swap(sent, "tensor", bit)
    return [blocks[s] for s in range(len(blocks))]


def gather_tensor(value):
    index = lax.axis_index("tensor")
    value = value[None]
    for bit in reversed(range(bits_of("tensor"))):
        other = swap(value, "tensor", bit)
        mine = ((index >> bit) & 1) == 0
        low = jnp.where(mine, value, other)
        high = jnp.where(mine, other, value)
        value = jnp.stack([low, high], axis=1).reshape((-1,) + value.shape[1:])
    return value


def after(value, *others):
    return lax.optimization_barrier((value, *others))[0]


def gather_direct(value, axis):
    count = lax.axis_size(axis)
    index = lax.axis_index(axis)
    found = [value]
    for hop in range(1, count):
        found.append(lax.ppermute(value, axis, [(j, (j + hop) % count) for j in range(count)]))
    turned = jnp.stack(found[::-1] * 2)
    return lax.dynamic_slice_in_dim(turned, count - 1 - index, count, 0)


def scatter_direct(value, axis):
    count = lax.axis_size(axis)
    index = lax.axis_index(axis)
    total = pick(value, index, 0)
    for hop in range(1, count):
        sent = pick(value, (index + hop) % count, 0)
        total = total + lax.ppermute(sent, axis, [(j, (j + hop) % count) for j in range(count)])
    return total


def copies_of_blocks(index, blocks, target, sems):
    copies = []
    for s, block in enumerate(blocks):
        rows = block.shape[0]
        where = pl.multiple_of((index ^ s) * rows, rows)
        copies.append(pltpu.make_async_copy(block, target.at[pl.ds(where, rows)], sems.at[s]))
    return copies


def copies_to_halves(index, source, keep, send, sems, rows):
    copies = []
    own = index & 1
    for block in range(source.shape[0] // rows):
        part = source.at[pl.ds(block * rows, rows)]
        copies.append(
            (
                own == block & 1,
                pltpu.make_async_copy(part, keep.at[block >> 1], sems.at[block]),
                pltpu.make_async_copy(part, send.at[block >> 1], sems.at[block]),
            )
        )
    return copies


def start_half(copy):
    is_kept, to_keep, to_send = copy

    @pl.when(is_kept)
    def _():
        to_keep.start()

    @pl.when(jnp.logical_not(is_kept))
    def _():
        to_send.start()


def normalize(rows):
    rows = rows.astype(F32)
    centered = rows - jnp.mean(rows, axis=-1, keepdims=True)
    scale = lax.rsqrt(jnp.mean(centered * centered, axis=-1, keepdims=True) + EPS)
    return centered * scale, scale


def gelu_pair(values):
    share = 0.5 * (1.0 + lax.erf(values * 0.7071067811865476))
    density = jnp.exp(-0.5 * values * values) * 0.3989422804014327
    return values * share, share + values * density


def rotate(values, table_cos, table_sin, sign):
    width = values.shape[1]
    half = ROT // 2
    lanes = lax.broadcasted_iota(jnp.int32, values.shape, 1) % HD
    partner = jnp.where(
        lanes < half, pltpu.roll(values, width - half, 1), pltpu.roll(values, half, 1)
    )
    return values * table_cos + partner * (table_sin * sign)


def unpack_table(packed, sign):
    width = packed.shape[1]
    lanes = lax.broadcasted_iota(jnp.int32, packed.shape, 1) % HD
    table_cos = jnp.where(lanes < ROT, packed, 1.0)
    table_sin = jnp.where(lanes < ROT, pltpu.roll(packed, width - ROT, 1) * sign, 0.0)
    return table_cos, table_sin


def rotate(values, table_cos, table_sin):
    width = values.shape[1]
    half = ROT // 2
    lanes = lax.broadcasted_iota(jnp.int32, values.shape, 1) % HD
    partner = jnp.where(
        lanes < half, pltpu.roll(values, width - half, 1), pltpu.roll(values, half, 1)
    )
    return values * table_cos + partner * table_sin


def chunks():
    return [slice(begin, begin + CHUNK) for begin in range(0, TOK_MB, CHUNK)]


class Order:
    def __init__(self):
        self.last = []

    def hold(self, *values):
        self.last = [*self.last, *values]

    def call(self, kernel, name, vmem, in_specs, out_specs, out_shape, scratch, args, **more):
        count = len(args)
        deps = self.last

        def outer(*refs):
            kernel(*refs[:count], *refs[count + len(deps) :])

        results = pl.pallas_call(
            outer,
            in_specs=in_specs + [ANY] * len(deps),
            out_specs=out_specs,
            out_shape=out_shape,
            scratch_shapes=scratch,
            compiler_params=pltpu.CompilerParams(vmem_limit_bytes=vmem << 20),
            cost_estimate=pl.CostEstimate(
                flops=FLOPS, bytes_accessed=1024, transcendentals=0
            ),
            name=name,
            **more,
        )(*args, *deps)
        self.last = [min(results, key=lambda result: result.size)]
        return results

    def pause(self):
        def nothing(out_ref):
            out_ref[...] = jnp.zeros_like(out_ref)

        self.call(nothing, "pause", 2, [], [VMEM], [shape((8, 128), F32)], [], [])


def loads_of_weights(source, row, target, sems, first=0):
    dp, _, share = source.shape
    rows = target.shape[0]
    return [
        pltpu.make_async_copy(
            source.at[j, pl.ds(row, rows)],
            target.at[:, pl.ds(j * share, share)],
            sems.at[first + j],
        )
        for j in range(dp)
    ]


def start_all(copies):
    for copy in copies:
        copy.start()


def wait_all(copies):
    for copy in copies:
        copy.wait()


class Leaving:
    def __init__(self, index, source, keep, send, sems):
        self.rows = keep.shape[1]
        self.copies = copies_to_halves(index, source, keep, send, sems, self.rows)
        self.done = 0

    def reached(self, end):
        while self.done < len(self.copies) and (self.done + 1) * self.rows <= end:
            start_half(self.copies[self.done])
            self.done += 1

    def wait(self):
        for copy in self.copies:
            copy[1].wait()


def masked(scores, starts, begin):
    key = lax.broadcasted_iota(jnp.int32, scores.shape, 0)
    query = lax.broadcasted_iota(jnp.int32, scores.shape, 1) + begin
    return jnp.where((key <= query) & (key >= starts), scores, -1e30)


def head_only(values, head):
    lanes = lax.broadcasted_iota(jnp.int32, values.shape, 1)
    inside = (lanes >= head * HD) & (lanes < (head + 1) * HD)
    return jnp.where(inside, values, jnp.zeros_like(values))


def turned_back(parts, w):
    rest = w - len(parts) * HD
    if rest:
        parts = parts + [jnp.zeros((rest, parts[0].shape[1]), F32)]
    return jnp.concatenate(parts, axis=0).T


def do_project(w, x_all, main, norms_ref, bias_ref, table_ref, q_ref, k_ref, v_ref, hidden_ref, slope_ref):
    for at in chunks():
        hat, _ = normalize(x_all[at])
        first = (hat * norms_ref[0:1] + norms_ref[2:3]).astype(BF)
        second = (hat * norms_ref[1:2] + norms_ref[3:4]).astype(BF)
        raw = dot(first, main[: 3 * w], 1, 1) + bias_ref[:, : 3 * w]
        table_cos, table_sin = unpack_table(table_ref[at], 1.0)
        q_ref[at] = rotate(raw[:, :w], table_cos, table_sin).astype(BF)
        k_ref[at] = rotate(raw[:, w : 2 * w], table_cos, table_sin).astype(BF)
        v_ref[at] = raw[:, 2 * w :].astype(BF)
        hidden, slope = gelu_pair(dot(second, main[3 * w :], 1, 1) + bias_ref[:, 3 * w :])
        hidden_ref[at] = hidden.astype(BF)
        slope_ref[at] = slope.astype(BF)


def do_attend(heads, w, starts_ref, q_ref, k_ref, v_ref, hidden_ref, low, loads, context_ref, logs_ref, v_turned, partial, leaving):
    v_turned[...] = v_ref[...].T
    logs_ref[...] = jnp.zeros_like(logs_ref)
    for at in chunks():
        starts = starts_ref[:, at]
        queries = q_ref[at] * BF(HD**-0.5)
        turned = []
        for head in range(heads):
            s = dot(k_ref[: at.stop], head_only(queries, head), 1, 1)
            s = masked(s, starts, at.start)
            top = jnp.max(s, axis=0, keepdims=True)
            e = jnp.exp(s - top)
            total = jnp.sum(e, axis=0, keepdims=True)
            part = v_turned[head * HD : (head + 1) * HD, : at.stop]
            turned.append(dot(part, e.astype(BF), 1, 0) / total)
            logs_ref[head : head + 1, at] = top + jnp.log(total)
        context = turned_back(turned, w).astype(BF)
        context_ref[at] = context
        if at.start == 0:
            wait_all(loads)
        total = dot(context, low[:w], 1, 0) + dot(hidden_ref[at], low[w:], 1, 0)
        partial[at] = total.astype(BF)
        leaving.reached(at.stop)


def do_enter(w, products, slope_ref, grad_context, pre_ref, sum_ref):
    total = jnp.zeros(sum_ref.shape, F32)
    for at in chunks():
        both = products(at)
        grad_context[at] = both[:, :w].astype(BF)
        grad_pre = (both[:, w:] * slope_ref[at].astype(F32)).astype(BF)
        pre_ref[at] = grad_pre
        total = total + jnp.sum(grad_pre.astype(F32), axis=0, keepdims=True)
    sum_ref[...] = total


def cotangent_kernel(blocks, row, *refs):
    index_ref = refs[0]
    c_refs = refs[1 : 1 + blocks]
    low_ref, out_ref, c_all, low, c_sems, low_sems = refs[1 + blocks :]
    loads = loads_of_weights(low_ref, row, low, low_sems)
    loads += copies_of_blocks(index_ref[0], c_refs, c_all, c_sems)
    start_all(loads)
    wait_all(loads)
    for at in chunks():
        out_ref[at] = dot(c_all[at], low[...], 1, 1)


def cotangent(order, index, c_blocks, weights):
    w, ff = weights["w"], weights["ff"]
    low, row = weights["low"]
    blocks = len(c_blocks)
    return order.call(
        functools.partial(cotangent_kernel, blocks, row),
        "cotangent",
        24,
        [SMEM] + [ANY] * (blocks + 1),
        [VMEM],
        [shape((TOK_MB, w + ff), F32)],
        held(D) + [pltpu.VMEM((w + ff, D), BF)] + dma(blocks, low.shape[0]),
        [index, *c_blocks, low],
    )[0]


def do_backward(
    heads,
    w,
    starts_ref,
    q_ref,
    k_ref,
    v_ref,
    context_ref,
    logs_ref,
    grad_context,
    pre_ref,
    x_loads,
    x_all,
    main,
    norms_ref,
    table_ref,
    raw_ref,
    vectors_ref,
    sum_ref,
    k_turned,
    grad_q,
    grad_k,
    grad_v,
    partial,
    leaving,
):
    k_turned[...] = (k_ref[...] * BF(HD**-0.5)).T
    grad_k[...] = jnp.zeros_like(grad_k)
    grad_v[...] = jnp.zeros_like(grad_v)
    for at in chunks():
        starts = starts_ref[:, at]
        queries = q_ref[at] * BF(HD**-0.5)
        grads = grad_context[at]
        products = (grads.astype(F32) * context_ref[at].astype(F32)).T
        to_k = to_v = 0.0
        turned = []
        for head in range(heads):
            lanes = slice(head * HD, (head + 1) * HD)
            q, g = head_only(queries, head), head_only(grads, head)
            weighted = jnp.sum(products[lanes], axis=0, keepdims=True)
            s = masked(dot(k_ref[: at.stop], q, 1, 1), starts, at.start)
            p = jnp.exp(s - logs_ref[head : head + 1, at])
            grad_p = dot(v_ref[: at.stop], g, 1, 1)
            grad_s = (p * (grad_p - weighted)).astype(BF)
            to_k = to_k + dot(grad_s, q, 1, 0)
            to_v = to_v + dot(p.astype(BF), g, 1, 0)
            turned.append(dot(k_turned[lanes, : at.stop], grad_s, 1, 0))
        grad_k[: at.stop] += to_k
        grad_v[: at.stop] += to_v
        grad_q[at] = turned_back(turned, w)
    wait_all(x_loads)
    sums = [jnp.zeros((1, D), F32) for _ in range(4)]
    raw_sum = jnp.zeros(sum_ref.shape, F32)
    for at in chunks():
        table_cos, table_sin = unpack_table(table_ref[at], -1.0)
        grad_raw = jnp.concatenate(
            [
                rotate(grad_q[at], table_cos, table_sin),
                rotate(grad_k[at], table_cos, table_sin),
                grad_v[at],
            ],
            axis=1,
        ).astype(BF)
        raw_ref[at] = grad_raw
        raw_sum = raw_sum + jnp.sum(grad_raw.astype(F32), axis=0, keepdims=True)
        grad_first = dot(grad_raw, main[: 3 * w], 1, 0)
        grad_second = dot(pre_ref[at], main[3 * w :], 1, 0)
        hat, _ = normalize(x_all[at])
        for i, term in enumerate(
            (grad_first * hat, grad_second * hat, grad_first, grad_second)
        ):
            sums[i] = sums[i] + jnp.sum(term, axis=0, keepdims=True)
        partial[at] = (grad_first * norms_ref[0:1] + grad_second * norms_ref[1:2]).astype(BF)
        leaving.reached(at.stop)
    vectors_ref[...] = jnp.concatenate(sums + [jnp.zeros((4, D), F32)], axis=0)
    sum_ref[...] = raw_sum


def rows_of(*widths):
    return [shape((TOK_MB, width), BF) for width in widths]


def halves_of(blocks):
    return [shape((blocks // 2, TOK_MB // blocks, D), BF)] * 2


def held(*widths):
    return [pltpu.VMEM((TOK_MB, width), BF) for width in widths]


def dma(*counts):
    return [pltpu.SemaphoreType.DMA((count,)) for count in counts]


def project_kernel(blocks, w, row, *refs):
    index_ref = refs[0]
    x_refs = refs[1 : 1 + blocks]
    main_ref, norms_ref, bias_ref, table_ref = refs[1 + blocks : 5 + blocks]
    outs = refs[5 + blocks : 10 + blocks]
    x_all, main, x_sems, main_sems = refs[10 + blocks :]
    loads = copies_of_blocks(index_ref[0], x_refs, x_all, x_sems)
    loads += loads_of_weights(main_ref, row, main, main_sems)
    start_all(loads)
    wait_all(loads)
    do_project(w, x_all, main, norms_ref, bias_ref, table_ref, *outs)


def project(order, index, x_blocks, weights, angles):
    blocks = len(x_blocks)
    w, ff = weights["w"], weights["ff"]
    main, row = weights["main"]
    return order.call(
        functools.partial(project_kernel, blocks, w, row),
        "project",
        24,
        [SMEM] + [ANY] * (blocks + 1) + [VMEM] * 3,
        [VMEM] * 5,
        rows_of(w, w, w, ff, ff),
        held(D) + [pltpu.VMEM((3 * w + ff, D), BF)] + dma(blocks, main.shape[0]),
        [index, *x_blocks, main, weights["norms"], weights["bias"], angles[1]],
    )


def attend_kernel(heads, w, row, *refs):
    index_ref, starts_ref, q_ref, k_ref, v_ref, hidden_ref, low_ref = refs[:7]
    keep_ref, send_ref, context_ref, logs_ref = refs[7:11]
    low, partial, v_turned, low_sems, out_sems = refs[11:]
    loads = loads_of_weights(low_ref, row, low, low_sems)
    start_all(loads)
    leaving = Leaving(index_ref[0], partial, keep_ref, send_ref, out_sems)
    do_attend(
        heads,
        w,
        starts_ref,
        q_ref,
        k_ref,
        v_ref,
        hidden_ref,
        low,
        loads,
        context_ref,
        logs_ref,
        v_turned,
        partial,
        leaving,
    )
    leaving.wait()


def attend(order, index, blocks, kept, weights, angles):
    w, heads, ff = weights["w"], weights["heads"], weights["ff"]
    low, row = weights["low"]
    return order.call(
        functools.partial(attend_kernel, heads, w, row),
        "attend",
        28,
        [SMEM] + [VMEM] * 5 + [ANY],
        [ANY, ANY, VMEM, VMEM],
        halves_of(blocks) + rows_of(w) + [shape((8, TOK_MB), F32)],
        [pltpu.VMEM((w + ff, D), BF)]
        + held(D)
        + [pltpu.VMEM((w, TOK_MB), BF)]
        + dma(low.shape[0], blocks),
        [index, angles[0], *kept[:4], low],
    )


def enter_kernel(blocks, w, row, *refs):
    index_ref = refs[0]
    c_refs = refs[1 : 1 + blocks]
    low_ref, slope_ref = refs[1 + blocks : 3 + blocks]
    context_ref, pre_ref, sum_ref = refs[3 + blocks : 6 + blocks]
    c_all, low, c_sems, low_sems = refs[6 + blocks :]
    loads = loads_of_weights(low_ref, row, low, low_sems)
    loads += copies_of_blocks(index_ref[0], c_refs, c_all, c_sems)
    start_all(loads)
    wait_all(loads)
    do_enter(
        w, lambda at: dot(c_all[at], low[...], 1, 1), slope_ref, context_ref, pre_ref, sum_ref
    )


def enter(order, index, c_blocks, kept, weights):
    w, ff = weights["w"], weights["ff"]
    low, row = weights["low"]
    blocks = len(c_blocks)
    return order.call(
        functools.partial(enter_kernel, blocks, w, row),
        "enter",
        60,
        [SMEM] + [ANY] * (blocks + 1) + [VMEM],
        [VMEM] * 3,
        rows_of(w, ff) + [shape((1, ff), F32)],
        held(D) + [pltpu.VMEM((w + ff, D), BF)] + dma(blocks, low.shape[0]),
        [index, *c_blocks, low, kept[4]],
    )


def scratch_of_backward(w):
    return [pltpu.VMEM((w, TOK_MB), BF)] + [pltpu.VMEM((TOK_MB, w), F32)] * 3


def backward_kernel(blocks, heads, w, row, *refs):
    index_ref = refs[0]
    x_refs = refs[1 : 1 + blocks]
    inner = refs[1 + blocks : 9 + blocks]
    main_ref, norms_ref, table_ref = refs[9 + blocks : 12 + blocks]
    keep_ref, send_ref, *outs = refs[12 + blocks : 17 + blocks]
    x_all, main, partial, *scratch, x_sems, main_sems, out_sems = refs[17 + blocks :]
    loads = copies_of_blocks(index_ref[0], x_refs, x_all, x_sems)
    loads += loads_of_weights(main_ref, row, main, main_sems)
    start_all(loads)
    leaving = Leaving(index_ref[0], partial, keep_ref, send_ref, out_sems)
    do_backward(
        heads, w, *inner, loads, x_all, main, norms_ref, table_ref, *outs, *scratch, partial, leaving
    )
    leaving.wait()


def backward(order, index, x_blocks, kept, entered, weights, angles):
    queries, keys, values, _, _, context, logs = kept
    blocks = len(x_blocks)
    w, heads, ff = weights["w"], weights["heads"], weights["ff"]
    main, row = weights["main"]
    return order.call(
        functools.partial(backward_kernel, blocks, heads, w, row),
        "backward",
        60,
        [SMEM] + [ANY] * blocks + [VMEM] * 8 + [ANY] + [VMEM] * 2,
        [ANY, ANY] + [VMEM] * 3,
        halves_of(blocks) + rows_of(3 * w) + [shape((8, D), F32), shape((1, 3 * w), F32)],
        held(D)
        + [pltpu.VMEM((3 * w + ff, D), BF)]
        + held(D)
        + scratch_of_backward(w)
        + dma(blocks, main.shape[0], blocks),
        [
            index,
            *x_blocks,
            angles[0],
            queries,
            keys,
            values,
            context,
            logs,
            entered[0],
            entered[1],
            main,
            weights["norms"],
            angles[1],
        ],
    )


def products_of(ready, index, source_refs, low_ref, low_row, c_all, low, c_sems, low_sems):
    if ready:
        loads = [pltpu.make_async_copy(source_refs[0], c_all, c_sems.at[0])]
        return loads, lambda at: c_all[at]
    loads = loads_of_weights(low_ref, low_row, low, low_sems)
    loads += copies_of_blocks(index, source_refs, c_all, c_sems)
    return loads, lambda at: dot(c_all[at], low[...], 1, 1)


def whole_backward_kernel(blocks, given, heads, w, main_row, low_row, *refs):
    index_ref = refs[0]
    c_refs = refs[1 : 1 + given]
    refs = refs[1 + given :]
    x_refs = refs[:blocks]
    starts_ref, q_ref, k_ref, v_ref, context_ref, logs_ref, slope_ref = refs[blocks : 7 + blocks]
    main_ref, low_ref, norms_ref, table_ref = refs[7 + blocks : 11 + blocks]
    keep_ref, send_ref, pre_ref, pre_sum_ref, *outs = refs[11 + blocks : 18 + blocks]
    c_all, x_all, main, low, partial, grad_context, *scratch = refs[18 + blocks : 28 + blocks]
    c_sems, x_sems, main_sems, low_sems, out_sems = refs[28 + blocks :]
    loads, products = products_of(
        given < blocks, index_ref[0], c_refs, low_ref, low_row, c_all, low, c_sems, low_sems
    )
    later = copies_of_blocks(index_ref[0], x_refs, x_all, x_sems)
    later += loads_of_weights(main_ref, main_row, main, main_sems)
    start_all(loads + later)
    leaving = Leaving(index_ref[0], partial, keep_ref, send_ref, out_sems)
    wait_all(loads)
    do_enter(w, products, slope_ref, grad_context, pre_ref, pre_sum_ref)
    do_backward(
        heads,
        w,
        starts_ref,
        q_ref,
        k_ref,
        v_ref,
        context_ref,
        logs_ref,
        grad_context,
        pre_ref,
        later,
        x_all,
        main,
        norms_ref,
        table_ref,
        *outs,
        *scratch,
        partial,
        leaving,
    )
    leaving.wait()


def held_cotangent(c_blocks, blocks):
    if len(c_blocks) < blocks:
        return [pltpu.VMEM(c_blocks[0].shape, F32)]
    return held(D)


def whole_backward(order, index, c_blocks, x_blocks, kept, weights, angles):
    queries, keys, values, _, slope, context, logs = kept
    blocks = len(x_blocks)
    w, heads, ff = weights["w"], weights["heads"], weights["ff"]
    main, main_row = weights["main"]
    low, low_row = weights["low"]
    dp = main.shape[0]
    return order.call(
        functools.partial(
            whole_backward_kernel, blocks, len(c_blocks), heads, w, main_row, low_row
        ),
        "whole_backward",
        60,
        [SMEM] + [ANY] * (len(c_blocks) + blocks) + [VMEM] * 7 + [ANY] * 2 + [VMEM] * 2,
        [ANY, ANY] + [VMEM] * 5,
        halves_of(blocks)
        + rows_of(ff)
        + [shape((1, ff), F32)]
        + rows_of(3 * w)
        + [shape((8, D), F32), shape((1, 3 * w), F32)],
        held_cotangent(c_blocks, blocks)
        + held(D)
        + [pltpu.VMEM((3 * w + ff, D), BF), pltpu.VMEM((w + ff, D), BF)]
        + held(D, w)
        + scratch_of_backward(w)
        + dma(blocks, blocks, dp, dp, blocks),
        [
            index,
            *c_blocks,
            *x_blocks,
            angles[0],
            queries,
            keys,
            values,
            context,
            logs,
            slope,
            main,
            low,
            weights["norms"],
            angles[1],
        ],
    )


def layer_kernel(blocks, heads, w, main_row, low_row, *refs):
    index_ref = refs[0]
    c_ref = refs[1]
    refs = refs[2:]
    x_refs = refs[:blocks]
    starts_ref, main_ref, low_ref, norms_ref, bias_ref, table_ref = refs[blocks : 6 + blocks]
    (y_keep, y_send, u_keep, u_send, hidden_ref, context_ref, pre_ref, pre_sum_ref, *outs) = refs[
        6 + blocks : 17 + blocks
    ]
    (c_all, x_all, main, low, y_all, u_all, q_ref, k_ref, v_ref, slope_ref, grad_context) = refs[
        17 + blocks : 28 + blocks
    ]
    logs_ref, v_turned, *scratch = refs[28 + blocks : 34 + blocks]
    c_sems, x_sems, main_sems, low_sems, y_sems, u_sems = refs[34 + blocks :]
    index = index_ref[0]
    loads = copies_of_blocks(index, x_refs, x_all, x_sems)
    loads += loads_of_weights(main_ref, main_row, main, main_sems)
    low_loads = loads_of_weights(low_ref, low_row, low, low_sems)
    c_loads = [pltpu.make_async_copy(c_ref, c_all, c_sems.at[0])]
    start_all(loads + low_loads + c_loads)
    y_leaving = Leaving(index, y_all, y_keep, y_send, y_sems)
    u_leaving = Leaving(index, u_all, u_keep, u_send, u_sems)
    wait_all(loads)
    do_project(
        w, x_all, main, norms_ref, bias_ref, table_ref, q_ref, k_ref, v_ref, hidden_ref, slope_ref
    )
    do_attend(
        heads,
        w,
        starts_ref,
        q_ref,
        k_ref,
        v_ref,
        hidden_ref,
        low,
        low_loads,
        context_ref,
        logs_ref,
        v_turned,
        y_all,
        y_leaving,
    )
    wait_all(c_loads)
    do_enter(w, lambda at: c_all[at], slope_ref, grad_context, pre_ref, pre_sum_ref)
    do_backward(
        heads,
        w,
        starts_ref,
        q_ref,
        k_ref,
        v_ref,
        context_ref,
        logs_ref,
        grad_context,
        pre_ref,
        [],
        x_all,
        main,
        norms_ref,
        table_ref,
        *outs,
        *scratch,
        u_all,
        u_leaving,
    )
    y_leaving.wait()
    u_leaving.wait()


def whole_layer(order, index, products, x_blocks, weights, angles):
    blocks = len(x_blocks)
    w, heads, ff = weights["w"], weights["heads"], weights["ff"]
    main, main_row = weights["main"]
    low, low_row = weights["low"]
    dp = main.shape[0]
    return order.call(
        functools.partial(layer_kernel, blocks, heads, w, main_row, low_row),
        "whole_layer",
        60,
        [SMEM] + [ANY] * (1 + blocks) + [VMEM] + [ANY] * 2 + [VMEM] * 3,
        [ANY] * 4 + [VMEM] * 7,
        halves_of(blocks)
        + halves_of(blocks)
        + rows_of(ff, w, ff)
        + [shape((1, ff), F32)]
        + rows_of(3 * w)
        + [shape((8, D), F32), shape((1, 3 * w), F32)],
        [pltpu.VMEM(products.shape, F32)]
        + held(D)
        + [pltpu.VMEM((3 * w + ff, D), BF), pltpu.VMEM((w + ff, D), BF)]
        + held(D, D, w, w, w, ff, w)
        + [pltpu.VMEM((8, TOK_MB), F32), pltpu.VMEM((w, TOK_MB), BF)]
        + scratch_of_backward(w)
        + dma(1, blocks, dp, dp, blocks, blocks),
        [
            index,
            products,
            *x_blocks,
            angles[0],
            main,
            low,
            weights["norms"],
            weights["bias"],
            angles[1],
        ],
    )


def put_vectors(out_ref, begin, stage_ref, vec_a, vec_b, raw_a, raw_b, pre_a, pre_b, own_ref, order_ref, raw_order, pre_order):
    dp, _, share = out_ref.shape
    half = dp // 2
    rows = [vec_a[:4] + vec_b[:4], own_ref[...], jnp.zeros((3, vec_a.shape[1]), F32)]
    norms = dot(jnp.concatenate(rows, axis=0).astype(BF), order_ref[...], 1, 0)

    def moved(first, second, order):
        value = (first[...] + second[...]).astype(BF)
        return dot(jnp.broadcast_to(value, (8, value.shape[1])), order[...], 1, 0)[:1]

    raw, pre = moved(raw_a, raw_b, raw_order), moved(pre_a, pre_b, pre_order)
    for j in range(dp):
        mine = jnp.where(stage_ref[0] == j // half, 1.0, 0.0)
        cols = slice(j % half * share, (j % half + 1) * share)
        block = [
            norms[:5, j * share : (j + 1) * share],
            raw[:, cols] * mine,
            pre[:, cols] * mine,
            jnp.zeros((SMALL - 7, share), F32),
        ]
        out_ref[j, begin : begin + SMALL] = jnp.concatenate(block, axis=0).astype(BF)


def grads_kernel(blocks, plan, extra, *refs):
    index_ref, norms_ref = refs[:2]
    with_cot = None in plan
    normed = sorted({which for which in plan if which is not None})
    count = MB * blocks
    row_refs = refs[2 : 2 + count]
    lefts = refs[2 + count : 2 + count + MB * len(plan)]
    rest = refs[2 + count + MB * len(plan) :]
    extras, rest = rest[:extra], rest[extra:]
    out_ref, total, *scratch = rest
    side_sems, sems = scratch.pop(), scratch.pop()
    sides, scratch = scratch[: MB * len(plan)], scratch[MB * len(plan) :]
    index = index_ref[0]
    dp, _, share = out_ref.shape
    loads = []
    for unit in range(MB):
        part = row_refs[unit * blocks : (unit + 1) * blocks]
        loads.append(copies_of_blocks(index, part, scratch[0].at[unit], sems.at[unit]))
        for i in range(len(plan)):
            left = lefts[i * MB + unit]
            loads[unit].append(
                pltpu.make_async_copy(left, sides[i * MB + unit], side_sems.at[i * MB + unit])
            )
        start_all(loads[unit])
    for unit in range(MB):
        wait_all(loads[unit])
        rights = {None: scratch[0]}
        if not with_cot:
            rights = dict(zip(normed, scratch))
            for at in chunks():
                hat, _ = normalize(scratch[0][unit, at])
                for norm in normed:
                    row = hat * norms_ref[norm : norm + 1] + norms_ref[2 + norm : 3 + norm]
                    rights[norm][unit, at] = row.astype(BF)
        begin = 0
        for i, which in enumerate(plan):
            left = sides[i * MB + unit]
            rows = slice(begin, begin + left.shape[1])
            part = dot(left[...], rights[which][unit], 0, 0)
            if unit:
                part = part + total[rows]
            if unit + 1 < MB:
                total[rows] = part
            else:
                for j in range(dp):
                    out_ref[j, rows] = part[:, j * share : (j + 1) * share].astype(BF)
            begin = rows.stop
    if extra:
        put_vectors(out_ref, begin, *extras)


def weight_grads(order, index, c_blocks, x_blocks, pieces, norms, dp, extra=()):
    plan = [which for _, which in pieces]
    blocks = len(x_blocks[0])
    rows = [block for unit in (c_blocks if None in plan else x_blocks) for block in unit]
    lefts = [left for part, _ in pieces for left in part]
    size = sum(part[0].shape[1] for part, _ in pieces) + (SMALL if extra else 0)
    buffers = len(set(plan))
    return order.call(
        functools.partial(grads_kernel, blocks, plan, len(extra)),
        "weight_grads",
        60,
        [SMEM, VMEM] + [ANY] * (len(rows) + len(lefts)) + [SMEM, *[VMEM] * (len(extra) - 1)][: len(extra)],
        [VMEM],
        [shape((dp, size, D // dp), BF)],
        [pltpu.VMEM((size, D), F32)]
        + [pltpu.VMEM(left.shape, BF) for left in lefts]
        + [pltpu.VMEM((MB, TOK_MB, D), BF)] * buffers
        + [pltpu.SemaphoreType.DMA((MB, blocks)), pltpu.SemaphoreType.DMA((len(lefts),))],
        [index, norms, *rows, *lefts, *extra],
    )[0]


SMALL = 16


def put_halves(at_first, keep, send, begin, size, low, high):
    keep[begin : begin + size] = jnp.where(at_first, low, high)
    send[begin : begin + size] = jnp.where(at_first, high, low)


def pack_kernel(width, w, stage_ref, qkv_ref, up_ref, out_ref, down_ref, keep_ref, send_ref, *held):
    (qkv, up, out, down), sems = held[:4], held[4]
    sources = (qkv_ref, up_ref, out_ref, down_ref)
    loads = [
        pltpu.make_async_copy(source, target, sems.at[i])
        for i, (source, target) in enumerate(zip(sources, held))
    ]
    start_all(loads)
    at_first = stage_ref[0] == 0
    ff = up.shape[1] // 2
    if w != width:
        keep_ref[...] = jnp.zeros_like(keep_ref)
        send_ref[...] = jnp.zeros_like(send_ref)
    wait_all(loads)
    for i in range(3):
        turned = qkv[i].T
        put_halves(at_first, keep_ref, send_ref, i * w, width, turned[:width], turned[width:])
    turned = up[...].T
    put_halves(at_first, keep_ref, send_ref, 3 * w, ff, turned[:ff], turned[ff:])
    begin = 3 * w + ff
    put_halves(at_first, keep_ref, send_ref, begin, width, out[:width], out[width:])
    put_halves(at_first, keep_ref, send_ref, begin + w, ff, down[:ff], down[ff:])


def pack(order, stage, qkv, up, out, down, w):
    width, ff, share = qkv.shape[2] // 2, up.shape[1] // 2, up.shape[0]
    return order.call(
        functools.partial(pack_kernel, width, w),
        "pack",
        60,
        [SMEM] + [ANY] * 4,
        [VMEM] * 2,
        [shape((4 * w + 2 * ff, share), BF)] * 2,
        [pltpu.VMEM(value.shape, BF) for value in (qkv, up, out, down)] + dma(4),
        [stage, qkv, up, out, down],
    )


def by_stage_kernel(stage_ref, *refs):
    at_first = stage_ref[0] == 0
    pairs, (first_ref, second_ref) = refs[:-2], refs[-2:]
    begin = 0
    for mine_ref, other_ref in zip(pairs[::2], pairs[1::2]):
        rows = slice(begin, begin + mine_ref.shape[0])
        mine, other = mine_ref[...], other_ref[...]
        first_ref[rows] = jnp.where(at_first, mine, other)
        second_ref[rows] = jnp.where(at_first, other, mine)
        begin = rows.stop


def by_stage(order, stage, *pairs):
    rows = sum(mine.shape[0] for mine in pairs[::2])
    return order.call(
        by_stage_kernel,
        "by_stage",
        16,
        [SMEM] + [VMEM] * len(pairs),
        [VMEM] * 2,
        [shape((rows, pairs[0].shape[1]), BF)] * 2,
        [],
        [stage, *pairs],
    )


def both_halves(stage_ref, mine0, mine1, from0, from1, begin, size):
    at_first = stage_ref[0] == 0
    rows = slice(begin, begin + size)
    low = jnp.where(at_first, mine0[rows], from1[rows])
    high = jnp.where(at_first, from0[rows], mine1[rows])
    return low.astype(F32), high.astype(F32)


def unpack_outer_kernel(width, w, ff, *refs):
    parts, (out_ref, down_ref) = refs[:5], refs[5:]
    out_ref[:width], out_ref[width:] = both_halves(*parts, 0, width)
    down_ref[:ff], down_ref[ff:] = both_halves(*parts, w, ff)


def unpack_inner_kernel(width, w, ff, *refs):
    parts, (up_ref, qkv_ref) = refs[:5], refs[5:]
    low, high = both_halves(*parts, 0, ff)
    up_ref[:, :ff] = low.T
    up_ref[:, ff:] = high.T
    for i in range(3):
        low, high = both_halves(*parts, ff + i * w, width)
        qkv_ref[i] = jnp.concatenate([low, high], axis=0).T


def unpack(kernel, order, stage, parts, out_shape):
    return order.call(
        kernel,
        "unpack",
        24,
        [SMEM] + [VMEM] * 4,
        [VMEM] * len(out_shape),
        out_shape,
        [],
        [stage, *parts],
    )


def picked_kernel(bit, flip, pairs, plains, *refs):
    index_ref = refs[0]
    out_ref, held, sems = refs[1 + pairs + plains :]
    want = (index_ref[0] >> bit) & 1
    if flip:
        want = 1 - want
    copies = []
    for i in range(pairs + plains):
        for j in range(out_ref.shape[0]):
            source = refs[1 + i].at[j, want] if i < pairs else refs[1 + i].at[j]
            copies.append(pltpu.make_async_copy(source, held.at[i, j], sems.at[i, j]))
    for copy in copies:
        copy.start()
    for copy in copies:
        copy.wait()
    total = held[0].astype(F32)
    for i in range(1, pairs + plains):
        total = total + held[i].astype(F32)
    out_ref[...] = total.astype(BF)


def picked_sum(order, where, bit, flip, pairs, plains=()):
    dims = (pairs[0].shape[0],) + pairs[0].shape[2:]
    terms = [*pairs, *plains]
    return order.call(
        functools.partial(picked_kernel, bit, flip, len(pairs), len(plains)),
        "picked_sum",
        20,
        [SMEM] + [ANY] * len(terms),
        [VMEM],
        [shape(dims, BF)],
        [
            pltpu.VMEM((len(terms), *dims), BF),
            pltpu.SemaphoreType.DMA((len(terms), dims[0])),
        ],
        [where, *terms],
    )[0]


class Sum:
    def __init__(self, where, keep, send):
        self.where = where
        self.terms = [keep, swap(send, "tensor", 0)]

    def send(self, order, *others):
        place = lax.axis_index("tensor")
        last = bits_of("tensor") - 1
        for bit in range(1, last + 1):
            pairs = [
                term.reshape((term.shape[0] // 2, 2) + term.shape[1:]) for term in self.terms
            ]
            sent = picked_sum(order, self.where, bit, True, pairs)
            self.sent = sent
            self.received = swap(after(sent, *others) if others else sent, "tensor", bit)
            if bit < last:
                own = (place >> bit) & 1
                self.terms = [pick(pair, own, 1) for pair in pairs] + [self.received]
        self.pairs = pairs
        return self

    def cross(self, order):
        last = bits_of("tensor") - 1
        self.own = picked_sum(order, self.where, last, False, self.pairs, [self.received])[0]
        self.other = swap(self.own, "pipe", 0)
        return self


def add_rows_kernel(x_ref, own_ref, other_ref, norms_ref, out_ref):
    bias = norms_ref[4:5] + norms_ref[5:6]
    total = x_ref[...].astype(F32) + own_ref[...].astype(F32) + other_ref[...].astype(F32)
    out_ref[...] = (total + bias).astype(out_ref.dtype)


def add_rows(order, x_rows, summed, weights):
    return order.call(
        add_rows_kernel,
        "add_rows",
        12,
        [VMEM] * 4,
        [VMEM],
        [shape(x_rows.shape, BF)],
        [],
        [x_rows, summed.own, summed.other, weights["norms"]],
    )[0]


def norm_back_rows(x_ref, own_ref, other_ref, cot_ref):
    grad_hat = own_ref[...].astype(F32) + other_ref[...].astype(F32)
    hat, scale = normalize(x_ref[...])
    mean = jnp.mean(grad_hat, axis=-1, keepdims=True)
    along = jnp.mean(grad_hat * hat, axis=-1, keepdims=True)
    return cot_ref[...].astype(F32) + (grad_hat - mean - hat * along) * scale


def norm_back_kernel(x_ref, own_ref, other_ref, cot_ref, out_ref):
    out_ref[...] = norm_back_rows(x_ref, own_ref, other_ref, cot_ref).astype(BF)


def norm_back(order, x_rows, summed, cot_rows):
    return order.call(
        norm_back_kernel,
        "norm_back",
        16,
        [VMEM] * 4,
        [VMEM],
        [shape(x_rows.shape, BF)],
        [],
        [x_rows, summed.own, summed.other, cot_rows],
    )[0]


def ends_kernel(unit, stage_ref, x_ref, own_ref, other_ref, cot_ref, *refs):
    middle_ref, y_own_ref, y_other_ref, norms_ref = refs[:4]
    ends_ref, token_ref, held, sem = refs[-4:]
    token_ref[...] = jnp.zeros_like(token_ref)

    @pl.when(stage_ref[0] == 0)
    def _():
        held[...] = norm_back_rows(x_ref, own_ref, other_ref, cot_ref)

    @pl.when(stage_ref[0] != 0)
    def _():
        add_rows_kernel(middle_ref, y_own_ref, y_other_ref, norms_ref, held)

    copy = pltpu.make_async_copy(held, ends_ref.at[unit], sem)
    copy.start()
    copy.wait()


def write_ends(order, unit, stage, ends, x_rows, summed, cot_rows, middle_rows, y_sum, weights):
    args = [
        stage,
        x_rows,
        summed.own,
        summed.other,
        cot_rows,
        middle_rows,
        y_sum.own,
        y_sum.other,
        weights["norms"],
    ]
    more = {}
    if ends is not None:
        more = dict(input_output_aliases={len(args): 0})
        args.append(ends)
    return order.call(
        functools.partial(ends_kernel, unit),
        "ends",
        20,
        [SMEM] + [VMEM] * 8 + [ANY] * len(more),
        [ANY, VMEM],
        [shape((MB, *x_rows.shape), F32), shape((8, 128), F32)],
        [pltpu.VMEM(x_rows.shape, F32), pltpu.SemaphoreType.DMA],
        args,
        **more,
    )[0]


def angles_for(lengths_row, w):
    finish = jnp.cumsum(lengths_row)
    places = jnp.arange(TOK_MB, dtype=jnp.int32)
    after = (places[:, None] >= finish[None, :]).astype(jnp.int32)
    starts = jnp.sum(after * lengths_row[None, :], axis=1)
    position = (places - starts).astype(F32)
    inverse_freq = 10000.0 ** (-jnp.arange(ROT // 2, dtype=F32) * 2.0 / ROT)
    phase = position[:, None] * inverse_freq[None, :]
    cosine, sine = jnp.cos(phase), jnp.sin(phase)
    rest = jnp.zeros((TOK_MB, HD - 2 * ROT), F32)
    table = jnp.concatenate([cosine, cosine, -sine, sine, rest], axis=1)
    return starts[None], jnp.tile(table, (1, w // HD))


def body(
    boundary,
    lengths,
    gains,
    biases,
    qkv_weight,
    qkv_bias,
    out_weight,
    up_weight,
    up_bias,
    down_weight,
):
    stage = lax.axis_index("pipe")
    at_first = stage == 0
    dp = lax.axis_size("dp")
    tensor = lax.axis_size("tensor")
    index = lax.axis_index("tensor").astype(jnp.int32)[None]
    stage_word = stage.astype(jnp.int32)[None]
    order = Order()
    share = D // dp
    width = qkv_weight.shape[3] // 2
    ff = up_weight.shape[2] // 2
    heads = width // HD
    w = max(width, 128)
    cut = 3 * w + ff

    def split(mine, other):
        return jnp.where(at_first, mine, other), jnp.where(at_first, other, mine)

    def half(value, which, axis):
        size = value.shape[axis] // 2
        return lax.dynamic_slice_in_dim(value, which * size, size, axis)

    def padded(value, axis):
        if w == width:
            return value
        pads = [(0, 0)] * value.ndim
        pads[axis] = (0, w - width)
        return jnp.pad(value, pads)

    tiles = boundary[0, :, 0]
    angles = [angles_for(lengths[unit, 0], w) for unit in range(MB)]
    far = tensor // 2

    def gather_far(value):
        blocks = {0: value}
        for bit in reversed(range(1, bits_of("tensor"))):
            for s in list(blocks):
                blocks[s | (1 << bit)] = swap(blocks[s], "tensor", bit)
        return [blocks[s] for s in sorted(blocks)]

    piece = gains.shape[2]
    small = jnp.concatenate([gains[0], biases[0]])
    small = jnp.moveaxis(gather_tensor(small), 0, 1).reshape(6, share)
    flat = jnp.concatenate([qkv_bias[0].reshape(-1), up_bias[0]])
    flat = jnp.pad(flat, (0, (SMALL - 6) * share - flat.shape[0])).reshape(-1, share)
    small = jnp.concatenate([small, flat])

    mine, sent = pack(
        order,
        stage_word,
        jnp.moveaxis(qkv_weight[0], 1, 0),
        up_weight[0],
        out_weight[0],
        down_weight[0],
        w,
    )
    other = swap(sent, "pipe", 0)
    order.hold(small)
    order.pause()
    small_other = swap(small, "pipe", 0)
    def gather_near(order, blocks):
        found = [None] * tensor
        for i, rows in enumerate(blocks):
            found[2 * i] = rows
            found[2 * i + 1] = swap(after(rows, order.last[0]), "tensor", 0)
        return found

    order.pause()
    stack_0, stack_1 = by_stage(order, stage_word, mine, other, small, small_other)
    far_tiles = [gather_far(after(tile, order.last[0])) for tile in tiles]
    stack_0 = lax.all_gather(stack_0, "dp", axis=0)

    def vectors_of(gathered, row):
        small = gathered[:, row : row + SMALL].astype(F32)
        norms = small[:, :6].reshape(dp, 6, tensor, piece).transpose(1, 2, 0, 3).reshape(6, D)
        flat = small[:, 6:].reshape(dp, -1)
        raw = flat[:, : 3 * piece].reshape(dp, 3, piece).transpose(1, 0, 2)
        raw = padded(half(raw.reshape(3, 2 * width), stage, 1), 1).reshape(1, 3 * w)
        up = flat[:, 3 * piece : 3 * piece + up_bias.shape[1]].reshape(1, 2 * ff)
        return dict(norms=norms, bias=jnp.concatenate([raw, half(up, stage, 1)], axis=1))

    x_rows, cot_rows, x_blocks, c_blocks = [], [], [], []

    def take_tiles(unit):
        others = [swap(tile, "pipe", 0) for tile in far_tiles[unit]]
        order.pause()
        x_far, cot_far = [], []
        for mine, other in zip(far_tiles[unit], others):
            rows, cot = by_stage(order, stage_word, mine, other)
            x_far.append(rows)
            cot_far.append(cot)
        x_rows.append(x_far[0])
        cot_rows.append(cot_far[0])
        order.pause()
        x_blocks.append(gather_near(order, x_far))
        order.pause()
        order.hold(*x_blocks[unit])
        order.pause()
        c_blocks.append(gather_near(order, cot_far))
        order.pause()
        order.hold(*c_blocks[unit])

    order.hold(*[value for pair in angles for value in pair])
    order.pause()
    take_tiles(0)
    stack_1 = lax.all_gather(after(stack_1, x_rows[0]), "dp", axis=0)
    take_tiles(1)
    order.pause()
    row = 4 * w + 2 * ff
    layers = [
        dict(w=w, ff=ff, heads=heads, main=(stack, 0), low=(stack, cut))
        for stack in (stack_0, stack_1)
    ]
    layers[0].update(vectors_of(stack_0, row))

    units = range(MB)
    kept = [[None] * MB, [None] * MB]
    entered = [[None] * MB, [None] * MB]
    back = [[None] * MB, [None] * MB]

    def picks(sources, count):
        return (jnp.arange(count)[:, None] == sources[None, :]).astype(BF)

    column = jnp.arange(D)
    order_norms = picks(
        column % share // piece * (D // tensor) + column // share * piece + column % piece, D
    )
    column = jnp.arange(dp // 2 * share)
    group, place = column // share, column % share
    order_raw = picks(
        jnp.where(place < 3 * piece, place // piece * w + group * piece + place % piece, -1), 3 * w
    )
    up_piece = 2 * ff // dp
    order_pre = picks(jnp.where(place < up_piece, group * up_piece + place, -1), ff)

    def vector_rows(layer, cots):
        own = sum(jnp.sum(rows.astype(F32), axis=0) for rows in cots)
        own = own * jnp.where(at_first, 1.0, 0.0)
        sources = ((back, 1), (back, 2), (entered, 2))
        parts = [source[layer][unit][at] for source, at in sources for unit in units]
        return [stage_word, *parts, own[None], order_norms, order_raw, order_pre]

    def vectors_from(rows_0, rows_1):
        both = jnp.stack([rows_0, rows_1]).astype(F32)
        norm = both[:, :5].reshape(2, 5, tensor, piece).transpose(2, 0, 1, 3)
        place = lax.axis_index("tensor")
        total = pick(norm, place, 0)
        for s in range(1, tensor):
            pairs = [(i, i ^ s) for i in range(tensor)]
            total = total + lax.ppermute(pick(norm, place ^ s, 0), "tensor", pairs)
        flat = jnp.concatenate([total.reshape(2, -1), both[:, 5:7].reshape(2, -1)], axis=1)
        mine = jnp.where(at_first, flat[0], flat[1])
        total = mine + swap(jnp.where(at_first, flat[1], flat[0]), "pipe", 0)
        norm = total[: 5 * piece].reshape(5, piece)
        raw = total[5 * piece : 5 * piece + 3 * piece].reshape(3, piece)
        begin = 5 * piece + share
        return norm, raw, total[begin : begin + up_bias.shape[1]]

    def run_project(layer, unit, blocks):
        kept[layer][unit] = project(order, index, blocks, layers[layer], angles[unit])

    def run_attend(layer, unit):
        keep, send, *rest = attend(
            order, index, tensor, kept[layer][unit], layers[layer], angles[unit]
        )
        kept[layer][unit] = [*kept[layer][unit], *rest]
        return Sum(index, keep, send)

    def run_backward(layer, unit, cots, blocks):
        keep, send, pre, pre_sum, *back[layer][unit] = whole_backward(
            order, index, cots, blocks, kept[layer][unit], layers[layer], angles[unit]
        )
        entered[layer][unit] = [None, pre, pre_sum]
        return Sum(index, keep, send)

    def run_layer(unit, blocks):
        y_keep, y_send, u_keep, u_send, hidden, context, pre, pre_sum, *rest = whole_layer(
            order, index, products[unit], blocks, layers[1], angles[unit]
        )
        kept[1][unit] = [None, None, None, hidden, None, context, None]
        entered[1][unit] = [None, pre, pre_sum]
        back[1][unit] = rest
        return Sum(index, y_keep, y_send), Sum(index, u_keep, u_send)

    def reduced(layer, names, cots, rows, extra=()):
        sources = dict(
            out=(kept, 5, None), down=(kept, 3, None), up=(entered, 1, 1), qkv=(back, 0, 0)
        )
        pieces = []
        for name in names:
            held_in, place, which = sources[name]
            pieces.append(([held_in[layer][unit][place] for unit in units], which))
        norms = layers[layer]["norms"]
        value = weight_grads(order, index, cots, rows, pieces, norms, dp, extra)
        return lax.psum_scatter(value, "dp", scatter_dimension=0)

    run_project(0, 0, x_blocks[0])
    sum_a = run_attend(0, 0)
    order.pause()
    sum_a.send(order)
    run_project(0, 1, x_blocks[1])
    sum_b = run_attend(0, 1)
    sum_a.cross(order)
    sum_b.send(order)
    middle_a = add_rows(order, x_rows[0], sum_a, layers[0])
    far_a = gather_far(middle_a)
    sum_b.cross(order)
    layers[1].update(vectors_of(after(stack_1, order.last[0]), row))
    products = [cotangent(order, index, c_blocks[unit], layers[1]) for unit in units]
    blocks_a = gather_near(order, far_a)
    order.hold(stack_1)
    middle_b = add_rows(order, x_rows[1], sum_b, layers[0])
    far_b = gather_far(middle_b)

    y_a, sum_a = run_layer(0, blocks_a)
    order.pause()
    blocks_b = gather_near(order, far_b)
    middle_blocks = [blocks_a, blocks_b]
    order.hold(y_a.terms[1])
    sum_a.send(order)
    run_project(1, 1, blocks_b)
    y_b = run_attend(1, 1)
    sum_a.cross(order)
    order.hold(y_b.terms[1])
    y_a.send(order)
    y_b.send(order)
    sum_b = run_backward(1, 1, [products[1]], blocks_b)
    cot_a = norm_back(order, middle_a, sum_a, cot_rows[0])
    sum_b.send(order)
    y_a.cross(order)
    outer_1 = reduced(1, ("out", "down"), c_blocks, middle_blocks)
    sum_b.cross(order)
    far_a = gather_far(after(cot_a, order.last[0]))
    inner_1 = reduced(1, ("up", "qkv"), c_blocks, middle_blocks, vector_rows(1, cot_rows))
    cot_blocks = [gather_near(order, far_a)]
    y_b.cross(order)
    cot_b = norm_back(order, middle_b, sum_b, cot_rows[1])
    far_b = gather_far(cot_b)

    order.hold(outer_1, y_a.other)
    order.pause()
    from_outer_1 = swap(outer_1, "pipe", 0)
    sum_a = run_backward(0, 0, cot_blocks[0], x_blocks[0])
    cot_blocks.append(gather_near(order, far_b))
    order.pause()
    outer_0 = reduced(0, ("out", "down"), cot_blocks, x_blocks)
    sum_a.send(order)
    order.hold(from_outer_1, inner_1, y_b.other)
    order.pause()
    from_inner_1 = swap(inner_1, "pipe", 0)
    sum_b = run_backward(0, 1, cot_blocks[1], x_blocks[1])
    order.hold(from_inner_1)
    inner_0 = reduced(0, ("up", "qkv"), cot_blocks, x_blocks, vector_rows(0, (cot_a, cot_b)))
    from_outer_0 = swap(after(outer_0, order.last[0]), "pipe", 0)
    order.pause()
    sum_b.send(order)
    sum_a.cross(order)
    order.pause()
    sum_b.cross(order)
    ends = write_ends(
        order, 0, stage_word, None, x_rows[0], sum_a, cot_a, middle_a, y_a, layers[1]
    )
    order.hold(from_outer_0)
    grad_out, grad_down = unpack(
        functools.partial(unpack_outer_kernel, width, w, ff),
        order,
        stage_word,
        [outer_0, outer_1, from_outer_0, from_outer_1],
        [shape((2 * width, share), F32), shape((2 * ff, share), F32)],
    )
    order.hold(inner_0)
    ends = write_ends(
        order, 1, stage_word, ends, x_rows[1], sum_b, cot_b, middle_b, y_b, layers[1]
    )
    last = 3 * w + ff
    from_inner_0 = swap(inner_0, "pipe", 0)
    vectors = vectors_from(inner_0[last:], after(inner_1, order.last[0])[last:])
    order.hold(from_inner_0)
    grad_up, grad_qkv = unpack(
        functools.partial(unpack_inner_kernel, width, w, ff),
        order,
        stage_word,
        [inner_0, inner_1, from_inner_0, from_inner_1],
        [shape((share, 2 * ff), F32), shape((3, share, 2 * width), F32)],
    )
    grad_qkv = jnp.moveaxis(grad_qkv, 0, 1)
    norm_grads, grad_qkv_bias, grad_up_bias = vectors
    grad_gains = norm_grads[:2]
    grad_biases = jnp.concatenate([norm_grads[2:5], norm_grads[4:5]])
    return (
        ends[None, :, None],
        grad_gains[None],
        grad_biases[None],
        grad_qkv[None],
        grad_qkv_bias[None],
        grad_out[None],
        grad_up[None],
        grad_up_bias[None],
        grad_down[None],
    )


def solution(mesh):
    placed = (
        P("pipe", None, "dp", "tensor", None),
        P(None, "dp", None),
        P("pipe", None, ("tensor", "dp")),
        P("pipe", None, ("tensor", "dp")),
        P("pipe", "dp", None, "tensor"),
        P("pipe", None, ("tensor", "dp")),
        P("pipe", "tensor", "dp"),
        P("pipe", "dp", "tensor"),
        P("pipe", ("tensor", "dp")),
        P("pipe", "tensor", "dp"),
    )
    return jax.shard_map(
        body,
        mesh=mesh,
        in_specs=placed,
        out_specs=(placed[0],) + placed[2:],
        check_vma=False,
    )
```
